32 devices in a mesh: groups: 2 (over x), pool: 4 (over y, core), tp: 4 (over z).
Axes of the slice: x: 2, y: 2, z: 4, core: 2. Of those that a mesh axis runs over, the one named last changes fastest.
Arguments:
- tokens: bfloat16 [1024, 8192], P(('groups', 'pool')), parts along dimension 0, may hold values from -6 to 6
- input_norm_gain: bfloat16 [8192], replicated, may hold values from 0.25 to 1.75
- query_matrix: bfloat16 [8192, 8192], P('pool', 'tp'), may hold values from -0.0625 to 0.0625
- key_matrix: bfloat16 [8192, 1024], P('pool', 'tp'), may hold values from -0.0625 to 0.0625
- value_matrix: bfloat16 [8192, 1024], P('pool', 'tp'), may hold values from -0.0625 to 0.0625
- output_matrix: bfloat16 [8192, 8192], P('tp', 'pool'), may hold values from -0.0625 to 0.0625
- rotated_key_cache: bfloat16 [1024, 8, 64, 128], P(('groups', 'pool'), 'tp'), parts along dimension 0, may hold values from -105 to 105
- cached_value_rows: bfloat16 [1024, 8, 64, 128], P(('groups', 'pool'), 'tp'), parts along dimension 0, may hold values from -6 to 6
- cache_length_per_row: int32 [1024], P(('groups', 'pool')), parts along dimension 0, may hold values from 1 to 64, as said below
- row_adapter_index: int32 [1024], P(('groups', 'pool')), parts along dimension 0, may hold values from 0 to 127, as said below
- query_down_maps: bfloat16 [128, 16, 8192], P('pool', None, 'tp'), may hold values from -0.0625 to 0.0625
- query_up_maps: bfloat16 [128, 16, 8192], P('pool', None, 'tp'), may hold values from -1.5 to 1.5
- value_down_maps: bfloat16 [128, 16, 8192], P('pool', None, 'tp'), may hold values from -0.0625 to 0.0625
- value_up_maps: bfloat16 [128, 16, 1024], P('pool', None, 'tp'), may hold values from -1.5 to 1.5
Outputs:
- attn_out: bfloat16 [1024, 8192], P(('groups', 'tp'), 'pool'), parts along dimension 0
- new_key: bfloat16 [1024, 1024], P(('groups', 'pool'), 'tp'), parts along dimension 0
- new_value: bfloat16 [1024, 1024], P(('groups', 'pool'), 'tp'), parts along dimension 0
The draws below stay inside these ranges and needn't reach their ends.
There are 2 independent parts, one for each index of `groups`. The reference program is written for one: setup_inputs(seed, part) draws one part's arguments, and reference() takes and returns one part's arrays. A program takes and returns all parts, laid end to end along the dimension named above; an argument that names none is the same for every part. Nothing has to cross between parts.
Inputs may be any that keep to these rules, and one draw needn't show every extreme that they name: `row_adapter_index`: adapter i is held by pool index i // 32. The rows of one pool index name adapters held by any one pool index at most 64 times. Positions 0 to cache_length_per_row - 1 of a row's cache hold its keys and values; the new token sits at position cache_length_per_row.
All inputs are finite; a program needn't handle non-finite values.
Results may differ from the reference program's by a relative error of at most 0.0099.
Values may be sent and summed in bfloat16 or wider, within the bound.
No kernel may reach another device: no remote copies, remote signals or barrier semaphores. Data moves between devices by JAX's collectives and lax.ppermute only.
A program may use at most 128 MiB of HBM per device.

```python
import math
import jax
import jax.numpy as jnp
from jax import lax

MODEL_WIDTH = 8192
QUERY_HEADS = 64
KEY_VALUE_HEADS = 8
HEAD_WIDTH = 128
ADAPTER_RANK = 16
ROWS_DEV = 128
CACHE = 64
ADAPT_DEV = 32
ROWS = 512
ADAPTER_COUNT = 128
CAP = 64


def draw_row_adapter_index(key, part):
    key = jax.random.fold_in(key, 11)
    blocks = ROWS // ROWS_DEV
    slot_total = 2 * ROWS_DEV
    hot_key, block_key = jax.random.split(key)
    hot_owner = jax.random.randint(hot_key, (), 0, blocks)

    def one_block(sub_key):
        order_key, local_key, shuffle_key = jax.random.split(sub_key, 3)
        rank_of = jax.random.permutation(order_key, slot_total)
        slot_ids = jnp.arange(slot_total)
        forced = (slot_ids // CAP == hot_owner) | (slot_ids == 0) | (slot_ids == slot_total - 1)
        priority = jnp.where(forced, rank_of - slot_total, rank_of)
        chosen = jnp.argsort(priority, stable=True)[:ROWS_DEV]
        chosen = jax.random.permutation(shuffle_key, chosen)
        owner_of = chosen // CAP
        local_pick = jax.random.randint(local_key, (ROWS_DEV,), 0, ADAPT_DEV)
        local_pick = jnp.where(chosen == 0, 0, jnp.where(chosen == slot_total - 1, ADAPT_DEV - 1, local_pick))
        return (owner_of * ADAPT_DEV + local_pick).astype(jnp.int32)
    return jax.vmap(one_block)(jax.random.split(block_key, blocks)).reshape(ROWS)


def draw_cache_length_per_row(key, part):
    key = jax.random.fold_in(key, 23)
    subkeys = jax.random.split(key, 4)
    blocks = ROWS // ROWS_DEV
    divisor = jax.random.randint(subkeys[0], (blocks, 1), 1, 5)
    block_limit = CACHE // divisor
    lengths = jax.random.randint(subkeys[1], (blocks, ROWS_DEV), 1, block_limit + 1).reshape(ROWS)
    longest_row = jax.random.randint(subkeys[2], (), 0, ROWS)
    shortest_row = (longest_row + jax.random.randint(subkeys[3], (), 1, ROWS)) % ROWS
    return lengths.at[longest_row].set(CACHE).at[shortest_row].set(1).astype(jnp.int32)


def draw_rotated_key_cache(key, part):
    key = jax.random.fold_in(key, 37)
    subkeys = jax.random.split(key, 1)
    cache_shape = (ROWS, KEY_VALUE_HEADS, CACHE, HEAD_WIDTH)
    return jnp.clip(jax.random.normal(subkeys[0], cache_shape, jnp.float32), -6.0, 6.0).astype(jnp.bfloat16)


def level_of(key, shape, shards, low, top_value):
    def one(axis_at, shards_of):
        draws = jax.random.uniform(jax.random.fold_in(jax.random.fold_in(key, 6), axis_at), (shards_of,), jnp.float32, low / len(shards), top_value / len(shards))
        return jnp.repeat(jnp.exp(draws), shape[axis_at] // shards_of).reshape((-1,) + (1,) * (len(shape) - axis_at - 1))

    gain = one(*shards[0])
    for cut in shards[1:]:
        gain = gain * one(*cut)
    return gain


def noise(stream_key, dims, deviation, reach, shards=(), kind=jnp.bfloat16):
    array = deviation * jax.random.normal(stream_key, dims, jnp.float32)
    if shards:
        array = array * level_of(stream_key, dims, shards, -0.22, 0.18)
    return jnp.clip(array, -reach, reach).astype(kind)


def setup_inputs(seed: int = 0, part: int = 0) -> dict:
    seeds = jax.random.split(jax.random.key(seed), 15)
    own_keys = jax.random.split(jax.random.fold_in(seeds[14], part), 15)
    return {
        "tokens": noise(own_keys[0], (ROWS, MODEL_WIDTH), 1.0, 6.0, ((0, 4),)),
        "input_norm_gain": jnp.clip(1.0 + 0.15 * jax.random.normal(seeds[1], (MODEL_WIDTH,), jnp.float32), 0.25, 1.75).astype(jnp.bfloat16),
        "query_matrix": noise(seeds[2], (MODEL_WIDTH, QUERY_HEADS * HEAD_WIDTH), MODEL_WIDTH ** -0.5, 0.0625, ((0, 4), (1, 4))),
        "key_matrix": noise(seeds[3], (MODEL_WIDTH, KEY_VALUE_HEADS * HEAD_WIDTH), MODEL_WIDTH ** -0.5, 0.0625, ((0, 4), (1, 4))),
        "value_matrix": noise(seeds[4], (MODEL_WIDTH, KEY_VALUE_HEADS * HEAD_WIDTH), MODEL_WIDTH ** -0.5, 0.0625, ((0, 4), (1, 4))),
        "output_matrix": noise(seeds[5], (QUERY_HEADS * HEAD_WIDTH, MODEL_WIDTH), (QUERY_HEADS * HEAD_WIDTH) ** -0.5, 0.0625, ((0, 4), (1, 4))),
        "rotated_key_cache": draw_rotated_key_cache(jax.random.fold_in(jax.random.fold_in(seeds[14], part), 71), part),
        "cached_value_rows": noise(own_keys[7], (ROWS, KEY_VALUE_HEADS, CACHE, HEAD_WIDTH), 1.0, 6.0, ((0, 4), (1, 4))),
        "cache_length_per_row": draw_cache_length_per_row(jax.random.fold_in(jax.random.fold_in(seeds[14], part), 71), part),
        "row_adapter_index": draw_row_adapter_index(jax.random.fold_in(jax.random.fold_in(seeds[14], part), 71), part),
        "query_down_maps": noise(seeds[10], (ADAPTER_COUNT, ADAPTER_RANK, MODEL_WIDTH), MODEL_WIDTH ** -0.5, 0.0625, ((0, 4), (2, 4))),
        "query_up_maps": noise(seeds[11], (ADAPTER_COUNT, ADAPTER_RANK, QUERY_HEADS * HEAD_WIDTH), ADAPTER_RANK ** -0.5, 1.5, ((0, 4), (2, 4))),
        "value_down_maps": noise(seeds[12], (ADAPTER_COUNT, ADAPTER_RANK, MODEL_WIDTH), MODEL_WIDTH ** -0.5, 0.0625, ((0, 4), (2, 4))),
        "value_up_maps": noise(seeds[13], (ADAPTER_COUNT, ADAPTER_RANK, KEY_VALUE_HEADS * HEAD_WIDTH), ADAPTER_RANK ** -0.5, 1.5, ((0, 4), (2, 4))),
    }


epsilon = 1e-05
adapter_scale = 0.5
rope_base = 500000.0

def rms_norm(tokens, input_norm_gain):
    values = tokens.astype(jnp.float32)
    mean_square = lax.optimization_barrier(jnp.mean(values * values, axis=-1, keepdims=True))
    return (values * lax.rsqrt(mean_square + epsilon) * input_norm_gain.astype(jnp.float32)).astype(jnp.bfloat16)

def rotate(values, positions):
    head_dim = values.shape[-1]
    half_dim = head_dim // 2
    frequency = jnp.power(jnp.float32(rope_base), jnp.arange(half_dim, dtype=jnp.float32) * (-2.0 / head_dim))
    angles = positions.astype(jnp.float32)[:, None] * frequency[None, :]
    cosines = jnp.cos(angles)[:, None, :]
    sine_terms = jnp.sin(angles)[:, None, :]
    first_half = values[..., :half_dim]
    second_half = values[..., half_dim:]
    return jnp.concatenate([first_half * cosines - second_half * sine_terms, second_half * cosines + first_half * sine_terms], axis=-1)

def attend_row(row_items):
    query_row, key_rows, value_rows, own_key, own_value, length = row_items
    score_scale = 1.0 / math.sqrt(HEAD_WIDTH)
    query_float = query_row.astype(jnp.float32)
    scores = jnp.einsum('gid,gjd->gij', query_float, key_rows.astype(jnp.float32)) * score_scale
    own_score = jnp.einsum('gid,gd->gi', query_float, own_key.astype(jnp.float32)) * score_scale
    in_range = jnp.arange(CACHE) < length
    masked = jnp.where(in_range[None, None, :], scores, -jnp.inf)
    peak_score = jnp.maximum(lax.optimization_barrier(jnp.max(masked, axis=-1)), own_score)
    weights = jnp.exp(masked - peak_score[..., None])
    own_weight = jnp.exp(own_score - peak_score)
    denominator = lax.optimization_barrier(jnp.sum(weights, axis=-1)) + own_weight
    probability = (weights / denominator[..., None]).astype(jnp.bfloat16)
    own_prob = (own_weight / denominator).astype(jnp.bfloat16)
    mixed_rows = jnp.einsum('gij,gjd->gid', probability.astype(jnp.float32), value_rows.astype(jnp.float32))
    mixed_rows = mixed_rows + own_prob.astype(jnp.float32)[..., None] * own_value.astype(jnp.float32)[:, None, :]
    return mixed_rows.astype(jnp.bfloat16)

def reference(tokens, input_norm_gain, query_matrix, key_matrix, value_matrix, output_matrix, rotated_key_cache, cached_value_rows, cache_length_per_row, row_adapter_index, query_down_maps, query_up_maps, value_down_maps, value_up_maps):
    normed = rms_norm(tokens, input_norm_gain)
    base_query = jnp.dot(normed, query_matrix, preferred_element_type=jnp.float32)
    base_key = jnp.dot(normed, key_matrix, preferred_element_type=jnp.float32)
    base_value = jnp.dot(normed, value_matrix, preferred_element_type=jnp.float32)

    def adapt_row(row_items):
        normed_row, adapter = row_items
        gathered_results = []
        for down_map_table, up_map_table in ((query_down_maps, query_up_maps), (value_down_maps, value_up_maps)):
            shrink = jnp.dot(down_map_table[adapter], normed_row, preferred_element_type=jnp.float32)
            low_part = shrink.astype(jnp.bfloat16)
            expanded_rows = jnp.dot(low_part, up_map_table[adapter], preferred_element_type=jnp.float32)
            gathered_results.append((expanded_rows * adapter_scale).astype(jnp.bfloat16))
        return (gathered_results[0], gathered_results[1])
    delta_query, delta_value = lax.map(adapt_row, (normed, row_adapter_index))
    group_size = QUERY_HEADS // KEY_VALUE_HEADS
    query_full = base_query + delta_query.astype(jnp.float32)
    query = rotate(query_full.reshape(ROWS, QUERY_HEADS, HEAD_WIDTH), cache_length_per_row).astype(jnp.bfloat16).reshape(ROWS, KEY_VALUE_HEADS, group_size, HEAD_WIDTH)
    new_key = rotate(base_key.reshape(ROWS, KEY_VALUE_HEADS, HEAD_WIDTH), cache_length_per_row).astype(jnp.bfloat16)
    new_value = (base_value + delta_value.astype(jnp.float32)).astype(jnp.bfloat16).reshape(ROWS, KEY_VALUE_HEADS, HEAD_WIDTH)
    attended = lax.map(attend_row, (query, rotated_key_cache, cached_value_rows, new_key, new_value, cache_length_per_row))
    attended = attended.reshape(ROWS, QUERY_HEADS * HEAD_WIDTH)
    attn_out = jnp.dot(attended, output_matrix, preferred_element_type=jnp.float32).astype(jnp.bfloat16)
    return (attn_out, new_key.reshape(ROWS, KEY_VALUE_HEADS * HEAD_WIDTH), new_value.reshape(ROWS, KEY_VALUE_HEADS * HEAD_WIDTH))
```

```python
import functools
import math

import jax
import jax.numpy as jnp
from jax import lax
from jax.experimental import pallas as pl
from jax.experimental.pallas import tpu as pltpu
from jax.sharding import PartitionSpec as P

epsilon = 1e-05
adapter_scale = 0.5
rope_base = 500000.0
tile = 256
masked_score = -1e30


def params(mib):
    return pltpu.CompilerParams(vmem_limit_bytes=mib * 1024 * 1024)


def core_swap(x, pool_count):
    return lax.ppermute(x, "pool", [(p, p ^ 1) for p in range(pool_count)])


def chip_move(x, pool_count, d, e=0):
    chips = pool_count // 2
    return lax.ppermute(
        x,
        "pool",
        [(p, (p // 2 + d) % chips * 2 + ((p % 2) ^ e)) for p in range(pool_count)],
    )


def shrink_kernel(*refs):
    ids, *blocks, query_down, value_down, out = refs
    adapters = query_down.shape[0] // 16
    rows = blocks[0].shape[0]
    per = 2 if len(blocks) % 2 == 0 else 1
    for first in range(0, len(blocks), per):
        x = jnp.concatenate([b[...] for b in blocks[first : first + per]], axis=0)
        span = slice(first * rows, (first + per) * rows)
        label = ids[:, span].reshape(1, 1, per * rows)
        chosen = lax.broadcasted_iota(jnp.int32, (adapters, 1, per * rows), 0) == label
        for at, table in enumerate((query_down, value_down)):
            terms = lax.dot_general(
                table[...], x, (((1,), (1,)), ((), ())), preferred_element_type=jnp.float32
            ).reshape(adapters, 16, per * rows)
            out[at * 16 : (at + 1) * 16, span] = jnp.sum(jnp.where(chosen, terms, 0.0), axis=0)


def project_kernel(parts, block_count, *refs):
    ids = refs[0]
    lows = refs[1 : 1 + parts]
    blocks = refs[1 + parts : 1 + parts + block_count]
    wq, wk, wv, uq, uv, keep, send, xs, spread_q, spread_v = refs[1 + parts + block_count :]
    step = pl.program_id(0)
    last = pl.num_programs(0) - 1
    rows = blocks[0].shape[0]
    adapters = uq.shape[0] // 16
    total = rows * block_count

    @pl.when(step == 0)
    def _():
        for at, block in enumerate(blocks):
            xs[at * rows : (at + 1) * rows, :] = block[...]
        low = lows[0][...]
        for other in lows[1:]:
            low = low + other[...]
        low = low.astype(jnp.bfloat16).astype(jnp.float32) * adapter_scale
        chosen = lax.broadcasted_iota(jnp.int32, (adapters, 1, total), 0) == ids[...].reshape(
            1, 1, total
        )
        for at, spread in enumerate((spread_q, spread_v)):
            wide = jnp.where(chosen, low[at * 16 : (at + 1) * 16][None], 0.0)
            spread[...] = wide.reshape(adapters * 16, total).T.astype(jnp.bfloat16)

    def write(acc):
        for d in range(block_count // 2):
            at = 2 * d * rows
            keep[d] = acc[at : at + rows]
            send[d] = acc[at + rows : at + 2 * rows].astype(jnp.bfloat16)

    @pl.when(step < last)
    def _():
        write(
            jnp.dot(xs[...], wq[...], preferred_element_type=jnp.float32)
            + jnp.dot(spread_q[...], uq[...], preferred_element_type=jnp.float32)
        )

    @pl.when(step == last)
    def _():
        both = jnp.concatenate([wk[...], wv[...]], axis=1)
        acc = jnp.dot(xs[...], both, preferred_element_type=jnp.float32)
        extra = jnp.dot(spread_v[...], uv[...], preferred_element_type=jnp.float32)
        write(jnp.concatenate([acc[:, : wk.shape[1]], acc[:, wk.shape[1] :] + extra], axis=1))


def project(g, kv_heads, ids, lows, blocks, wq, wk, wv, uq, uv):
    rows, width = blocks[0].shape
    block_count = len(blocks)
    total = rows * block_count
    query_cols = wq.shape[1] // kv_heads
    head = wk.shape[1] // kv_heads
    steps = query_cols // tile
    columns = query_cols + 2 * head
    slots = uq.shape[0]

    def whole(x):
        return pl.BlockSpec(x.shape, lambda i: (0,) * x.ndim)

    def query_block(i):
        return (0, g * steps + jnp.minimum(i, steps - 1))

    def out_spec():
        return pl.BlockSpec((block_count // 2, rows, tile), lambda i: (0, 0, i))

    return pl.pallas_call(
        functools.partial(project_kernel, len(lows), block_count),
        grid=(steps + 1,),
        in_specs=[
            whole(ids),
            *[whole(x) for x in lows],
            *[whole(x) for x in blocks],
            pl.BlockSpec((width, tile), query_block),
            pl.BlockSpec((width, head), lambda i: (0, g)),
            pl.BlockSpec((width, head), lambda i: (0, g)),
            pl.BlockSpec((slots, tile), query_block),
            pl.BlockSpec((slots, head), lambda i: (0, g)),
        ],
        out_specs=[out_spec(), out_spec()],
        out_shape=[
            jax.ShapeDtypeStruct((block_count // 2, rows, columns), jnp.float32),
            jax.ShapeDtypeStruct((block_count // 2, rows, columns), jnp.bfloat16),
        ],
        scratch_shapes=[
            pltpu.VMEM((total, width), jnp.bfloat16),
            pltpu.VMEM((total, slots), jnp.bfloat16),
            pltpu.VMEM((total, slots), jnp.bfloat16),
        ],
        compiler_params=params(40),
        cost_estimate=pl.CostEstimate(
            flops=2 * total * (width + slots) * columns,
            bytes_accessed=2 * (width + slots) * columns + 6 * total * columns // 2,
            transcendentals=0,
        ),
        name=f"project_{g}",
    )(ids, *lows, *blocks, wq, wk, wv, uq, uv)


def attend_kernel(arrived, *refs):
    keep, swapped = refs[:2]
    moved = refs[2 : 2 + arrived]
    scale, cosines, sines, lengths, keys, values, out, key_out, value_out = refs[2 + arrived :]
    head = cosines.shape[1]
    rows_block = out.shape[0]
    group = out.shape[1] // head
    cache = keys.shape[2]
    score_scale = 1.0 / math.sqrt(head)
    sub = 8
    for pair in range(rows_block // 16):
        attended, new_keys, new_values = [], [], []
        for half in range(2):
            at = pair * 16 + half * sub
            r = slice(at, at + sub)
            x = keep[0, r] + swapped[0, r].astype(jnp.float32)
            for m in moved:
                x = x + m[r].astype(jnp.float32)
            x = x * scale[r]
            cos, sin = cosines[r], sines[r]

            def turn(v):
                return v * cos + pltpu.roll(v, head // 2, 1) * sin

            query = jnp.concatenate(
                [turn(x[:, h * head : (h + 1) * head]) for h in range(group)], axis=0
            ).astype(jnp.bfloat16)
            new_key = turn(x[:, group * head : (group + 1) * head]).astype(jnp.bfloat16)
            new_value = x[:, (group + 1) * head :].astype(jnp.bfloat16)
            k = keys[r, 0].reshape(sub * cache, head)
            v = values[r, 0].reshape(sub * cache, head)
            scores = (
                lax.dot_general(
                    query, k, (((1,), (1,)), ((), ())), preferred_element_type=jnp.float32
                )
                * score_scale
            )
            column = lax.broadcasted_iota(jnp.int32, (sub, sub * cache), 1)
            row = lax.broadcasted_iota(jnp.int32, (sub, sub * cache), 0)
            start = row * cache
            inside = (column >= start) & (column < start + lengths[r])
            own_key = jnp.concatenate([new_key.astype(jnp.float32)] * group, axis=0)
            own = (
                jnp.sum(query.astype(jnp.float32) * own_key, axis=1, keepdims=True) * score_scale
            )
            scores = jnp.where(
                inside[None], scores.reshape(group, sub, sub * cache), masked_score
            ).reshape(group * sub, sub * cache)
            peak = jnp.maximum(jnp.max(scores, axis=1, keepdims=True), own)
            weights = jnp.exp(scores - peak)
            own_weight = jnp.exp(own - peak)
            inverse = 1.0 / (jnp.sum(weights, axis=1, keepdims=True) + own_weight)
            mixed = jnp.dot(weights.astype(jnp.bfloat16), v, preferred_element_type=jnp.float32)
            own_value = jnp.concatenate([new_value.astype(jnp.float32)] * group, axis=0)
            mixed = (mixed + own_weight * own_value) * inverse
            attended.append(
                jnp.concatenate([mixed[h * sub : (h + 1) * sub] for h in range(group)], axis=1)
            )
            new_keys.append(new_key.astype(jnp.float32))
            new_values.append(new_value.astype(jnp.float32))
        r = slice(pair * 16, pair * 16 + 16)
        out[r] = jnp.concatenate(attended, axis=0).astype(jnp.bfloat16)
        key_out[r] = jnp.concatenate(new_keys, axis=0).astype(jnp.bfloat16)
        value_out[r] = jnp.concatenate(new_values, axis=0).astype(jnp.bfloat16)


def attend(g, keep, swapped, moved, scale, cosines, sines, lengths, keys, values):
    _, rows, columns = keep.shape
    head = keys.shape[3]
    cache = keys.shape[2]
    query_cols = columns - 2 * head
    block = 32 if rows % 32 == 0 else 16

    def by_rows(x):
        return pl.BlockSpec((block, x.shape[1]), lambda i: (i, 0))

    first = pl.BlockSpec((1, block, columns), lambda i: (0, i, 0))
    cached = pl.BlockSpec((block, 1, cache, head), lambda i: (i, g, 0, 0))
    return pl.pallas_call(
        functools.partial(attend_kernel, len(moved)),
        grid=(rows // block,),
        in_specs=[
            first,
            first,
            *[by_rows(x) for x in moved],
            by_rows(scale),
            by_rows(cosines),
            by_rows(sines),
            by_rows(lengths),
            cached,
            cached,
        ],
        out_specs=[
            pl.BlockSpec((block, query_cols), lambda i: (i, 0)),
            pl.BlockSpec((block, head), lambda i: (i, 0)),
            pl.BlockSpec((block, head), lambda i: (i, 0)),
        ],
        out_shape=[
            jax.ShapeDtypeStruct((rows, query_cols), jnp.bfloat16),
            jax.ShapeDtypeStruct((rows, head), jnp.bfloat16),
            jax.ShapeDtypeStruct((rows, head), jnp.bfloat16),
        ],
        compiler_params=params(32),
        cost_estimate=pl.CostEstimate(
            flops=4 * rows * 8 * cache * query_cols,
            bytes_accessed=4 * rows * cache * head + 8 * rows * columns,
            transcendentals=rows * 8 * cache * query_cols // head,
        ),
        name=f"attend_{g}",
    )(keep, swapped, *moved, scale, cosines, sines, lengths, keys, values)


def output_kernel(heads, *refs):
    order = refs[0]
    weights, out, xs = refs[-3:]
    blocks = refs[1:-3]
    rows, width = blocks[0].shape

    @pl.when(pl.program_id(0) == 0)
    def _():
        for at, block in enumerate(blocks):
            b, g = at // heads, at % heads
            xs[b * rows : (b + 1) * rows, g * width : (g + 1) * width] = block[...]

    acc = jnp.dot(xs[...], weights[...], preferred_element_type=jnp.float32).astype(jnp.bfloat16)
    for b in range(len(blocks) // heads):
        to = pl.multiple_of(order[b] * rows, rows)
        out[pl.ds(to, rows), :] = acc[b * rows : (b + 1) * rows]


def output_part(half, halves, heads, order, blocks, weights):
    rows, width = blocks[0].shape
    depth, columns = weights.shape
    steps = columns // halves // tile
    total = rows * len(blocks) // heads
    return pl.pallas_call(
        functools.partial(output_kernel, heads),
        grid=(steps,),
        in_specs=[
            pl.BlockSpec(memory_space=pltpu.SMEM),
            *[pl.BlockSpec(x.shape, lambda i: (0, 0)) for x in blocks],
            pl.BlockSpec((depth, tile), lambda i: (0, half * steps + i)),
        ],
        out_specs=pl.BlockSpec((total, tile), lambda i: (0, i)),
        out_shape=jax.ShapeDtypeStruct((total, columns // halves), jnp.bfloat16),
        scratch_shapes=[pltpu.VMEM((total, depth), jnp.bfloat16)],
        compiler_params=params(40),
        cost_estimate=pl.CostEstimate(
            flops=2 * total * depth * columns // halves,
            bytes_accessed=2 * depth * columns // halves + 2 * total * depth,
            transcendentals=0,
        ),
        name=f"output_{half}",
    )(order, *blocks, weights)


def line_sum(partial, n):
    z = lax.axis_index("tp")
    rows = partial.shape[0] // n

    def block(b):
        return lax.dynamic_slice_in_dim(partial, jnp.clip(b, 0, n - 1) * rows, rows, 0).astype(
            jnp.float32
        )

    right = left = None
    for s in range(1, n):
        go_right = block(n - s + z)
        go_left = block(z + s - n)
        if s > 1:
            go_right = go_right + right.astype(jnp.float32)
            go_left = go_left + left.astype(jnp.float32)
        right = lax.ppermute(
            go_right.astype(jnp.bfloat16), "tp", [(i, i + 1) for i in range(s)]
        )
        left = lax.ppermute(
            go_left.astype(jnp.bfloat16), "tp", [(n - 1 - i, n - 2 - i) for i in range(s)]
        )
    own = block(z)
    return (own + right.astype(jnp.float32) + left.astype(jnp.float32)).astype(jnp.bfloat16)


def shards(
    tokens,
    input_norm_gain,
    query_matrix,
    key_matrix,
    value_matrix,
    output_matrix,
    rotated_key_cache,
    cached_value_rows,
    cache_length_per_row,
    row_adapter_index,
    query_down_maps,
    query_up_maps,
    value_down_maps,
    value_up_maps,
):
    pool_count = lax.axis_size("pool")
    tp_count = lax.axis_size("tp")
    chips = pool_count // 2
    pool_at = lax.axis_index("pool")
    tp_at = lax.axis_index("tp")
    chip, core = pool_at // 2, pool_at % 2
    rows = tokens.shape[0]
    adapters, rank, piece = query_down_maps.shape
    base = query_matrix.shape[0]
    kv_heads = rotated_key_cache.shape[1]
    head = rotated_key_cache.shape[3]

    def scaled(start, width):
        x = lax.dynamic_slice_in_dim(tokens, start, width, 1).astype(jnp.float32)
        gain = lax.dynamic_slice_in_dim(input_norm_gain, start, width, 0).astype(jnp.float32)
        return (x * gain[None, :]).astype(jnp.bfloat16)

    def gather_pool(x):
        same = [x] + [chip_move(x, pool_count, d) for d in range(1, chips)]
        return [b for s in same for b in (s, core_swap(s, pool_count))]

    adapter_rows = gather_pool(scaled(tp_at * piece, piece))
    local_ids = (
        jnp.concatenate(gather_pool(row_adapter_index.reshape(1, rows)), axis=1)
        - pool_at * adapters
    )

    blocks = []
    for d in range(chips):
        for e in range(2):
            target = (chip + d) % chips * 2 + (core + e) % 2
            x = scaled(target * base, base)
            blocks.append(x if d == e == 0 else chip_move(x, pool_count, d, e))

    shrunk = pl.pallas_call(
        shrink_kernel,
        out_shape=jax.ShapeDtypeStruct((2 * rank, rows * pool_count), jnp.float32),
        compiler_params=params(40),
        cost_estimate=pl.CostEstimate(
            flops=4 * adapters * rank * piece * rows * pool_count,
            bytes_accessed=4 * adapters * rank * piece + 2 * piece * rows * pool_count,
            transcendentals=0,
        ),
        name="shrink",
    )(
        local_ids,
        *adapter_rows,
        query_down_maps.reshape(adapters * rank, piece),
        value_down_maps.reshape(adapters * rank, piece),
    )
    lows = [shrunk] + [
        lax.ppermute(shrunk, "tp", [(i, (i + d) % tp_count) for i in range(tp_count)])
        for d in range(1, tp_count)
    ]

    values = tokens.astype(jnp.float32)
    scale = lax.rsqrt(jnp.mean(values * values, axis=-1, keepdims=True) + epsilon)
    half_dim = head // 2
    frequency = jnp.power(
        jnp.float32(rope_base), jnp.arange(half_dim, dtype=jnp.float32) * (-2.0 / head)
    )
    angles = cache_length_per_row.astype(jnp.float32)[:, None] * frequency[None, :]
    cosines = jnp.concatenate([jnp.cos(angles)] * 2, axis=1)
    sines = jnp.concatenate([-jnp.sin(angles), jnp.sin(angles)], axis=1)
    lengths = cache_length_per_row.reshape(rows, 1)

    up_q = query_up_maps.reshape(adapters * rank, query_up_maps.shape[2])
    up_v = value_up_maps.reshape(adapters * rank, value_up_maps.shape[2])
    attended, new_keys, new_values = [], [], []
    for g in range(kv_heads):
        keep, send = project(
            g,
            kv_heads,
            local_ids,
            lows,
            blocks,
            query_matrix,
            key_matrix,
            value_matrix,
            up_q,
            up_v,
        )
        moved = []
        for d in range(1, chips):
            both = keep[d] + core_swap(send[d], pool_count).astype(jnp.float32)
            moved.append(chip_move(both.astype(jnp.bfloat16), pool_count, -d))
        swapped = core_swap(send[:1], pool_count)
        out, new_key, new_value = attend(
            g,
            keep,
            swapped,
            moved,
            scale,
            cosines,
            sines,
            lengths,
            rotated_key_cache,
            cached_value_rows,
        )
        attended.append(gather_pool(out))
        new_keys.append(new_key)
        new_values.append(new_value)

    order = jnp.stack(
        [(chip - d) % chips * 2 + (core + e) % 2 for d in range(chips) for e in range(2)]
    ).astype(jnp.int32)
    halves = 2
    columns = []
    for half in range(halves):
        partial = output_part(
            half,
            halves,
            kv_heads,
            order,
            [attended[g][b] for b in range(pool_count) for g in range(kv_heads)],
            output_matrix,
        )
        columns.append(line_sum(partial, tp_count))
    return (
        jnp.concatenate(columns, axis=1),
        jnp.concatenate(new_keys, axis=1),
        jnp.concatenate(new_values, axis=1),
    )


def solution(mesh):
    return jax.shard_map(
        shards,
        mesh=mesh,
        in_specs=(
            P(("groups", "pool"), None),
            P(),
            P("pool", "tp"),
            P("pool", "tp"),
            P("pool", "tp"),
            P("tp", "pool"),
            P(("groups", "pool"), "tp", None, None),
            P(("groups", "pool"), "tp", None, None),
            P(("groups", "pool")),
            P(("groups", "pool")),
            P("pool", None, "tp"),
            P("pool", None, "tp"),
            P("pool", None, "tp"),
            P("pool", None, "tp"),
        ),
        out_specs=(
            P(("groups", "tp"), "pool"),
            P(("groups", "pool"), "tp"),
            P(("groups", "pool"), "tp"),
        ),
        check_vma=False,
    )
```

```python
import functools
import math

import jax
import jax.numpy as jnp
from jax import lax
from jax.experimental import pallas as pl
from jax.experimental.pallas import tpu as pltpu
from jax.sharding import PartitionSpec as P

epsilon = 1e-05
adapter_scale = 0.5
rope_base = 500000.0
masked_score = -1e30


def params(mib):
    return pltpu.CompilerParams(vmem_limit_bytes=mib * 1024 * 1024)


def core_swap(x, pool_count):
    return lax.ppermute(x, "pool", [(p, p ^ 1) for p in range(pool_count)])


def chip_move(x, pool_count, d, e=0):
    chips = pool_count // 2
    return lax.ppermute(
        x,
        "pool",
        [(p, (p // 2 + d) % chips * 2 + ((p % 2) ^ e)) for p in range(pool_count)],
    )


def shrink_kernel(*refs):
    ids, *blocks, query_down, value_down, out = refs
    adapters = query_down.shape[0] // 16
    rows = blocks[0].shape[0]
    per = 2 if len(blocks) % 2 == 0 else 1
    for first in range(0, len(blocks), per):
        x = jnp.concatenate([b[...] for b in blocks[first : first + per]], axis=0)
        span = slice(first * rows, (first + per) * rows)
        label = ids[:, span].reshape(1, 1, per * rows)
        chosen = lax.broadcasted_iota(jnp.int32, (adapters, 1, per * rows), 0) == label
        for at, table in enumerate((query_down, value_down)):
            terms = lax.dot_general(
                table[...], x, (((1,), (1,)), ((), ())), preferred_element_type=jnp.float32
            ).reshape(adapters, 16, per * rows)
            out[at * 16 : (at + 1) * 16, span] = jnp.sum(jnp.where(chosen, terms, 0.0), axis=0)


def project_kernel(parts, chunks, *refs):
    ids = refs[0]
    lows = refs[1 : 1 + parts]
    blocks = refs[1 + parts : 3 + parts]
    wq, wk, wv, uq, uv, keep, *sends, xs, spread_q, spread_v = refs[3 + parts :]
    step = pl.program_id(0)
    last = pl.num_programs(0) - 1
    rows = blocks[0].shape[0]
    adapters = uq.shape[0] // 16
    total = 2 * rows

    @pl.when(step == 0)
    def _():
        for at, block in enumerate(blocks):
            xs[at * rows : (at + 1) * rows, :] = block[...]
        low = lows[0][...]
        for other in lows[1:]:
            low = low + other[...]
        low = low.astype(jnp.bfloat16).astype(jnp.float32) * adapter_scale
        chosen = lax.broadcasted_iota(jnp.int32, (adapters, 1, total), 0) == ids[...].reshape(
            1, 1, total
        )
        for at, spread in enumerate((spread_q, spread_v)):
            wide = jnp.where(chosen, low[at * 16 : (at + 1) * 16][None], 0.0)
            spread[...] = wide.reshape(adapters * 16, total).T.astype(jnp.bfloat16)

    def write(acc, columns):
        keep[:, columns] = acc[:rows]
        part = rows // chunks
        for c, send in enumerate(sends):
            at = rows + c * part
            send[:, columns] = acc[at : at + part].astype(jnp.bfloat16)

    @pl.when(step < last)
    def _():
        write(
            jnp.dot(xs[...], wq[...], preferred_element_type=jnp.float32)
            + jnp.dot(spread_q[...], uq[...], preferred_element_type=jnp.float32),
            slice(None),
        )

    @pl.when(step == last)
    def _():
        kv = wk.shape[1]
        write(jnp.dot(xs[...], wk[...], preferred_element_type=jnp.float32), slice(0, kv))
        write(
            jnp.dot(xs[...], wv[...], preferred_element_type=jnp.float32)
            + jnp.dot(spread_v[...], uv[...], preferred_element_type=jnp.float32),
            slice(kv, 2 * kv),
        )


def project(d, chunks, ids, lows, blocks, wq, wk, wv, uq, uv):
    rows, width = blocks[0].shape
    total = 2 * rows
    query_cols, kv_cols = wq.shape[1], wk.shape[1]
    tile = 2 * kv_cols
    steps = query_cols // tile
    columns = query_cols + tile
    slots = uq.shape[0]
    part = rows // chunks

    def whole(x):
        return pl.BlockSpec(x.shape, lambda i: (0, 0))

    def lanes(x):
        return pl.BlockSpec((x.shape[0], total), lambda i: (0, d))

    def query_block(i):
        return (0, jnp.minimum(i, steps - 1))

    keep, *sends = pl.pallas_call(
        functools.partial(project_kernel, len(lows), chunks),
        grid=(steps + 1,),
        in_specs=[
            lanes(ids),
            *[lanes(x) for x in lows],
            *[whole(x) for x in blocks],
            pl.BlockSpec((width, tile), query_block),
            whole(wk),
            whole(wv),
            pl.BlockSpec((slots, tile), query_block),
            whole(uv),
        ],
        out_specs=[
            pl.BlockSpec((rows, tile), lambda i: (0, i)),
            *[pl.BlockSpec((part, tile), lambda i: (0, i))] * chunks,
        ],
        out_shape=[
            jax.ShapeDtypeStruct((rows, columns), jnp.float32),
            *[jax.ShapeDtypeStruct((part, columns), jnp.bfloat16)] * chunks,
        ],
        scratch_shapes=[
            pltpu.VMEM((total, width), jnp.bfloat16),
            pltpu.VMEM((total, slots), jnp.bfloat16),
            pltpu.VMEM((total, slots), jnp.bfloat16),
        ],
        compiler_params=params(40),
        cost_estimate=pl.CostEstimate(
            flops=2 * total * (width + slots) * columns,
            bytes_accessed=2 * (width + slots) * columns + 6 * rows * columns,
            transcendentals=0,
        ),
        name=f"project_{d}",
    )(ids, *lows, *blocks, wq, wk, wv, uq, uv)
    return keep, sends


def attend_kernel(arrived, *refs):
    keep, swapped = refs[:2]
    moved = refs[2 : 2 + arrived]
    scale, cosines, sines, lengths, keys, values, out, key_out, value_out = refs[2 + arrived :]
    head = cosines.shape[1]
    rows_block = out.shape[0]
    _, kv_heads, cache, _ = keys.shape
    heads = out.shape[1] // head
    group = heads // kv_heads
    score_scale = 1.0 / math.sqrt(head)
    sub = 8
    column = lax.broadcasted_iota(jnp.int32, (sub, sub * cache), 1)
    start = lax.broadcasted_iota(jnp.int32, (sub, sub * cache), 0) * cache
    for pair in range(rows_block // 16):
        attended, new_keys, new_values = [], [], []
        for half in range(2):
            at = pair * 16 + half * sub
            r = slice(at, at + sub)
            x = keep[r] + swapped[r].astype(jnp.float32)
            for m in moved:
                x = x + m[r].astype(jnp.float32)
            x = x * scale[r]
            cos, sin = cosines[r], sines[r]
            inside = (column >= start) & (column < start + lengths[r])

            def piece(i):
                return x[:, i * head : (i + 1) * head]

            def turn(v):
                return v * cos + pltpu.roll(v, head // 2, 1) * sin

            for g in range(kv_heads):
                query = jnp.concatenate(
                    [turn(piece(g * group + h)) for h in range(group)], axis=0
                ).astype(jnp.bfloat16)
                new_key = turn(piece(heads + g)).astype(jnp.bfloat16).astype(jnp.float32)
                new_value = piece(heads + kv_heads + g).astype(jnp.bfloat16).astype(jnp.float32)
                k = keys[r, g].reshape(sub * cache, head)
                v = values[r, g].reshape(sub * cache, head)
                scores = (
                    lax.dot_general(
                        query, k, (((1,), (1,)), ((), ())), preferred_element_type=jnp.float32
                    )
                    * score_scale
                )
                own_key = jnp.concatenate([new_key] * group, axis=0)
                own = (
                    jnp.sum(query.astype(jnp.float32) * own_key, axis=1, keepdims=True)
                    * score_scale
                )
                scores = jnp.where(
                    inside[None], scores.reshape(group, sub, sub * cache), masked_score
                ).reshape(group * sub, sub * cache)
                peak = jnp.maximum(jnp.max(scores, axis=1, keepdims=True), own)
                weights = jnp.exp(scores - peak)
                own_weight = jnp.exp(own - peak)
                inverse = 1.0 / (jnp.sum(weights, axis=1, keepdims=True) + own_weight)
                mixed = jnp.dot(weights.astype(jnp.bfloat16), v, preferred_element_type=jnp.float32)
                own_value = jnp.concatenate([new_value] * group, axis=0)
                mixed = (mixed + own_weight * own_value) * inverse
                attended += [mixed[h * sub : (h + 1) * sub] for h in range(group)]
                new_keys.append(new_key)
                new_values.append(new_value)
        r = slice(pair * 16, pair * 16 + 16)

        def both(pieces):
            n = len(pieces) // 2
            return jnp.concatenate(
                [jnp.concatenate([pieces[i], pieces[n + i]], axis=0) for i in range(n)], axis=1
            ).astype(jnp.bfloat16)

        out[r] = both(attended)
        key_out[r] = both(new_keys)
        value_out[r] = both(new_values)


def attend(c, chunks, keep, swapped, moved, scale, cosines, sines, lengths, keys, values):
    rows, columns = keep.shape
    _, kv_heads, cache, head = keys.shape
    kv_cols = kv_heads * head
    query_cols = columns - 2 * kv_cols
    part = rows // chunks
    block = 32 if part % 32 == 0 else 16
    steps = part // block

    def own(x):
        return pl.BlockSpec((block, x.shape[1]), lambda i: (c * steps + i, 0))

    cached = pl.BlockSpec((block, kv_heads, cache, head), lambda i: (c * steps + i, 0, 0, 0))
    widths = (query_cols, kv_cols, kv_cols)
    return pl.pallas_call(
        functools.partial(attend_kernel, len(moved)),
        grid=(steps,),
        in_specs=[
            own(keep),
            pl.BlockSpec((block, columns), lambda i: (i, 0)),
            *[pl.BlockSpec((block, columns), lambda i: (i, 0)) for _ in moved],
            own(scale),
            own(cosines),
            own(sines),
            own(lengths),
            cached,
            cached,
        ],
        out_specs=[pl.BlockSpec((block, w), lambda i: (i, 0)) for w in widths],
        out_shape=[jax.ShapeDtypeStruct((part, w), jnp.bfloat16) for w in widths],
        compiler_params=params(32),
        cost_estimate=pl.CostEstimate(
            flops=4 * part * 8 * cache * query_cols,
            bytes_accessed=4 * part * cache * kv_cols + 8 * part * columns,
            transcendentals=part * 8 * cache * query_cols // head,
        ),
        name=f"attend_{c}",
    )(keep, swapped, *moved, scale, cosines, sines, lengths, keys, values)


def output_kernel(*refs):
    order, *blocks, weights, out, xs = refs
    rows = blocks[0].shape[0]

    @pl.when(pl.program_id(0) == 0)
    def _():
        for b, block in enumerate(blocks):
            xs[b * rows : (b + 1) * rows, :] = block[...]

    acc = jnp.dot(xs[...], weights[...], preferred_element_type=jnp.float32).astype(jnp.bfloat16)
    for b in range(len(blocks)):
        to = pl.multiple_of(order[b] * rows, rows)
        out[pl.ds(to, rows), :] = acc[b * rows : (b + 1) * rows]


def output_part(c, order, blocks, weights):
    rows = blocks[0].shape[0]
    depth, columns = weights.shape
    tile = 512 if columns % 512 == 0 else columns
    total = rows * len(blocks)
    return pl.pallas_call(
        output_kernel,
        grid=(columns // tile,),
        in_specs=[
            pl.BlockSpec(memory_space=pltpu.SMEM),
            *[pl.BlockSpec(x.shape, lambda i: (0, 0)) for x in blocks],
            pl.BlockSpec((depth, tile), lambda i: (0, i)),
        ],
        out_specs=pl.BlockSpec((total, tile), lambda i: (0, i)),
        out_shape=jax.ShapeDtypeStruct((total, columns), jnp.bfloat16),
        scratch_shapes=[pltpu.VMEM((total, depth), jnp.bfloat16)],
        compiler_params=params(40),
        cost_estimate=pl.CostEstimate(
            flops=2 * total * depth * columns,
            bytes_accessed=2 * depth * columns + 2 * total * (depth + columns),
            transcendentals=0,
        ),
        name=f"output_{c}",
    )(order, *blocks, weights)


def shards(
    tokens,
    input_norm_gain,
    query_matrix,
    key_matrix,
    value_matrix,
    output_matrix,
    rotated_key_cache,
    cached_value_rows,
    cache_length_per_row,
    row_adapter_index,
    query_down_maps,
    query_up_maps,
    value_down_maps,
    value_up_maps,
):
    pool_count = lax.axis_size("pool")
    tp_count = lax.axis_size("tp")
    chips = pool_count // 2
    pool_at = lax.axis_index("pool")
    tp_at = lax.axis_index("tp")
    chip, core = pool_at // 2, pool_at % 2
    rows = tokens.shape[0]
    adapters, rank, piece = query_down_maps.shape
    base = query_matrix.shape[0]
    kv_heads = rotated_key_cache.shape[1]
    head = rotated_key_cache.shape[3]

    def scaled(start, width):
        x = lax.dynamic_slice_in_dim(tokens, start, width, 1).astype(jnp.float32)
        gain = lax.dynamic_slice_in_dim(input_norm_gain, start, width, 0).astype(jnp.float32)
        return (x * gain[None, :]).astype(jnp.bfloat16)

    def gather_pool(x):
        same = [x] + [chip_move(x, pool_count, d) for d in range(1, chips)]
        return [b for s in same for b in (s, core_swap(s, pool_count))]

    first = scaled(tp_at * piece, piece)
    first, tokens, input_norm_gain = lax.optimization_barrier((first, tokens, input_norm_gain))
    adapter_rows = gather_pool(first)
    local_ids = (
        jnp.concatenate(gather_pool(row_adapter_index.reshape(1, rows)), axis=1)
        - pool_at * adapters
    )

    blocks = []
    for d in range(chips):
        for e in range(2):
            target = (chip + d) % chips * 2 + (core + e) % 2
            x = scaled(target * base, base)
            blocks.append(x if d == e == 0 else chip_move(x, pool_count, d, e))

    shrunk = pl.pallas_call(
        shrink_kernel,
        out_shape=jax.ShapeDtypeStruct((2 * rank, rows * pool_count), jnp.float32),
        compiler_params=params(40),
        cost_estimate=pl.CostEstimate(
            flops=4 * adapters * rank * piece * rows * pool_count,
            bytes_accessed=4 * adapters * rank * piece + 2 * piece * rows * pool_count,
            transcendentals=0,
        ),
        name="shrink",
    )(
        local_ids,
        *adapter_rows,
        query_down_maps.reshape(adapters * rank, piece),
        value_down_maps.reshape(adapters * rank, piece),
    )
    lows = [shrunk] + [
        lax.ppermute(shrunk, "tp", [(i, (i + d) % tp_count) for i in range(tp_count)])
        for d in range(1, tp_count)
    ]

    values = tokens.astype(jnp.float32)
    scale = lax.rsqrt(jnp.mean(values * values, axis=-1, keepdims=True) + epsilon)
    half_dim = head // 2
    frequency = jnp.power(
        jnp.float32(rope_base), jnp.arange(half_dim, dtype=jnp.float32) * (-2.0 / head)
    )
    angles = cache_length_per_row.astype(jnp.float32)[:, None] * frequency[None, :]
    cosines = jnp.concatenate([jnp.cos(angles)] * 2, axis=1)
    sines = jnp.concatenate([-jnp.sin(angles), jnp.sin(angles)], axis=1)
    lengths = cache_length_per_row.reshape(rows, 1)

    up_q = query_up_maps.reshape(adapters * rank, query_up_maps.shape[2])
    up_v = value_up_maps.reshape(adapters * rank, value_up_maps.shape[2])
    weights = (query_matrix, key_matrix, value_matrix, up_q, up_v)
    chunks = 2
    own_sums, own_sends = project(0, chunks, local_ids, lows, blocks[:2], *weights)
    swapped = [core_swap(x, pool_count) for x in own_sends]
    moved = [[] for _ in range(chunks)]
    part = rows // chunks
    for d in range(1, chips):
        keep, sends = project(d, chunks, local_ids, lows, blocks[2 * d : 2 * d + 2], *weights)
        for c in range(chunks):
            both = keep[c * part : (c + 1) * part] + core_swap(sends[c], pool_count).astype(
                jnp.float32
            )
            moved[c].append(chip_move(both.astype(jnp.bfloat16), pool_count, -d))

    order = jnp.stack(
        [(chip - d) % chips * 2 + (core + e) % 2 for d in range(chips) for e in range(2)]
    ).astype(jnp.int32)
    outputs = []
    for c in range(chunks):
        attended, new_key, new_value = attend(
            c,
            chunks,
            own_sums,
            swapped[c],
            moved[c],
            scale,
            cosines,
            sines,
            lengths,
            rotated_key_cache,
            cached_value_rows,
        )
        partial = output_part(c, order, gather_pool(attended), output_matrix)
        summed = lax.psum_scatter(partial, "tp", scatter_dimension=0, tiled=True)
        outputs.append((summed.reshape(-1, part, summed.shape[1]), new_key, new_value))
    attn_out = jnp.concatenate([o[0] for o in outputs], axis=1)
    return (
        attn_out.reshape(-1, attn_out.shape[2]),
        jnp.concatenate([o[1] for o in outputs], axis=0),
        jnp.concatenate([o[2] for o in outputs], axis=0),
    )


def solution(mesh):
    return jax.shard_map(
        shards,
        mesh=mesh,
        in_specs=(
            P(("groups", "pool"), None),
            P(),
            P("pool", "tp"),
            P("pool", "tp"),
            P("pool", "tp"),
            P("tp", "pool"),
            P(("groups", "pool"), "tp", None, None),
            P(("groups", "pool"), "tp", None, None),
            P(("groups", "pool")),
            P(("groups", "pool")),
            P("pool", None, "tp"),
            P("pool", None, "tp"),
            P("pool", None, "tp"),
            P("pool", None, "tp"),
        ),
        out_specs=(
            P(("groups", "tp"), "pool"),
            P(("groups", "pool"), "tp"),
            P(("groups", "pool"), "tp"),
        ),
        check_vma=False,
    )
```

```python
import functools
import math

import jax
import jax.numpy as jnp
from jax import lax
from jax.experimental import pallas as pl
from jax.experimental.pallas import tpu as pltpu
from jax.sharding import PartitionSpec as P

epsilon = 1e-05
adapter_scale = 0.5
rope_base = 500000.0
masked_score = -1e30


def params():
    return pltpu.CompilerParams(vmem_limit_bytes=28 * 1024 * 1024)


VMEM = pl.BlockSpec(memory_space=pltpu.VMEM)
HBM = pl.BlockSpec(memory_space=pltpu.HBM)


def columns_of(ref, i, width):
    return ref.at[:, pl.ds(pl.multiple_of(i * width, width), width)]


def small_cost():
    return pl.CostEstimate(flops=1000, bytes_accessed=1000, transcendentals=0)


def after(x, *earlier):
    return lax.optimization_barrier((x, *earlier))[0]


def core_swap(x, pool_count):
    return lax.ppermute(x, "pool", [(p, p ^ 1) for p in range(pool_count)])


def chip_move(x, pool_count, d, e=0):
    chips = pool_count // 2
    return lax.ppermute(
        x,
        "pool",
        [(p, (p // 2 + d) % chips * 2 + ((p % 2) ^ e)) for p in range(pool_count)],
    )


def shrink_kernel(*refs):
    ids, *blocks, query_down, value_down, out, query_held, value_held, sems = refs
    tables = ((query_down, query_held), (value_down, value_held))
    copies = [
        pltpu.make_async_copy(far, near, sems.at[i]) for i, (far, near) in enumerate(tables)
    ]
    for copy in copies:
        copy.start()
    adapters = query_down.shape[0] // 16
    rows = blocks[0].shape[0]
    per = 2
    for at, (_, table) in enumerate(tables):
        copies[at].wait()
        for first in range(0, len(blocks), per):
            x = jnp.concatenate([b[...] for b in blocks[first : first + per]], axis=0)
            span = slice(first * rows, (first + per) * rows)
            label = ids[:, span].reshape(1, 1, per * rows)
            chosen = lax.broadcasted_iota(jnp.int32, (adapters, 1, per * rows), 0) == label
            terms = lax.dot_general(
                table[...], x, (((1,), (1,)), ((), ())), preferred_element_type=jnp.float32
            ).reshape(adapters, 16, per * rows)
            out[at * 16 : (at + 1) * 16, span] = jnp.sum(jnp.where(chosen, terms, 0.0), axis=0)


def spread_lows(low, ids, adapters):
    total = ids.shape[1]
    low = low.astype(jnp.bfloat16).astype(jnp.float32) * adapter_scale
    chosen = lax.broadcasted_iota(jnp.int32, (adapters, 1, total), 0) == ids.reshape(1, 1, total)
    return [
        jnp.where(chosen, low[at : at + 16][None], 0.0)
        .reshape(adapters * 16, total)
        .T.astype(jnp.bfloat16)
        for at in (0, 16)
    ]


def project_kernel(parts, n, spans, tile, window, *refs):
    ids = refs[0] if parts else None
    lows = refs[1 : 1 + parts]
    refs = refs[1 + parts :] if parts else refs
    count = 5 if parts else 3
    blocks, far, refs = refs[:n], refs[n : n + count], refs[n + count :]
    (keep, *sends), near, refs = refs[:4], refs[4 : 4 + count], refs[4 + count :]
    xs, sem_q, sem_v, *spreads = refs
    wq, wk, wv, *up = near
    steps = wq.shape[1] // tile
    first, rows = window
    wide = [(0, 0)] + ([(3, 1)] if parts else [])
    narrow = [(1, 0), (2, 1)] + ([(4, 2)] if parts else [])

    def wide_copy(which, slot, i):
        return pltpu.make_async_copy(
            columns_of(far[which], i, tile), columns_of(near[which], i, tile), sem_q.at[slot, i]
        )

    def narrow_copy(which, slot):
        return pltpu.make_async_copy(far[which], near[which], sem_v.at[slot])

    for i in range(steps):
        for which, slot in wide:
            wide_copy(which, slot, i).start()
    for which, slot in narrow:
        narrow_copy(which, slot).start()

    xs[:rows, :] = blocks[0][first : first + rows, :]
    at = rows
    for block in blocks[1:]:
        size = min(rows, block.shape[0])
        xs[at : at + size, :] = block[first : first + size, :]
        at += size
    if parts:
        low = lows[0][...]
        for other in lows[1:]:
            low = low + other[...]
        low = jnp.concatenate([low[:, at : at + rows] for at in spans], axis=1)
        label = jnp.concatenate([ids[:, at : at + rows] for at in spans], axis=1)
        for ref, value in zip(spreads, spread_lows(low, label, up[0].shape[0] // 16)):
            ref[...] = value

    def sums(w, spread=None, u=None):
        acc = jnp.dot(xs[...], w, preferred_element_type=jnp.float32)
        if u is not None:
            acc = acc + jnp.dot(spread[...], u, preferred_element_type=jnp.float32)
        return acc

    for half in range(2):

        @pl.loop(0, steps // 2)
        def _(j):
            i = half * (steps // 2) + j
            for which, slot in wide:
                wide_copy(which, slot, i).wait()
            columns = pl.ds(pl.multiple_of(i * tile, tile), tile)
            extra = (spreads[0], up[0][:, columns]) if parts else ()
            acc = sums(wq[:, columns], *extra)
            keep[:, columns] = acc[:rows]
            columns = pl.ds(pl.multiple_of(j * tile, tile), tile)
            sends[half][:, columns] = acc[rows:].astype(sends[half].dtype)

    for which, slot in narrow:
        narrow_copy(which, slot).wait()
    start, kv = wq.shape[1], wk.shape[1]
    for at, w in enumerate((wk, wv)):
        extra = (spreads[1], up[1][...]) if parts and at else ()
        acc = sums(w[...], *extra)
        keep[:, start + at * kv : start + (at + 1) * kv] = acc[:rows]
        sends[2][:, at * kv : (at + 1) * kv] = acc[rows:].astype(sends[2].dtype)


def project(name, blocks, wq, wk, wv, adapter=None, spans=None, window=None):
    rows, width = blocks[0].shape
    window = window or (0, rows)
    rows = window[1]
    tile = min(512, wq.shape[1] // 2)
    columns = wq.shape[1] + 2 * wk.shape[1]
    ids, lows, *up = adapter if adapter else (None, [])
    front = [ids, *lows] if adapter else []
    far = [wq, wk, wv, *up]
    send_type = jnp.bfloat16 if adapter else jnp.float32
    spreads = [pltpu.VMEM((2 * rows, u.shape[0]), jnp.bfloat16) for u in up]
    return pl.pallas_call(
        functools.partial(project_kernel, len(lows), len(blocks), spans, tile, window),
        in_specs=[VMEM] * (len(front) + len(blocks)) + [HBM] * len(far),
        out_specs=[VMEM] * 4,
        out_shape=[
            jax.ShapeDtypeStruct((rows, columns), jnp.float32),
            *[jax.ShapeDtypeStruct((rows, wq.shape[1] // 2), send_type)] * 2,
            jax.ShapeDtypeStruct((rows, 2 * wk.shape[1]), send_type),
        ],
        scratch_shapes=[
            *[pltpu.VMEM(x.shape, x.dtype) for x in far],
            pltpu.VMEM((2 * rows, width), jnp.bfloat16),
            pltpu.SemaphoreType.DMA((2, wq.shape[1] // tile)),
            pltpu.SemaphoreType.DMA((3,)),
            *spreads,
        ],
        compiler_params=params(),
        cost_estimate=small_cost(),
        name=name,
    )(*front, *blocks, *far)


def add_adapters_kernel(parts, tile, *refs):
    ids, *refs = refs
    lows, refs = refs[:parts], refs[parts:]
    keep0, low0, high0, kv0, far_q, far_v, keep, send, uq, uv, spread_q, spread_v, sems = refs
    copies = [
        pltpu.make_async_copy(far_q, uq, sems.at[0]),
        pltpu.make_async_copy(far_v, uv, sems.at[1]),
    ]
    for copy in copies:
        copy.start()
    rows = keep.shape[0]
    low = lows[0][:, : 2 * rows]
    for other in lows[1:]:
        low = low + other[:, : 2 * rows]
    both = spread_lows(low, ids[:, : 2 * rows], uq.shape[0] // 16)
    spread_q[...], spread_v[...] = both
    wide, kv = uq.shape[1], uv.shape[1]

    def write(extra, columns, at, at_columns):
        keep[:, columns] = keep0[:, columns] + extra[:rows]
        send[:, columns] = (at[:, at_columns] + extra[rows:]).astype(send.dtype)

    keep[:, wide : wide + kv] = keep0[:, wide : wide + kv]
    send[:, wide : wide + kv] = kv0[:, :kv].astype(send.dtype)
    copies[0].wait()

    for half, at in enumerate((low0, high0)):

        @pl.loop(0, wide // 2 // tile)
        def _(j):
            columns = pl.ds(pl.multiple_of(half * (wide // 2) + j * tile, tile), tile)
            extra = jnp.dot(spread_q[...], uq[:, columns], preferred_element_type=jnp.float32)
            write(extra, columns, at, pl.ds(pl.multiple_of(j * tile, tile), tile))

    copies[1].wait()
    extra = jnp.dot(spread_v[...], uv[...], preferred_element_type=jnp.float32)
    write(extra, slice(wide + kv, wide + 2 * kv), kv0, slice(kv, 2 * kv))


def add_adapters(keep, sends, adapter):
    ids, lows, uq, uv = adapter
    rows = keep.shape[0]
    spread = pltpu.VMEM((2 * rows, uq.shape[0]), jnp.bfloat16)
    return pl.pallas_call(
        functools.partial(add_adapters_kernel, len(lows), min(512, uq.shape[1] // 2)),
        in_specs=[VMEM] * (len(lows) + 5) + [HBM] * 2,
        out_specs=[VMEM] * 2,
        out_shape=[
            jax.ShapeDtypeStruct(keep.shape, jnp.float32),
            jax.ShapeDtypeStruct(keep.shape, jnp.bfloat16),
        ],
        scratch_shapes=[
            pltpu.VMEM(uq.shape, uq.dtype),
            pltpu.VMEM(uv.shape, uv.dtype),
            spread,
            spread,
            pltpu.SemaphoreType.DMA((2,)),
        ],
        compiler_params=params(),
        cost_estimate=small_cost(),
        name="add_adapters",
    )(ids, *lows, keep, *sends, uq, uv)


def attend_kernel(arrived, first_row, block, *refs):
    keep, swapped = refs[:2]
    moved = refs[2 : 2 + arrived]
    scale, cosines, sines, lengths, far_keys, far_values, *refs = refs[2 + arrived :]
    out, key_out, value_out, keys, values, sems = refs
    head = cosines.shape[1]
    rows = out.shape[0]
    _, kv_heads, cache, _ = keys.shape
    heads = out.shape[1] // head
    group = heads // kv_heads
    score_scale = 1.0 / math.sqrt(head)
    sub = 8

    def copies(i):
        to = pl.ds(pl.multiple_of(i * block, block), block)
        at = pl.ds(pl.multiple_of(first_row + i * block, block), block)
        return [
            pltpu.make_async_copy(far.at[at], near.at[to], sems.at[which, i])
            for which, (far, near) in enumerate(((far_keys, keys), (far_values, values)))
        ]

    for i in range(rows // block):
        for copy in copies(i):
            copy.start()

    column = lax.broadcasted_iota(jnp.int32, (sub, sub * cache), 1)
    start = lax.broadcasted_iota(jnp.int32, (sub, sub * cache), 0) * cache

    @pl.loop(0, rows // block)
    def _(i):
        for copy in copies(i):
            copy.wait()
        attended, new_keys, new_values = [], [], []
        for half in range(block // sub):
            here = pl.ds(pl.multiple_of(i * block + half * sub, sub), sub)
            whole = pl.ds(pl.multiple_of(first_row + i * block + half * sub, sub), sub)
            x = keep[whole] + swapped[whole].astype(jnp.float32)
            for m in moved:
                x = x + m[here].astype(jnp.float32)
            x = x * scale[whole]
            cos, sin = cosines[whole], sines[whole]
            inside = (column >= start) & (column < start + lengths[whole])

            def piece(i):
                return x[:, i * head : (i + 1) * head]

            def turn(v):
                return v * cos + pltpu.roll(v, head // 2, 1) * sin

            for g in range(kv_heads):
                query = jnp.concatenate(
                    [turn(piece(g * group + h)) for h in range(group)], axis=0
                ).astype(jnp.bfloat16)
                new_key = turn(piece(heads + g)).astype(jnp.bfloat16).astype(jnp.float32)
                new_value = piece(heads + kv_heads + g).astype(jnp.bfloat16).astype(jnp.float32)
                k = keys[here, g].reshape(sub * cache, head)
                v = values[here, g].reshape(sub * cache, head)
                scores = (
                    lax.dot_general(
                        query, k, (((1,), (1,)), ((), ())), preferred_element_type=jnp.float32
                    )
                    * score_scale
                )
                own_key = jnp.concatenate([new_key] * group, axis=0)
                own = (
                    jnp.sum(query.astype(jnp.float32) * own_key, axis=1, keepdims=True)
                    * score_scale
                )
                scores = jnp.where(
                    inside[None], scores.reshape(group, sub, sub * cache), masked_score
                ).reshape(group * sub, sub * cache)
                peak = jnp.maximum(jnp.max(scores, axis=1, keepdims=True), own)
                weights = jnp.exp(scores - peak)
                own_weight = jnp.exp(own - peak)
                inverse = 1.0 / (jnp.sum(weights, axis=1, keepdims=True) + own_weight)
                mixed = jnp.dot(weights.astype(jnp.bfloat16), v, preferred_element_type=jnp.float32)
                own_value = jnp.concatenate([new_value] * group, axis=0)
                mixed = (mixed + own_weight * own_value) * inverse
                attended += [mixed[h * sub : (h + 1) * sub] for h in range(group)]
                new_keys.append(new_key)
                new_values.append(new_value)
        r = pl.ds(pl.multiple_of(i * block, block), block)

        def joined(pieces):
            n = len(pieces) * sub // block
            return jnp.concatenate(
                [jnp.concatenate(pieces[j::n], axis=0) for j in range(n)], axis=1
            ).astype(jnp.bfloat16)

        out[r] = joined(attended)
        key_out[r] = joined(new_keys)
        value_out[r] = joined(new_values)


def attend(c, window, keep, swapped, moved, scale, cosines, sines, lengths, keys, values):
    rows, columns = keep.shape
    _, kv_heads, cache, head = keys.shape
    kv_cols = kv_heads * head
    first, part = window
    block = 16
    widths = (columns - 2 * kv_cols, kv_cols, kv_cols)
    held = pltpu.VMEM((part, kv_heads, cache, head), jnp.bfloat16)
    return pl.pallas_call(
        functools.partial(attend_kernel, len(moved), first, block),
        in_specs=[VMEM] * (len(moved) + 6) + [HBM] * 2,
        out_specs=[VMEM] * 3,
        out_shape=[jax.ShapeDtypeStruct((part, w), jnp.bfloat16) for w in widths],
        scratch_shapes=[held, held, pltpu.SemaphoreType.DMA((2, part // block))],
        compiler_params=params(),
        cost_estimate=small_cost(),
        name=f"attend_{c}",
    )(keep, swapped, *moved, scale, cosines, sines, lengths, keys, values)


def output_kernel(tile, *refs):
    order, *blocks, far, keep, send, weights, xs, sems = refs
    rows = blocks[0].shape[0]
    steps = far.shape[1] // tile

    def copy(i):
        return pltpu.make_async_copy(
            columns_of(far, i, tile), columns_of(weights, i, tile), sems.at[i]
        )

    for i in range(steps):
        copy(i).start()
    for b, block in enumerate(blocks):
        to = pl.multiple_of(order[b] * rows, rows)
        xs[pl.ds(to, rows), :] = block[...]
    half = keep.shape[0]

    @pl.loop(0, steps)
    def _(i):
        copy(i).wait()
        columns = pl.ds(pl.multiple_of(i * tile, tile), tile)
        acc = jnp.dot(xs[...], weights[:, columns], preferred_element_type=jnp.float32)
        keep[:, columns] = acc[:half].astype(jnp.bfloat16)
        send[:, columns] = acc[half:].astype(jnp.bfloat16)


def output_part(c, order, blocks, weights):
    rows = blocks[0].shape[0]
    depth, columns = weights.shape
    tile = min(512, columns)
    total = rows * len(blocks)
    half = jax.ShapeDtypeStruct((total // 2, columns), jnp.bfloat16)
    return pl.pallas_call(
        functools.partial(output_kernel, tile),
        in_specs=[pl.BlockSpec(memory_space=pltpu.SMEM), *[VMEM] * len(blocks), HBM],
        out_specs=[VMEM] * 2,
        out_shape=[half, half],
        scratch_shapes=[
            pltpu.VMEM(weights.shape, weights.dtype),
            pltpu.VMEM((total, depth), jnp.bfloat16),
            pltpu.SemaphoreType.DMA((columns // tile,)),
        ],
        compiler_params=params(),
        cost_estimate=small_cost(),
        name=f"output_{c}",
    )(order, *blocks, weights)


def reversed_bits(x, count):
    out, bit = 0, 1
    while bit < count:
        out = out * 2 + (x // bit) % 2
        bit *= 2
    return out


def halving_sum(keep, send, count, earlier):
    step, totals = 1, []
    while True:
        got = lax.ppermute(send, "tp", [(z, z ^ step) for z in range(count)])
        if earlier:
            got = after(got, earlier[len(totals)])
        total = keep.astype(jnp.float32) + got.astype(jnp.float32)
        totals.append(total)
        step *= 2
        if step == count:
            return total.astype(jnp.bfloat16), totals
        half = total.shape[0] // 2
        keep, send = total[:half], total[half:].astype(jnp.bfloat16)


def shards(
    tokens,
    input_norm_gain,
    query_matrix,
    key_matrix,
    value_matrix,
    output_matrix,
    rotated_key_cache,
    cached_value_rows,
    cache_length_per_row,
    row_adapter_index,
    query_down_maps,
    query_up_maps,
    value_down_maps,
    value_up_maps,
):
    pool_count = lax.axis_size("pool")
    tp_count = lax.axis_size("tp")
    chips = pool_count // 2
    pool_at = lax.axis_index("pool")
    tp_at = lax.axis_index("tp")
    chip, core = pool_at // 2, pool_at % 2
    rows = tokens.shape[0]
    adapters, rank, piece = query_down_maps.shape
    base = query_matrix.shape[0]
    kv_heads = rotated_key_cache.shape[1]
    head = rotated_key_cache.shape[3]

    def scaled(start, width):
        x = lax.dynamic_slice_in_dim(tokens, start, width, 1).astype(jnp.float32)
        gain = lax.dynamic_slice_in_dim(input_norm_gain, start, width, 0).astype(jnp.float32)
        return (x * gain[None, :]).astype(jnp.bfloat16)

    def gather_pool(x):
        same = [x] + [chip_move(x, pool_count, d) for d in range(1, chips)]
        return [b for s in same for b in (s, core_swap(s, pool_count))]

    first = scaled(tp_at * piece, piece)
    first, tokens, input_norm_gain = lax.optimization_barrier((first, tokens, input_norm_gain))
    same_core = [first] + [chip_move(first, pool_count, d) for d in range(1, chips)]
    local_ids = (
        jnp.concatenate(gather_pool(row_adapter_index.reshape(1, rows)), axis=1)
        - pool_at * adapters
    )

    cut = rows * 3 // 8
    chunks = [(0, cut), (cut, rows - cut)]
    own = scaled(pool_at * base, base)
    partner = scaled((pool_at // 2 * 2 + 1 - core) * base, base)
    partner = [
        core_swap(partner[at : at + rows // 2], pool_count) for at in range(0, rows, rows // 2)
    ]
    weights = (query_matrix, key_matrix, value_matrix)
    own_base, *own_sends = project("project_own", [own, *partner], *weights)
    same_core[1:] = [after(x, own_base) for x in same_core[1:]]
    adapter_rows = [b for x in same_core for b in (x, core_swap(x, pool_count))]
    tokens, input_norm_gain = lax.optimization_barrier((tokens, input_norm_gain, own_base))[:2]

    remote = [[] for _ in range(chips)]
    for d in range(1, chips):
        for e in range(2):
            target = (chip + d) % chips * 2 + (core + e) % 2
            x = after(scaled(target * base, base), same_core[-1])
            remote[d].append(chip_move(x, pool_count, d, e))

    down = [x.reshape(adapters * rank, piece) for x in (query_down_maps, value_down_maps)]
    shrunk = pl.pallas_call(
        shrink_kernel,
        in_specs=[VMEM] * (len(adapter_rows) + 1) + [HBM] * 2,
        out_specs=VMEM,
        out_shape=jax.ShapeDtypeStruct((2 * rank, rows * pool_count), jnp.float32),
        scratch_shapes=[
            *[pltpu.VMEM(x.shape, x.dtype) for x in down],
            pltpu.SemaphoreType.DMA((2,)),
        ],
        compiler_params=params(),
        cost_estimate=small_cost(),
        name="shrink",
    )(local_ids, *adapter_rows, *down)
    lows = [shrunk] + [
        lax.ppermute(shrunk, "tp", [(i, (i + d) % tp_count) for i in range(tp_count)])
        for d in range(1, tp_count)
    ]

    values = tokens.astype(jnp.float32)
    scale = lax.rsqrt(jnp.mean(values * values, axis=-1, keepdims=True) + epsilon)
    half_dim = head // 2
    frequency = jnp.power(
        jnp.float32(rope_base), jnp.arange(half_dim, dtype=jnp.float32) * (-2.0 / head)
    )
    angles = cache_length_per_row.astype(jnp.float32)[:, None] * frequency[None, :]
    cosines = jnp.concatenate([jnp.cos(angles)] * 2, axis=1)
    sines = jnp.concatenate([-jnp.sin(angles), jnp.sin(angles)], axis=1)
    lengths = cache_length_per_row.reshape(rows, 1)

    up_q = query_up_maps.reshape(adapters * rank, query_up_maps.shape[2])
    up_v = value_up_maps.reshape(adapters * rank, value_up_maps.shape[2])
    adapter = (local_ids, lows, up_q, up_v)
    own_sums, own_send = add_adapters(own_base, own_sends, adapter)
    swapped = core_swap(own_send, pool_count)
    adapter = (after(local_ids, own_sums), lows, up_q, up_v)
    moved = [[] for _ in chunks]
    both = None
    for c, (at, part) in enumerate(chunks):
        for d in range(1, chips):
            spans = [(2 * d + e) * rows + at for e in range(2)]
            if both is not None:
                remote[d][0] = after(remote[d][0], both)
            keep, *sends = project(
                f"project_{c}_{d}",
                remote[d],
                *weights,
                adapter=adapter,
                spans=spans,
                window=(at, part),
            )
            swaps = [core_swap(x, pool_count) for x in sends]
            if c:
                keep = after(keep, moved[c - 1][-1])
            swaps = jnp.concatenate(swaps, axis=1)
            both = (keep + swaps.astype(jnp.float32)).astype(jnp.bfloat16)
            moved[c].append(chip_move(both, pool_count, -d))
    moved[0][0] = after(moved[0][0], both)

    share = pool_count // tp_count
    order = []
    for d in range(chips):
        for e in range(2):
            p = (chip - d) % chips * 2 + (core + e) % 2
            order.append(
                reversed_bits(jnp.bitwise_xor(p // share, tp_at), tp_count) * share + p % share
            )
    order = jnp.stack(order).astype(jnp.int32)
    gathered, new_keys, new_values = [], [], []
    for c, window in enumerate(chunks):
        attended, new_key, new_value = attend(
            c,
            window,
            own_sums,
            swapped,
            moved[c],
            scale,
            cosines,
            sines,
            lengths,
            rotated_key_cache,
            cached_value_rows,
        )
        if c + 1 < len(chunks):
            attended, *moved[c + 1] = lax.optimization_barrier((attended, *moved[c + 1]))
        if c:
            attended = after(attended, gathered[-1][-2])
        gathered.append(gather_pool(attended))
        new_keys.append(new_key)
        new_values.append(new_value)
    gathered[0][0] = after(gathered[0][0], *new_keys)
    outputs, totals = [], []
    for c, (_, part) in enumerate(chunks):
        if c:
            gathered[c][0] = after(gathered[c][0], keep)
        keep, send = output_part(c, order, gathered[c], output_matrix)
        summed, totals = halving_sum(keep, send, tp_count, totals)
        outputs.append(summed.reshape(-1, part, summed.shape[1]))
    attn_out = jnp.concatenate(outputs, axis=1)
    return (
        attn_out.reshape(-1, attn_out.shape[2]),
        jnp.concatenate(new_keys, axis=0),
        jnp.concatenate(new_values, axis=0),
    )


def solution(mesh):
    return jax.shard_map(
        shards,
        mesh=mesh,
        in_specs=(
            P(("groups", "pool"), None),
            P(),
            P("pool", "tp"),
            P("pool", "tp"),
            P("pool", "tp"),
            P("tp", "pool"),
            P(("groups", "pool"), "tp", None, None),
            P(("groups", "pool"), "tp", None, None),
            P(("groups", "pool")),
            P(("groups", "pool")),
            P("pool", None, "tp"),
            P("pool", None, "tp"),
            P("pool", None, "tp"),
            P("pool", None, "tp"),
        ),
        out_specs=(
            P(("groups", "tp"), "pool"),
            P(("groups", "pool"), "tp"),
            P(("groups", "pool"), "tp"),
        ),
        check_vma=False,
    )
```

```python
import functools
import math

import jax
import jax.numpy as jnp
from jax import lax
from jax.experimental import pallas as pl
from jax.experimental.pallas import tpu as pltpu
from jax.sharding import PartitionSpec as P

epsilon = 1e-05
adapter_scale = 0.5
rope_base = 500000.0
masked_score = -1e30


VMEM = pl.BlockSpec(memory_space=pltpu.VMEM)
HBM = pl.BlockSpec(memory_space=pltpu.HBM)
SMEM = pl.BlockSpec(memory_space=pltpu.SMEM)


def local_call(kernel, name, operands, outs, scratch, far=(), carried=()):
    near = [spec for _, spec in operands]
    counts = (len(operands), len(far), len(carried), len(outs), len(carried), len(scratch))

    def body(*refs):
        groups, at = [], 0
        for n in counts:
            groups.append(refs[at : at + n])
            at += n
        ins, far_refs, sources, out_refs, targets, scratch_refs = groups
        copies = [
            pltpu.make_async_copy(source, target, refs[-1].at[i])
            for i, (source, target) in enumerate(zip(sources, targets))
        ]
        kernel(ins, far_refs, out_refs, scratch_refs, [copy.start for copy in copies])
        for copy in copies:
            copy.wait()

    sems = [pltpu.SemaphoreType.DMA((len(carried),))] if carried else []
    return pl.pallas_call(
        body,
        in_specs=near + [HBM] * (len(far) + len(carried)),
        out_specs=[VMEM] * (len(outs) + len(carried)),
        out_shape=[*outs, *[pltpu.VMEM(x.shape, x.dtype) for x in carried]],
        scratch_shapes=[*scratch, *sems],
        compiler_params=pltpu.CompilerParams(vmem_limit_bytes=16 * 1024 * 1024),
        cost_estimate=pl.CostEstimate(flops=1000, bytes_accessed=1000, transcendentals=0),
        name=name,
    )(
        *[x for x, _ in operands],
        *[pltpu.with_memory_space_constraint(x, pltpu.HBM) for x in (*far, *carried)],
    )


def in_vmem(arrays):
    return [(x, VMEM) for x in arrays]


def shaped(shape, dtype=jnp.float32):
    return jax.ShapeDtypeStruct(shape, dtype)


def after(x, *earlier):
    return lax.optimization_barrier((x, *earlier))[0]


def core_swap(x, pool_count):
    return lax.ppermute(x, "pool", [(p, p ^ 1) for p in range(pool_count)])


def chip_move(x, pool_count, d, e=0):
    chips = pool_count // 2
    return lax.ppermute(
        x,
        "pool",
        [(p, (p // 2 + d) % chips * 2 + ((p % 2) ^ e)) for p in range(pool_count)],
    )


def shrink(ids, blocks, query_down, value_down, carried):
    slots, _ = query_down.shape
    rows = blocks[0].shape[0]
    adapters = slots // 16

    def kernel(ins, _, outs, scratch, starts):
        ids, *blocks, query_down, value_down = ins
        (out,) = outs
        for start in starts:
            start()
        for first in range(0, len(blocks), 2):
            x = jnp.concatenate([b[...] for b in blocks[first : first + 2]], axis=0)
            span = slice(first * rows, (first + 2) * rows)
            label = ids[:, span].reshape(1, 1, 2 * rows)
            chosen = lax.broadcasted_iota(jnp.int32, (adapters, 1, 2 * rows), 0) == label
            for at, table in enumerate((query_down, value_down)):
                terms = lax.dot_general(
                    table[...], x, (((1,), (1,)), ((), ())), preferred_element_type=jnp.float32
                ).reshape(adapters, 16, 2 * rows)
                out[at * 16 : (at + 1) * 16, span] = jnp.sum(
                    jnp.where(chosen, terms, 0.0), axis=0
                )

    return local_call(
        kernel,
        "shrink",
        in_vmem([ids, *blocks, query_down, value_down]),
        [shaped((32, rows * len(blocks)))],
        [],
        carried=carried,
    )


def spread_lows(low, ids, adapters):
    total = ids.shape[1]
    low = low.astype(jnp.bfloat16).astype(jnp.float32) * adapter_scale
    chosen = lax.broadcasted_iota(jnp.int32, (adapters, 1, total), 0) == ids.reshape(1, 1, total)
    return [
        jnp.where(chosen, low[at : at + 16][None], 0.0)
        .reshape(adapters * 16, total)
        .T.astype(jnp.bfloat16)
        for at in (0, 16)
    ]


def columns_at(start, width):
    return pl.ds(pl.multiple_of(start, width), width)


def project_own(blocks, wq, wk, wv, carried):
    rows, depth = blocks[0].shape
    wide, kv = wq.shape[1], wk.shape[1]
    tile = min(512, wide // 2)
    steps = wide // tile

    def kernel(ins, far, outs, scratch, starts):
        keep, send, *near = outs
        xs, sems = scratch

        def copies():
            for i in range(steps):
                yield far[0].at[:, columns_at(i * tile, tile)], near[0].at[
                    :, columns_at(i * tile, tile)
                ], sems.at[i]
            yield far[1], near[1], sems.at[steps]
            yield far[2], near[2], sems.at[steps + 1]

        for copy in copies():
            pltpu.make_async_copy(*copy).start()
        for start in starts:
            start()
        at = 0
        for block in ins:
            xs[at : at + block.shape[0], :] = block[...]
            at += block.shape[0]

        def write(w, columns):
            acc = jnp.dot(xs[...], w, preferred_element_type=jnp.float32)
            keep[:, columns] = acc[:rows]
            send[:, columns] = acc[rows:]

        @pl.loop(0, steps)
        def _(i):
            columns = columns_at(i * tile, tile)
            pltpu.make_async_copy(
                far[0].at[:, columns], near[0].at[:, columns], sems.at[i]
            ).wait()
            write(near[0][:, columns], columns)

        for j in range(2):
            pltpu.make_async_copy(far[1 + j], near[1 + j], sems.at[steps + j]).wait()
            write(near[1 + j][...], slice(wide + j * kv, wide + (j + 1) * kv))

    sums = shaped((rows, wide + 2 * kv))
    return local_call(
        kernel,
        "project_own",
        in_vmem(blocks),
        [sums, sums, *[pltpu.VMEM(w.shape, w.dtype) for w in (wq, wk, wv)]],
        [
            pltpu.VMEM((2 * rows, depth), jnp.bfloat16),
            pltpu.SemaphoreType.DMA((steps + 2,)),
        ],
        far=[wq, wk, wv],
        carried=carried,
    )


def project(name, window, spans, ids, lows, blocks, weights, carried):
    first, rows = window
    depth = blocks[0].shape[1]
    wide, kv, slots = weights[0].shape[1], weights[1].shape[1], weights[3].shape[0]
    tile = min(512, wide // 2)

    def kernel(ins, _, outs, scratch, starts):
        ids, *ins = ins
        low_refs, (b0, b1, wq, wk, wv, uq, uv) = ins[: len(lows)], ins[len(lows) :]
        keep, *sends = outs
        xs, spread_q, spread_v = scratch
        for start in starts:
            start()
        xs[:rows, :] = b0[first : first + rows, :]
        xs[rows:, :] = b1[first : first + rows, :]
        low = low_refs[0][...]
        for other in low_refs[1:]:
            low = low + other[...]
        low = jnp.concatenate([low[:, at : at + rows] for at in spans], axis=1)
        label = jnp.concatenate([ids[:, at : at + rows] for at in spans], axis=1)
        spread_q[...], spread_v[...] = spread_lows(low, label, slots // 16)

        def sums(w, spread=None, u=None):
            acc = jnp.dot(xs[...], w, preferred_element_type=jnp.float32)
            if u is not None:
                acc = acc + jnp.dot(spread[...], u, preferred_element_type=jnp.float32)
            return acc

        for half in range(2):

            @pl.loop(0, wide // 2 // tile)
            def _(j):
                columns = columns_at(half * (wide // 2) + j * tile, tile)
                acc = sums(wq[:, columns], spread_q, uq[:, columns])
                keep[:, columns] = acc[:rows]
                sends[half][:, columns_at(j * tile, tile)] = acc[rows:].astype(jnp.bfloat16)

        for j, acc in enumerate((sums(wk[...]), sums(wv[...], spread_v, uv[...]))):
            keep[:, wide + j * kv : wide + (j + 1) * kv] = acc[:rows]
            sends[2][:, j * kv : (j + 1) * kv] = acc[rows:].astype(jnp.bfloat16)

    spread = pltpu.VMEM((2 * rows, slots), jnp.bfloat16)
    results = local_call(
        kernel,
        name,
        in_vmem([ids, *lows, *blocks, *weights]),
        [
            shaped((rows, wide + 2 * kv)),
            *[shaped((rows, wide // 2), jnp.bfloat16)] * 2,
            shaped((rows, 2 * kv), jnp.bfloat16),
        ],
        [pltpu.VMEM((2 * rows, depth), jnp.bfloat16), spread, spread],
        carried=carried,
    )
    return results[0], results[1:4], results[4:]


def add_adapters(keep, send, ids, lows, uq, uv, carried):
    rows = keep.shape[0]
    wide, kv, slots = uq.shape[1], uv.shape[1], uq.shape[0]
    tile = min(512, wide)

    def kernel(ins, _, outs, scratch, starts):
        ids, *ins = ins
        low_refs, (keep0, send0, uq, uv) = ins[: len(lows)], ins[len(lows) :]
        keep, send = outs
        spread_q, spread_v = scratch
        for start in starts:
            start()
        low = low_refs[0][:, : 2 * rows]
        for other in low_refs[1:]:
            low = low + other[:, : 2 * rows]
        spread_q[...], spread_v[...] = spread_lows(low, ids[:, : 2 * rows], slots // 16)

        def write(extra, columns):
            keep[:, columns] = keep0[:, columns] + extra[:rows]
            send[:, columns] = (send0[:, columns] + extra[rows:]).astype(send.dtype)

        @pl.loop(0, wide // tile)
        def _(i):
            columns = columns_at(i * tile, tile)
            write(
                jnp.dot(spread_q[...], uq[:, columns], preferred_element_type=jnp.float32),
                columns,
            )

        keep[:, wide : wide + kv] = keep0[:, wide : wide + kv]
        send[:, wide : wide + kv] = send0[:, wide : wide + kv].astype(send.dtype)
        write(
            jnp.dot(spread_v[...], uv[...], preferred_element_type=jnp.float32),
            slice(wide + kv, wide + 2 * kv),
        )

    spread = pltpu.VMEM((2 * rows, slots), jnp.bfloat16)
    return local_call(
        kernel,
        "add_adapters",
        in_vmem([ids, *lows, keep, send, uq, uv]),
        [shaped(keep.shape), shaped(keep.shape, jnp.bfloat16)],
        [spread, spread],
        carried=carried,
    )


def attend_kernel(first_row, block, ins, outs):
    keep, swapped, *moved, scale, cosines, sines, lengths, keys, values = ins
    out, key_out, value_out = outs
    head = cosines.shape[1]
    rows = out.shape[0]
    _, kv_heads, cache, _ = keys.shape
    heads = out.shape[1] // head
    group = heads // kv_heads
    score_scale = 1.0 / math.sqrt(head)
    sub = 8
    column = lax.broadcasted_iota(jnp.int32, (sub, sub * cache), 1)
    start = lax.broadcasted_iota(jnp.int32, (sub, sub * cache), 0) * cache

    @pl.loop(0, rows // block)
    def _(i):
        attended, new_keys, new_values = [], [], []
        for half in range(block // sub):
            here = pl.ds(pl.multiple_of(i * block + half * sub, sub), sub)
            whole = pl.ds(pl.multiple_of(first_row + i * block + half * sub, sub), sub)
            x = keep[whole] + swapped[whole].astype(jnp.float32)
            for m in moved:
                x = x + m[here].astype(jnp.float32)
            x = x * scale[whole]
            cos, sin = cosines[whole], sines[whole]
            inside = (column >= start) & (column < start + lengths[whole])

            def piece(i):
                return x[:, i * head : (i + 1) * head]

            def turn(v):
                return v * cos + pltpu.roll(v, head // 2, 1) * sin

            for g in range(kv_heads):
                query = jnp.concatenate(
                    [turn(piece(g * group + h)) for h in range(group)], axis=0
                ).astype(jnp.bfloat16)
                new_key = turn(piece(heads + g)).astype(jnp.bfloat16).astype(jnp.float32)
                new_value = piece(heads + kv_heads + g).astype(jnp.bfloat16).astype(jnp.float32)
                k = keys[whole, g].reshape(sub * cache, head)
                v = values[whole, g].reshape(sub * cache, head)
                scores = (
                    lax.dot_general(
                        query, k, (((1,), (1,)), ((), ())), preferred_element_type=jnp.float32
                    )
                    * score_scale
                )
                own_key = jnp.concatenate([new_key] * group, axis=0)
                own = (
                    jnp.sum(query.astype(jnp.float32) * own_key, axis=1, keepdims=True)
                    * score_scale
                )
                scores = jnp.where(
                    inside[None], scores.reshape(group, sub, sub * cache), masked_score
                ).reshape(group * sub, sub * cache)
                peak = jnp.maximum(jnp.max(scores, axis=1, keepdims=True), own)
                weights = jnp.exp(scores - peak)
                own_weight = jnp.exp(own - peak)
                inverse = 1.0 / (jnp.sum(weights, axis=1, keepdims=True) + own_weight)
                mixed = jnp.dot(weights.astype(jnp.bfloat16), v, preferred_element_type=jnp.float32)
                own_value = jnp.concatenate([new_value] * group, axis=0)
                mixed = (mixed + own_weight * own_value) * inverse
                attended += [mixed[h * sub : (h + 1) * sub] for h in range(group)]
                new_keys.append(new_key)
                new_values.append(new_value)
        r = pl.ds(pl.multiple_of(i * block, block), block)

        def joined(pieces):
            n = len(pieces) * sub // block
            return jnp.concatenate(
                [jnp.concatenate(pieces[j::n], axis=0) for j in range(n)], axis=1
            ).astype(jnp.bfloat16)

        out[r] = joined(attended)
        key_out[r] = joined(new_keys)
        value_out[r] = joined(new_values)


def attend(name, window, keep, swapped, moved, rest, keys, values, carried):
    _, columns = keep.shape
    _, kv_heads, _, head = keys.shape
    kv_cols = kv_heads * head
    first, part = window

    def kernel(ins, _, outs, scratch, starts):
        for start in starts:
            start()
        attend_kernel(first, 16, ins, outs)

    widths = (columns - 2 * kv_cols, kv_cols, kv_cols)
    return local_call(
        kernel,
        name,
        in_vmem([keep, swapped, *moved, *rest, keys, values]),
        [shaped((part, w), jnp.bfloat16) for w in widths],
        [],
        carried=carried,
    )


def output_part(name, span, order, blocks, weights):
    rows = blocks[0].shape[0]
    first, columns = span
    depth = weights.shape[0]
    tile = math.gcd(512, columns)
    total = rows * len(blocks)

    def kernel(ins, _, outs, scratch, starts):
        order, *blocks, weights = ins
        keep, send = outs
        (xs,) = scratch
        for b, block in enumerate(blocks):
            xs[pl.ds(pl.multiple_of(order[b] * rows, rows), rows), :] = block[...]

        @pl.loop(0, columns // tile)
        def _(i):
            w = weights[:, columns_at(first + i * tile, tile)]
            acc = jnp.dot(xs[...], w, preferred_element_type=jnp.float32).astype(jnp.bfloat16)
            keep[:, columns_at(i * tile, tile)] = acc[: total // 2]
            send[:, columns_at(i * tile, tile)] = acc[total // 2 :]

    return local_call(
        kernel,
        name,
        [(order, SMEM), *in_vmem([*blocks, weights])],
        [shaped((total // 2, columns), jnp.bfloat16)] * 2,
        [pltpu.VMEM((total, depth), jnp.bfloat16)],
    )


def reversed_bits(x, count):
    out, bit = 0, 1
    while bit < count:
        out = out * 2 + (x // bit) % 2
        bit *= 2
    return out


def halving_steps(keep, send, count, earlier):
    step, totals = 1, []
    while True:
        got = lax.ppermute(send, "tp", [(z, z ^ step) for z in range(count)])
        step *= 2
        if step == count:
            return keep, got, totals
        if earlier:
            got = after(got, earlier[len(totals)])
        total = keep.astype(jnp.float32) + got.astype(jnp.float32)
        totals.append(total)
        half = total.shape[0] // 2
        keep, send = total[:half], total[half:].astype(jnp.bfloat16)


def shards(
    tokens,
    input_norm_gain,
    query_matrix,
    key_matrix,
    value_matrix,
    output_matrix,
    rotated_key_cache,
    cached_value_rows,
    cache_length_per_row,
    row_adapter_index,
    query_down_maps,
    query_up_maps,
    value_down_maps,
    value_up_maps,
):
    pool_count = lax.axis_size("pool")
    tp_count = lax.axis_size("tp")
    chips = pool_count // 2
    pool_at = lax.axis_index("pool")
    tp_at = lax.axis_index("tp")
    chip, core = pool_at // 2, pool_at % 2
    rows = tokens.shape[0]
    adapters, rank, piece = query_down_maps.shape
    base = query_matrix.shape[0]
    kv_heads = rotated_key_cache.shape[1]
    head = rotated_key_cache.shape[3]

    def scaled(start, width, tokens=tokens, gain=input_norm_gain, window=(0, rows)):
        x = lax.dynamic_slice(tokens, (window[0], start), (window[1], width)).astype(jnp.float32)
        factor = lax.dynamic_slice_in_dim(gain, start, width, 0).astype(jnp.float32)
        return (x * factor[None, :]).astype(jnp.bfloat16)

    ids = row_adapter_index.reshape(1, rows)
    ids = [ids] + [chip_move(ids, pool_count, d) for d in range(1, chips)]
    first = after(scaled(tp_at * piece, piece), *ids[1:])
    first, tokens_1, gain_1 = lax.optimization_barrier((first, tokens, input_norm_gain))
    same_core = [first] + [chip_move(first, pool_count, d) for d in range(1, chips)]
    ids = [b for x in ids for b in (x, core_swap(x, pool_count))]
    local_ids = jnp.concatenate(ids, axis=1) - pool_at * adapters

    cut = rows * 3 // 8
    chunks = [(0, cut), (cut, rows - cut)]
    own = scaled(pool_at * base, base, tokens_1, gain_1)
    partner_at = (pool_at // 2 * 2 + 1 - core) * base
    partner = [
        scaled(partner_at, base, tokens_1, gain_1, (at, rows // 2)) for at in (0, rows // 2)
    ]
    *partner, tokens_2, gain_2 = lax.optimization_barrier((*partner, tokens, input_norm_gain))
    partner = [core_swap(x, pool_count) for x in partner]
    away = {}
    for d in range(1, chips):
        for e in range(2):
            target = (chip + d) % chips * 2 + (core + e) % 2
            away[d, e] = scaled(target * base, base, tokens_2, gain_2)
    own = after(own, *away.values())
    flat_down = [x.reshape(adapters * rank, piece) for x in (query_down_maps, value_down_maps)]
    own_keep, own_send, *weights, down_q, down_v = project_own(
        [own, *partner], query_matrix, key_matrix, value_matrix, flat_down
    )
    remote = [[] for _ in range(chips)]
    for (d, e), x in away.items():
        remote[d].append(chip_move(after(x, *same_core[1:]), pool_count, d, e))

    same_core[1:] = [after(x, own_keep) for x in same_core[1:]]
    adapter_rows = [b for x in same_core for b in (x, core_swap(x, pool_count))]
    flat_up = [x.reshape(adapters * rank, x.shape[2]) for x in (query_up_maps, value_up_maps)]
    shrunk, up_q, up_v = shrink(local_ids, adapter_rows, down_q, down_v, flat_up)
    lows = [shrunk] + [
        lax.ppermute(shrunk, "tp", [(i, (i + d) % tp_count) for i in range(tp_count)])
        for d in range(1, tp_count)
    ]
    weights += [up_q, up_v]

    values = tokens.astype(jnp.float32)
    scale = lax.rsqrt(jnp.mean(values * values, axis=-1, keepdims=True) + epsilon)
    half_dim = head // 2
    frequency = jnp.power(
        jnp.float32(rope_base), jnp.arange(half_dim, dtype=jnp.float32) * (-2.0 / head)
    )
    angles = cache_length_per_row.astype(jnp.float32)[:, None] * frequency[None, :]
    cosines = jnp.concatenate([jnp.cos(angles)] * 2, axis=1)
    sines = jnp.concatenate([-jnp.sin(angles), jnp.sin(angles)], axis=1)
    lengths = cache_length_per_row.reshape(rows, 1)

    own_sums, own_send, keys = add_adapters(
        own_keep, own_send, local_ids, lows, up_q, up_v, [rotated_key_cache]
    )
    swapped = core_swap(own_send, pool_count)
    local_ids = after(local_ids, own_sums)
    moved = [[] for _ in chunks]
    both, to_carry, cached = None, [cached_value_rows], None
    for c, (at, part) in enumerate(chunks):
        for d in range(1, chips):
            spans = [(2 * d + e) * rows + at for e in range(2)]
            if both is not None:
                remote[d][0] = after(remote[d][0], both)
            keep, sends, carried = project(
                f"project_{c}_{d}",
                (at, part),
                spans,
                local_ids,
                lows,
                remote[d],
                weights,
                to_carry,
            )
            cached, to_carry = cached or carried, []
            swaps = [core_swap(x, pool_count) for x in sends]
            if c:
                keep = after(keep, moved[c - 1][-1])
            swaps = jnp.concatenate(swaps, axis=1)
            both = (keep + swaps.astype(jnp.float32)).astype(jnp.bfloat16)
            moved[c].append(chip_move(both, pool_count, -d))
    moved[0][0] = after(moved[0][0], both)

    share = pool_count // tp_count
    order = []
    for d in range(chips):
        for e in range(2):
            p = (chip - d) % chips * 2 + (core + e) % 2
            order.append(
                reversed_bits(jnp.bitwise_xor(p // share, tp_at), tp_count) * share + p % share
            )
    order = jnp.stack(order).astype(jnp.int32)

    attended, new_keys, new_values, out_weights = [], [], [], None
    for c, window in enumerate(chunks):
        out, new_key, new_value, *carried = attend(
            f"attend_{c}",
            window,
            own_sums,
            swapped,
            moved[c],
            (scale, cosines, sines, lengths),
            keys,
            cached[0],
            [] if c else [output_matrix],
        )
        out_weights = out_weights or carried
        if c + 1 < len(chunks):
            out, *moved[c + 1] = lax.optimization_barrier((out, *moved[c + 1]))
        if c:
            out = after(out, attended[-1][-1])
        attended.append([out] + [chip_move(out, pool_count, d) for d in range(1, chips)])
        new_keys.append(new_key)
        new_values.append(new_value)
    attended[0][0] = after(attended[0][0], *new_keys)

    pieces, totals, keep = [], [], None
    columns = output_matrix.shape[1]
    spans = [(0, columns * 3 // 4), (columns * 3 // 4, columns // 4)]
    for c in range(len(chunks)):
        if c:
            attended[c] = [after(x, keep) for x in attended[c]]
        gathered = [b for x in attended[c] for b in (x, core_swap(x, pool_count))]
        for j, span in enumerate(spans):
            if j:
                gathered[0] = after(gathered[0], keep)
            keep, send = output_part(f"output_{c}_{j}", span, order, gathered, out_weights[0])
            *halves, totals = halving_steps(keep, send, tp_count, totals)
            pieces.append(halves)
    outputs, row_count = [], len(spans)
    for c, (_, part) in enumerate(chunks):
        sums = []
        for mine, got in pieces[c * row_count : (c + 1) * row_count]:
            total = mine.astype(jnp.float32) + after(got, keep).astype(jnp.float32)
            keep = total.astype(jnp.bfloat16)
            sums.append(keep.reshape(-1, part, total.shape[1]))
        outputs.append(jnp.concatenate(sums, axis=2))
    attn_out = jnp.concatenate(outputs, axis=1)
    return (
        attn_out.reshape(-1, attn_out.shape[2]),
        jnp.concatenate(new_keys, axis=0),
        jnp.concatenate(new_values, axis=0),
    )


def solution(mesh):
    return jax.shard_map(
        shards,
        mesh=mesh,
        in_specs=(
            P(("groups", "pool"), None),
            P(),
            P("pool", "tp"),
            P("pool", "tp"),
            P("pool", "tp"),
            P("tp", "pool"),
            P(("groups", "pool"), "tp", None, None),
            P(("groups", "pool"), "tp", None, None),
            P(("groups", "pool")),
            P(("groups", "pool")),
            P("pool", None, "tp"),
            P("pool", None, "tp"),
            P("pool", None, "tp"),
            P("pool", None, "tp"),
        ),
        out_specs=(
            P(("groups", "tp"), "pool"),
            P(("groups", "pool"), "tp"),
            P(("groups", "pool"), "tp"),
        ),
        check_vma=False,
    )
```

```python
import functools
import math

import jax
import jax.numpy as jnp
from jax import lax
from jax.experimental import pallas as pl
from jax.experimental.pallas import tpu as pltpu
from jax.sharding import PartitionSpec as P

epsilon = 1e-05
adapter_scale = 0.5
rope_base = 500000.0
masked_score = -1e30


VMEM = pl.BlockSpec(memory_space=pltpu.VMEM)
HBM = pl.BlockSpec(memory_space=pltpu.HBM)
SMEM = pl.BlockSpec(memory_space=pltpu.SMEM)


def local_call(kernel, name, operands, outs, scratch, far=(), mib=16):
    counts = (len(operands), len(far), len(outs), len(scratch))

    def body(*refs):
        groups, at = [], 0
        for n in counts:
            groups.append(refs[at : at + n])
            at += n
        kernel(*groups)

    return pl.pallas_call(
        body,
        in_specs=[spec for _, spec in operands] + [HBM] * len(far),
        out_specs=[VMEM] * len(outs),
        out_shape=outs,
        scratch_shapes=scratch,
        compiler_params=pltpu.CompilerParams(vmem_limit_bytes=mib * 1024 * 1024),
        cost_estimate=pl.CostEstimate(flops=1000, bytes_accessed=1000, transcendentals=0),
        name=name,
    )(
        *[x for x, _ in operands],
        *[pltpu.with_memory_space_constraint(x, pltpu.HBM) for x in far],
    )


def held(x):
    return pltpu.VMEM(x.shape, x.dtype)


def in_vmem(arrays):
    return [(x, VMEM) for x in arrays]


def shaped(shape, dtype=jnp.float32):
    return jax.ShapeDtypeStruct(shape, dtype)


def after(x, *earlier):
    return lax.optimization_barrier((x, *earlier))[0]


def core_swap(x, pool_count):
    return lax.ppermute(x, "pool", [(p, p ^ 1) for p in range(pool_count)])


def chip_move(x, pool_count, d, e=0):
    chips = pool_count // 2
    return lax.ppermute(
        x,
        "pool",
        [(p, (p // 2 + d) % chips * 2 + ((p % 2) ^ e)) for p in range(pool_count)],
    )


def tp_swap(x, tp_count, step):
    return lax.ppermute(x, "tp", [(z, z ^ step) for z in range(tp_count)])


def shrink(ids, blocks, query_down, value_down):
    slots, _ = query_down.shape
    rows = blocks[0].shape[0]
    adapters = slots // 16

    def kernel(ins, far, outs, scratch):
        ids, *blocks = ins
        (out,) = outs
        *tables, sems = scratch
        copies = [
            pltpu.make_async_copy(source, table, sems.at[i])
            for i, (source, table) in enumerate(zip(far, tables))
        ]
        for copy in copies:
            copy.start()
        for at, table in enumerate(tables):
            copies[at].wait()
            for first in range(0, len(blocks), 2):
                x = jnp.concatenate([b[...] for b in blocks[first : first + 2]], axis=0)
                span = slice(first * rows, (first + 2) * rows)
                label = ids[:, span].reshape(1, 1, 2 * rows)
                chosen = lax.broadcasted_iota(jnp.int32, (adapters, 1, 2 * rows), 0) == label
                terms = lax.dot_general(
                    table[...], x, (((1,), (1,)), ((), ())), preferred_element_type=jnp.float32
                ).reshape(adapters, 16, 2 * rows)
                out[at * 16 : (at + 1) * 16, span] = jnp.sum(
                    jnp.where(chosen, terms, 0.0), axis=0
                )

    return local_call(
        kernel,
        "shrink",
        in_vmem([ids, *blocks]),
        [shaped((32, rows * len(blocks)))],
        [held(query_down), held(value_down), pltpu.SemaphoreType.DMA((2,))],
        far=[query_down, value_down],
    )[0]


def spread_lows(low, ids, adapters):
    total = ids.shape[1]
    low = low.astype(jnp.bfloat16).astype(jnp.float32) * adapter_scale
    chosen = lax.broadcasted_iota(jnp.int32, (adapters, 1, total), 0) == ids.reshape(1, 1, total)
    return [
        jnp.where(chosen, low[at : at + 16][None], 0.0)
        .reshape(adapters * 16, total)
        .T.astype(jnp.bfloat16)
        for at in (0, 16)
    ]


def columns_at(start, width):
    return pl.ds(pl.multiple_of(start, width), width)


def project(name, kinds, span, ids, lows, blocks, far):
    wq, wk, wv, uq, uv = far
    rows, depth = blocks[0].shape
    wide, kv, slots = wq.shape[1], wk.shape[1], uq.shape[0]
    tile = 2 * kv
    steps = wide // tile
    total = span[1]
    outs = []
    for _, count, dtype, split in kinds:
        outs += [shaped((count, tile), dtype)] * (steps + 1) if split else [
            shaped((count, wide + tile), dtype)
        ]

    def kernel(ins, far, outs, scratch):
        ids, *ins = ins
        low_refs, blocks = ins[: len(lows)], ins[len(lows) :]
        wq, wk, wv, uq, uv, xs, spread_q, spread_v, wide_sems, sems = scratch
        narrow = [
            pltpu.make_async_copy(far[i], near, sems.at[at])
            for at, (i, near) in enumerate(((1, wk), (2, wv), (4, uv)))
        ]

        def wide_copies(i):
            columns = columns_at(i * tile, tile)
            return [
                pltpu.make_async_copy(
                    far[which].at[:, columns], near.at[:, columns], wide_sems.at[at, i]
                )
                for at, (which, near) in enumerate(((0, wq), (3, uq)))
            ]

        for copy in narrow:
            copy.start()
        for i in range(steps):
            for copy in wide_copies(i):
                copy.start()

        at = 0
        for block in blocks:
            xs[at : at + block.shape[0], :] = block[...]
            at += block.shape[0]
        low = low_refs[0][:, span[0] : span[0] + total]
        for other in low_refs[1:]:
            low = low + other[:, span[0] : span[0] + total]
        spread_q[...], spread_v[...] = spread_lows(
            low, ids[:, span[0] : span[0] + total], slots // 16
        )

        def write(acc, i, start, width):
            at = 0
            for first, count, dtype, split in kinds:
                to = start if split else i * tile + start
                outs[at + i if split else at][:, to : to + width] = acc[
                    first : first + count
                ].astype(dtype)
                at += steps + 1 if split else 1

        def sums(w, spread=None, u=None):
            acc = jnp.dot(xs[...], w, preferred_element_type=jnp.float32)
            if u is not None:
                acc = acc + jnp.dot(spread[...], u, preferred_element_type=jnp.float32)
            return acc

        narrow[0].wait()
        write(sums(wk[...]), steps, 0, kv)
        narrow[1].wait()
        narrow[2].wait()
        write(sums(wv[...], spread_v, uv[...]), steps, kv, kv)
        for i in range(steps):
            for copy in wide_copies(i):
                copy.wait()
            columns = slice(i * tile, (i + 1) * tile)
            write(sums(wq[:, columns], spread_q, uq[:, columns]), i, 0, tile)

    spread = pltpu.VMEM((total, slots), jnp.bfloat16)
    return local_call(
        kernel,
        name,
        in_vmem([ids, *lows, *blocks]),
        outs,
        [
            *[held(x) for x in far],
            pltpu.VMEM((total, depth), jnp.bfloat16),
            spread,
            spread,
            pltpu.SemaphoreType.DMA((2, steps)),
            pltpu.SemaphoreType.DMA((3,)),
        ],
        far=far,
        mib=28,
    )


def attend_kernel(first_row, block, count, ins, far, outs, scratch):
    keep, *ins = ins
    swapped, (*moved, scale, cosines, sines, lengths) = ins[:count], ins[count:]
    keys, values, sems = scratch
    out, key_out, value_out = outs
    head = cosines.shape[1]
    rows = out.shape[0]
    _, kv_heads, cache, _ = keys.shape
    heads = out.shape[1] // head
    group = heads // kv_heads
    score_scale = 1.0 / math.sqrt(head)
    sub = 8

    def copies(i):
        to = pl.ds(pl.multiple_of(i * block, block), block)
        at = pl.ds(pl.multiple_of(first_row + i * block, block), block)
        return [
            pltpu.make_async_copy(source.at[at], near.at[to], sems.at[which, i])
            for which, (source, near) in enumerate(zip(far, (keys, values)))
        ]

    for i in range(rows // block):
        for copy in copies(i):
            copy.start()

    column = lax.broadcasted_iota(jnp.int32, (sub, sub * cache), 1)
    start = lax.broadcasted_iota(jnp.int32, (sub, sub * cache), 0) * cache

    @pl.loop(0, rows // block)
    def _(i):
        for copy in copies(i):
            copy.wait()
        attended, new_keys, new_values = [], [], []
        for half in range(block // sub):
            here = pl.ds(pl.multiple_of(i * block + half * sub, sub), sub)
            whole = pl.ds(pl.multiple_of(first_row + i * block + half * sub, sub), sub)
            x = jnp.concatenate([part[whole] for part in swapped], axis=1).astype(jnp.float32)
            x = x + keep[whole]
            for m in moved:
                x = x + m[here].astype(jnp.float32)
            x = x * scale[whole]
            cos, sin = cosines[whole], sines[whole]
            inside = (column >= start) & (column < start + lengths[whole])

            def piece(i):
                return x[:, i * head : (i + 1) * head]

            def turn(v):
                return v * cos + pltpu.roll(v, head // 2, 1) * sin

            for g in range(kv_heads):
                query = jnp.concatenate(
                    [turn(piece(g * group + h)) for h in range(group)], axis=0
                ).astype(jnp.bfloat16)
                new_key = turn(piece(heads + g)).astype(jnp.bfloat16).astype(jnp.float32)
                new_value = piece(heads + kv_heads + g).astype(jnp.bfloat16).astype(jnp.float32)
                k = keys[here, g].reshape(sub * cache, head)
                v = values[here, g].reshape(sub * cache, head)
                scores = (
                    lax.dot_general(
                        query, k, (((1,), (1,)), ((), ())), preferred_element_type=jnp.float32
                    )
                    * score_scale
                )
                own_key = jnp.concatenate([new_key] * group, axis=0)
                own = (
                    jnp.sum(query.astype(jnp.float32) * own_key, axis=1, keepdims=True)
                    * score_scale
                )
                scores = jnp.where(
                    inside[None], scores.reshape(group, sub, sub * cache), masked_score
                ).reshape(group * sub, sub * cache)
                peak = jnp.maximum(jnp.max(scores, axis=1, keepdims=True), own)
                weights = jnp.exp(scores - peak)
                own_weight = jnp.exp(own - peak)
                inverse = 1.0 / (jnp.sum(weights, axis=1, keepdims=True) + own_weight)
                mixed = jnp.dot(weights.astype(jnp.bfloat16), v, preferred_element_type=jnp.float32)
                own_value = jnp.concatenate([new_value] * group, axis=0)
                mixed = (mixed + own_weight * own_value) * inverse
                attended += [mixed[h * sub : (h + 1) * sub] for h in range(group)]
                new_keys.append(new_key)
                new_values.append(new_value)
        r = pl.ds(pl.multiple_of(i * block, block), block)

        def joined(pieces):
            n = len(pieces) * sub // block
            return jnp.concatenate(
                [jnp.concatenate(pieces[j::n], axis=0) for j in range(n)], axis=1
            ).astype(jnp.bfloat16)

        out[r] = joined(attended)
        key_out[r] = joined(new_keys)
        value_out[r] = joined(new_values)


def attend(name, window, keep, swapped, moved, rest, keys, values):
    _, columns = keep.shape
    _, kv_heads, cache, head = keys.shape
    kv_cols = kv_heads * head
    first, part = window
    block = 16
    widths = (columns - 2 * kv_cols, kv_cols, kv_cols)
    near = pltpu.VMEM((part, kv_heads, cache, head), keys.dtype)
    return local_call(
        functools.partial(attend_kernel, first, block, len(swapped)),
        name,
        in_vmem([keep, *swapped, *moved, *rest]),
        [shaped((part, w), jnp.bfloat16) for w in widths],
        [near, near, pltpu.SemaphoreType.DMA((2, part // block))],
        far=[keys, values],
    )


def output_part(name, span, order, blocks, weights):
    rows = blocks[0].shape[0]
    first, columns = span
    depth = weights.shape[0]
    tile = math.gcd(512, columns)
    total = rows * len(blocks)

    def kernel(ins, far, outs, scratch):
        order, *blocks = ins
        keep, send = outs
        held, xs, sems = scratch

        def copy(i):
            return pltpu.make_async_copy(
                far[0].at[:, columns_at(first + i * tile, tile)],
                held.at[:, columns_at(i * tile, tile)],
                sems.at[i],
            )

        for i in range(columns // tile):
            copy(i).start()
        for b, block in enumerate(blocks):
            xs[pl.ds(pl.multiple_of(order[b] * rows, rows), rows), :] = block[...]

        @pl.loop(0, columns // tile)
        def _(i):
            copy(i).wait()
            w = held[:, columns_at(i * tile, tile)]
            acc = jnp.dot(xs[...], w, preferred_element_type=jnp.float32).astype(jnp.bfloat16)
            keep[:, columns_at(i * tile, tile)] = acc[: total // 2]
            send[:, columns_at(i * tile, tile)] = acc[total // 2 :]

    return local_call(
        kernel,
        name,
        [(order, SMEM), *in_vmem(blocks)],
        [shaped((total // 2, columns), jnp.bfloat16)] * 2,
        [
            pltpu.VMEM((depth, columns), weights.dtype),
            pltpu.VMEM((total, depth), jnp.bfloat16),
            pltpu.SemaphoreType.DMA((columns // tile,)),
        ],
        far=[weights],
    )


def reversed_bits(x, count):
    out, bit = 0, 1
    while bit < count:
        out = out * 2 + (x // bit) % 2
        bit *= 2
    return out


def shards(
    tokens,
    input_norm_gain,
    query_matrix,
    key_matrix,
    value_matrix,
    output_matrix,
    rotated_key_cache,
    cached_value_rows,
    cache_length_per_row,
    row_adapter_index,
    query_down_maps,
    query_up_maps,
    value_down_maps,
    value_up_maps,
):
    pool_count = lax.axis_size("pool")
    tp_count = lax.axis_size("tp")
    chips = pool_count // 2
    pool_at = lax.axis_index("pool")
    tp_at = lax.axis_index("tp")
    chip, core = pool_at // 2, pool_at % 2
    rows = tokens.shape[0]
    adapters, rank, piece = query_down_maps.shape
    base = query_matrix.shape[0]
    kv_heads = rotated_key_cache.shape[1]
    head = rotated_key_cache.shape[3]

    def scaled(start, width, tokens=tokens, gain=input_norm_gain, window=(0, rows)):
        x = lax.dynamic_slice(tokens, (window[0], start), (window[1], width)).astype(jnp.float32)
        factor = lax.dynamic_slice_in_dim(gain, start, width, 0).astype(jnp.float32)
        return (x * factor[None, :]).astype(jnp.bfloat16)

    ids = row_adapter_index.reshape(1, rows)
    ids = [ids] + [chip_move(ids, pool_count, d) for d in range(1, chips)]
    first = after(scaled(tp_at * piece, piece), *ids[1:])
    first, tokens_1, gain_1 = lax.optimization_barrier((first, tokens, input_norm_gain))
    same_core = [first] + [chip_move(first, pool_count, d) for d in range(1, chips)]
    ids = [b for x in ids for b in (x, core_swap(x, pool_count))]
    local_ids = jnp.concatenate(ids, axis=1) - pool_at * adapters

    cut = rows // 2
    chunks = [(0, cut), (cut, rows - cut)]
    own = scaled(pool_at * base, base, tokens_1, gain_1)
    partner_at = (pool_at // 2 * 2 + 1 - core) * base
    partner = [
        scaled(partner_at, base, tokens_1, gain_1, (at, rows // 2)) for at in (0, rows // 2)
    ]
    *partner, tokens_2, gain_2 = lax.optimization_barrier((*partner, tokens, input_norm_gain))
    partner = [core_swap(x, pool_count) for x in partner]
    away = {}
    for d in range(1, chips):
        for e in range(2):
            target = (chip + d) % chips * 2 + (core + e) % 2
            away[d, e] = scaled(target * base, base, tokens_2, gain_2)
    remote = [[] for _ in range(chips)]
    for (d, e), x in away.items():
        remote[d].append(chip_move(after(x, *same_core[1:]), pool_count, d, e))
    same_core[1:] = [after(x, *away.values()) for x in same_core[1:]]

    adapter_rows = [b for x in same_core for b in (x, core_swap(x, pool_count))]
    flat_down = [x.reshape(adapters * rank, piece) for x in (query_down_maps, value_down_maps)]
    flat_up = [x.reshape(adapters * rank, x.shape[2]) for x in (query_up_maps, value_up_maps)]
    shrunk = shrink(local_ids, adapter_rows, *flat_down)
    lows = [shrunk] + [
        lax.ppermute(shrunk, "tp", [(i, (i + d) % tp_count) for i in range(tp_count)])
        for d in range(1, tp_count)
    ]
    weights = [query_matrix, key_matrix, value_matrix, *flat_up]

    values = tokens.astype(jnp.float32)
    scale = lax.rsqrt(jnp.mean(values * values, axis=-1, keepdims=True) + epsilon)
    half_dim = head // 2
    frequency = jnp.power(
        jnp.float32(rope_base), jnp.arange(half_dim, dtype=jnp.float32) * (-2.0 / head)
    )
    angles = cache_length_per_row.astype(jnp.float32)[:, None] * frequency[None, :]
    cosines = jnp.concatenate([jnp.cos(angles)] * 2, axis=1)
    sines = jnp.concatenate([-jnp.sin(angles), jnp.sin(angles)], axis=1)
    lengths = cache_length_per_row.reshape(rows, 1)

    own_sums, *own_sends = project(
        "project_own",
        [(0, rows, jnp.float32, False), (rows, rows, jnp.bfloat16, True)],
        (0, 2 * rows),
        local_ids,
        lows,
        [own, *partner],
        weights,
    )
    swapped = [core_swap(x, pool_count) for x in own_sends]
    local_ids = after(local_ids, own_sums)
    moved = [[] for _ in chunks]
    both = None
    for d in range(1, chips):
        if both is not None:
            remote[d][0] = after(remote[d][0], both)
        at = 2 * d * rows
        (keep,) = project(
            f"project_{d}_0",
            [(0, rows, jnp.float32, False)],
            (at, rows),
            local_ids,
            lows,
            remote[d][:1],
            weights,
        )
        sends = project(
            f"project_{d}_1",
            [(first, part, jnp.bfloat16, False) for first, part in chunks],
            (at + rows, rows),
            local_ids,
            lows,
            [after(remote[d][1], keep)],
            weights,
        )
        for c, (first, part) in enumerate(chunks):
            swap = core_swap(sends[c], pool_count)
            if c:
                swap = after(swap, both)
            both = keep[first : first + part] + swap.astype(jnp.float32)
            both = both.astype(jnp.bfloat16)
            moved[c].append(chip_move(both, pool_count, -d))
    share = pool_count // tp_count
    order = []
    for d in range(chips):
        for e in range(2):
            p = (chip - d) % chips * 2 + (core + e) % 2
            order.append(
                reversed_bits(jnp.bitwise_xor(p // share, tp_at), tp_count) * share + p % share
            )
    order = jnp.stack(order).astype(jnp.int32)

    attended, new_keys, new_values = [], [], []
    for c, window in enumerate(chunks):
        out, new_key, new_value = attend(
            f"attend_{c}",
            window,
            own_sums,
            swapped,
            moved[c],
            (scale, cosines, sines, lengths),
            rotated_key_cache,
            cached_value_rows,
        )
        if c + 1 < len(chunks):
            out, *moved[c + 1] = lax.optimization_barrier((out, *moved[c + 1]))
        if c:
            out = after(out, attended[-1][-1])
        attended.append([out] + [chip_move(out, pool_count, d) for d in range(1, chips)])
        new_keys.append(new_key)
        new_values.append(new_value)
    attended[0][0] = after(attended[0][0], *new_keys)

    columns = output_matrix.shape[1]
    layout = [(0, 0, 2), (0, 1, 2), (1, 0, 2), (1, 2, 4), (1, 3, 4)]
    gathered, keeps, sends, products = {}, [], [], []

    def multiply(total):
        c, at, count = layout[len(keeps)]
        if c not in gathered:
            parts = [after(x, total) for x in attended[c]] if c else attended[c]
            gathered[c] = [b for x in parts for b in (x, core_swap(x, pool_count))]
        else:
            gathered[c][0] = after(gathered[c][0], products[-1])
        width = columns // count
        keep, send = output_part(
            f"output_{c}_{at}_{count}", (at * width, width), order, gathered[c], output_matrix
        )
        keeps.append(keep)
        sends.append(send)
        products.append(keep)

    stages = reversed_bits(1, tp_count).bit_length()
    total, got = None, {}
    for slot in range(len(layout) + stages - 1):
        while len(keeps) < min(slot + 2, len(layout)):
            multiply(total)
        for stage in range(stages):
            i = slot - stage
            if not 0 <= i < len(layout):
                continue
            if stage == 0:
                got[i] = tp_swap(sends[i], tp_count, 1)
            earlier = [products[-1]] + ([] if total is None else [total])
            total = keeps[i].astype(jnp.float32) + after(got[i], *earlier).astype(jnp.float32)
            if stage + 1 < stages:
                half = total.shape[0] // 2
                keeps[i] = total[:half]
                got[i] = tp_swap(total[half:].astype(jnp.bfloat16), tp_count, 2 << stage)
            else:
                total = total.astype(jnp.bfloat16)
                keeps[i] = total
    outputs = []
    for c, (_, part) in enumerate(chunks):
        sums = [keeps[i] for i, piece in enumerate(layout) if piece[0] == c]
        outputs.append(
            jnp.concatenate([x.reshape(-1, part, x.shape[1]) for x in sums], axis=2)
        )
    attn_out = jnp.concatenate(outputs, axis=1)
    return (
        attn_out.reshape(-1, attn_out.shape[2]),
        jnp.concatenate(new_keys, axis=0),
        jnp.concatenate(new_values, axis=0),
    )


def solution(mesh):
    return jax.shard_map(
        shards,
        mesh=mesh,
        in_specs=(
            P(("groups", "pool"), None),
            P(),
            P("pool", "tp"),
            P("pool", "tp"),
            P("pool", "tp"),
            P("tp", "pool"),
            P(("groups", "pool"), "tp", None, None),
            P(("groups", "pool"), "tp", None, None),
            P(("groups", "pool")),
            P(("groups", "pool")),
            P("pool", None, "tp"),
            P("pool", None, "tp"),
            P("pool", None, "tp"),
            P("pool", None, "tp"),
        ),
        out_specs=(
            P(("groups", "tp"), "pool"),
            P(("groups", "pool"), "tp"),
            P(("groups", "pool"), "tp"),
        ),
        check_vma=False,
    )
```

```python
import functools
import math

import jax
import jax.numpy as jnp
from jax import lax
from jax.experimental import pallas as pl
from jax.experimental.pallas import tpu as pltpu
from jax.sharding import PartitionSpec as P

epsilon = 1e-05
adapter_scale = 0.5
rope_base = 500000.0
masked_score = -1e30


VMEM = pl.BlockSpec(memory_space=pltpu.VMEM)
HBM = pl.BlockSpec(memory_space=pltpu.HBM)
SMEM = pl.BlockSpec(memory_space=pltpu.SMEM)


def local_call(kernel, name, operands, outs, scratch=(), carried=(), mib=16):
    counts = (len(operands), len(carried), len(outs), len(carried), len(scratch))

    def body(*refs):
        groups, at = [], 0
        for n in counts:
            groups.append(refs[at : at + n])
            at += n
        ins, sources, out_refs, targets, scratch_refs = groups
        copies = [
            pltpu.make_async_copy(source, target, refs[-1].at[i])
            for i, (source, target) in enumerate(zip(sources, targets))
        ]
        for copy in copies:
            copy.start()
        kernel(ins, out_refs, scratch_refs)
        for copy in copies:
            copy.wait()

    sems = [pltpu.SemaphoreType.DMA((len(carried),))] if carried else []
    return pl.pallas_call(
        body,
        in_specs=[spec for _, spec in operands] + [HBM] * len(carried),
        out_specs=[VMEM] * (len(outs) + len(carried)),
        out_shape=[*outs, *[pltpu.VMEM(x.shape, x.dtype) for x in carried]],
        scratch_shapes=[*scratch, *sems],
        compiler_params=pltpu.CompilerParams(vmem_limit_bytes=mib * 1024 * 1024),
        cost_estimate=pl.CostEstimate(flops=1000, bytes_accessed=1000, transcendentals=0),
        name=name,
    )(
        *[x for x, _ in operands],
        *[pltpu.with_memory_space_constraint(x, pltpu.HBM) for x in carried],
    )


def in_vmem(arrays):
    return [(x, VMEM) for x in arrays]


def shaped(shape, dtype=jnp.float32):
    return jax.ShapeDtypeStruct(shape, dtype)


def after(x, *earlier):
    return lax.optimization_barrier((x, *earlier))[0]


def core_swap(x, pool_count):
    return lax.ppermute(x, "pool", [(p, p ^ 1) for p in range(pool_count)])


def chip_move(x, pool_count, d, e=0):
    chips = pool_count // 2
    return lax.ppermute(
        x,
        "pool",
        [(p, (p // 2 + d) % chips * 2 + ((p % 2) ^ e)) for p in range(pool_count)],
    )


def tp_swap(x, tp_count, step):
    return lax.ppermute(x, "tp", [(z, z ^ step) for z in range(tp_count)])


def shrink(first_id, ids, blocks, query_down, value_down):
    slots, _ = query_down.shape
    rows = blocks[0].shape[0]
    adapters = slots // 16
    count = len(blocks)

    def kernel(ins, outs, _):
        first_id, *ins = ins
        ids, blocks, tables = ins[:count], ins[count : 2 * count], ins[2 * count :]
        local_ids, out = outs
        for b in range(count):
            local_ids[:, b * rows : (b + 1) * rows] = ids[b][...] - first_id[0]
        for first in range(0, count, 2):
            x = jnp.concatenate([b[...] for b in blocks[first : first + 2]], axis=0)
            span = slice(first * rows, (first + 2) * rows)
            label = local_ids[:, span].reshape(1, 1, 2 * rows)
            chosen = lax.broadcasted_iota(jnp.int32, (adapters, 1, 2 * rows), 0) == label
            for at, table in enumerate(tables):
                terms = lax.dot_general(
                    table[...], x, (((1,), (1,)), ((), ())), preferred_element_type=jnp.float32
                ).reshape(adapters, 16, 2 * rows)
                out[at * 16 : (at + 1) * 16, span] = jnp.sum(
                    jnp.where(chosen, terms, 0.0), axis=0
                )

    return local_call(
        kernel,
        "shrink",
        [(first_id, SMEM), *in_vmem([*ids, *blocks, query_down, value_down])],
        [shaped((1, rows * count), jnp.int32), shaped((32, rows * count))],
    )


def tables(tokens, lengths, head):
    rows = tokens.shape[0]
    half = head // 2

    def kernel(ins, outs, _):
        tokens, lengths = ins
        scale, cosines, sines, column = outs
        values = tokens[...].astype(jnp.float32)
        mean_square = jnp.mean(values * values, axis=1, keepdims=True)
        scale[...] = lax.rsqrt(mean_square + epsilon)
        here = lax.broadcasted_iota(jnp.int32, (rows, rows), 0)
        there = lax.broadcasted_iota(jnp.int32, (rows, rows), 1)
        positions = jnp.sum(
            jnp.where(here == there, lengths[...].astype(jnp.float32), 0.0), axis=1, keepdims=True
        )
        column[...] = positions.astype(jnp.int32)
        lane = lax.broadcasted_iota(jnp.int32, (1, head), 1)
        exponent = (lane % half).astype(jnp.float32) * (-2.0 / head)
        angles = positions * jnp.exp(exponent * math.log(rope_base))
        cosines[...] = jnp.cos(angles)
        sines[...] = jnp.where(lane < half, -1.0, 1.0) * jnp.sin(angles)

    return local_call(
        kernel,
        "tables",
        in_vmem([tokens, lengths]),
        [
            shaped((rows, 1)),
            shaped((rows, head)),
            shaped((rows, head)),
            shaped((rows, 1), jnp.int32),
        ],
        mib=24,
    )


def load(arrays):
    def kernel(ins, outs, _):
        pass

    return local_call(kernel, "load", [], [], carried=arrays)


def spread_lows(low, ids, adapters):
    total = ids.shape[1]
    low = low.astype(jnp.bfloat16).astype(jnp.float32) * adapter_scale
    chosen = lax.broadcasted_iota(jnp.int32, (adapters, 1, total), 0) == ids.reshape(1, 1, total)
    return [
        jnp.where(chosen, low[at : at + 16][None], 0.0)
        .reshape(adapters * 16, total)
        .T.astype(jnp.bfloat16)
        for at in (0, 16)
    ]


def columns_at(start, width):
    return pl.ds(pl.multiple_of(start, width), width)


def project(name, kinds, span, ids, lows, blocks, weights, carried=()):
    wq, wk, wv, uq, uv = weights
    depth = blocks[0].shape[1]
    wide, kv, slots = wq.shape[1], wk.shape[1], uq.shape[0]
    tile = min(512, wide)
    start, total = span

    def kernel(ins, outs, scratch):
        ids, *ins = ins
        low_refs, blocks = ins[: len(lows)], ins[len(lows) : -5]
        wq, wk, wv, uq, uv = ins[-5:]
        xs, spread_q, spread_v = scratch
        at = 0
        for block in blocks:
            xs[at : at + block.shape[0], :] = block[...]
            at += block.shape[0]
        low = low_refs[0][:, start : start + total]
        for other in low_refs[1:]:
            low = low + other[:, start : start + total]
        spread_q[...], spread_v[...] = spread_lows(
            low, ids[:, start : start + total], slots // 16
        )

        def sums(w, spread=None, u=None):
            acc = jnp.dot(xs[...], w, preferred_element_type=jnp.float32)
            if u is not None:
                acc = acc + jnp.dot(spread[...], u, preferred_element_type=jnp.float32)
            return acc

        def write(acc, columns):
            for out, (first, count, dtype) in zip(outs, kinds):
                out[:, columns] = acc[first : first + count].astype(dtype)

        @pl.loop(0, wide // tile)
        def _(i):
            columns = columns_at(i * tile, tile)
            write(sums(wq[:, columns], spread_q, uq[:, columns]), columns)

        write(sums(wk[...]), slice(wide, wide + kv))
        write(sums(wv[...], spread_v, uv[...]), slice(wide + kv, wide + 2 * kv))

    spread = pltpu.VMEM((total, slots), jnp.bfloat16)
    return local_call(
        kernel,
        name,
        in_vmem([ids, *lows, *blocks, *weights]),
        [shaped((count, wide + 2 * kv), dtype) for _, count, dtype in kinds],
        [pltpu.VMEM((total, depth), jnp.bfloat16), spread, spread],
        carried=carried,
    )


def add_sums(name, window, keep, other):
    first, part = window

    def kernel(ins, outs, _):
        keep, other = ins
        outs[0][...] = (
            keep[first : first + part, :] + other[...].astype(jnp.float32)
        ).astype(jnp.bfloat16)

    return local_call(
        kernel, name, in_vmem([keep, other]), [shaped((part, keep.shape[1]), jnp.bfloat16)]
    )[0]


def attend_kernel(first_row, block, done, ins, outs, scratch):
    if done:
        for full, source in zip(outs[1:], ins[:2]):
            full[: source.shape[0], :] = source[...]
    keep, swapped, *moved, scale, cosines, sines, lengths, keys, values = ins[2:] if done else ins
    out, key_out, value_out = outs
    head = cosines.shape[1]
    rows = out.shape[0]
    _, kv_heads, cache, _ = keys.shape
    heads = out.shape[1] // head
    group = heads // kv_heads
    score_scale = 1.0 / math.sqrt(head)
    sub = 8

    column = lax.broadcasted_iota(jnp.int32, (sub, sub * cache), 1)
    start = lax.broadcasted_iota(jnp.int32, (sub, sub * cache), 0) * cache

    @pl.loop(0, rows // block)
    def _(i):
        attended, new_keys, new_values = [], [], []
        for half in range(block // sub):
            here = pl.ds(pl.multiple_of(i * block + half * sub, sub), sub)
            whole = pl.ds(pl.multiple_of(first_row + i * block + half * sub, sub), sub)
            x = keep[whole] + swapped[whole].astype(jnp.float32)
            for m in moved:
                x = x + m[here].astype(jnp.float32)
            x = x * scale[whole]
            cos, sin = cosines[whole], sines[whole]
            inside = (column >= start) & (column < start + lengths[whole])

            def piece(i):
                return x[:, i * head : (i + 1) * head]

            def turn(v):
                return v * cos + pltpu.roll(v, head // 2, 1) * sin

            for g in range(kv_heads):
                query = jnp.concatenate(
                    [turn(piece(g * group + h)) for h in range(group)], axis=0
                ).astype(jnp.bfloat16)
                new_key = turn(piece(heads + g)).astype(jnp.bfloat16).astype(jnp.float32)
                new_value = piece(heads + kv_heads + g).astype(jnp.bfloat16).astype(jnp.float32)
                k = keys[whole, g].reshape(sub * cache, head)
                v = values[whole, g].reshape(sub * cache, head)
                scores = (
                    lax.dot_general(
                        query, k, (((1,), (1,)), ((), ())), preferred_element_type=jnp.float32
                    )
                    * score_scale
                )
                own_key = jnp.concatenate([new_key] * group, axis=0)
                own = (
                    jnp.sum(query.astype(jnp.float32) * own_key, axis=1, keepdims=True)
                    * score_scale
                )
                scores = jnp.where(
                    inside[None], scores.reshape(group, sub, sub * cache), masked_score
                ).reshape(group * sub, sub * cache)
                peak = jnp.maximum(jnp.max(scores, axis=1, keepdims=True), own)
                weights = jnp.exp(scores - peak)
                own_weight = jnp.exp(own - peak)
                inverse = 1.0 / (jnp.sum(weights, axis=1, keepdims=True) + own_weight)
                mixed = jnp.dot(weights.astype(jnp.bfloat16), v, preferred_element_type=jnp.float32)
                own_value = jnp.concatenate([new_value] * group, axis=0)
                mixed = (mixed + own_weight * own_value) * inverse
                attended += [mixed[h * sub : (h + 1) * sub] for h in range(group)]
                new_keys.append(new_key)
                new_values.append(new_value)
        r = pl.ds(pl.multiple_of(i * block, block), block)

        def joined(pieces):
            n = len(pieces) * sub // block
            return jnp.concatenate(
                [jnp.concatenate(pieces[j::n], axis=0) for j in range(n)], axis=1
            ).astype(jnp.bfloat16)

        out[r] = joined(attended)
        r = pl.ds(pl.multiple_of((first_row if done else 0) + i * block, block), block)
        key_out[r] = joined(new_keys)
        value_out[r] = joined(new_values)


def attend(name, window, keep, swapped, moved, rest, keys, values, earlier, carried=()):
    _, columns = keep.shape
    _, kv_heads, _, head = keys.shape
    kv_cols = kv_heads * head
    first, part = window
    kv_rows = first + part if earlier else part
    return local_call(
        functools.partial(attend_kernel, first, 16, bool(earlier)),
        name,
        in_vmem([*earlier, keep, swapped, *moved, *rest, keys, values]),
        [
            shaped((part, columns - 2 * kv_cols), jnp.bfloat16),
            *[shaped((kv_rows, kv_cols), jnp.bfloat16)] * 2,
        ],
        carried=carried,
    )


def output_part(name, span, order, blocks, weights):
    rows = blocks[0].shape[0]
    first, columns = span
    depth = weights.shape[0]
    tile = math.gcd(512, columns)
    total = rows * len(blocks)

    def kernel(ins, outs, scratch):
        order, *blocks, weights = ins
        keep, send = outs
        (xs,) = scratch
        for b, block in enumerate(blocks):
            xs[pl.ds(pl.multiple_of(order[b] * rows, rows), rows), :] = block[...]

        @pl.loop(0, columns // tile)
        def _(i):
            w = weights[:, columns_at(first + i * tile, tile)]
            acc = jnp.dot(xs[...], w, preferred_element_type=jnp.float32).astype(jnp.bfloat16)
            keep[:, columns_at(i * tile, tile)] = acc[: total // 2]
            send[:, columns_at(i * tile, tile)] = acc[total // 2 :]

    return local_call(
        kernel,
        name,
        [(order, SMEM), *in_vmem([*blocks, weights])],
        [shaped((total // 2, columns), jnp.bfloat16)] * 2,
        [pltpu.VMEM((total, depth), jnp.bfloat16)],
    )


def add_halves(name, keep, got):
    half, columns = keep.shape[0] // 2, keep.shape[1]

    def kernel(ins, outs, _):
        keep, got = ins
        total = keep[...].astype(jnp.float32) + got[...].astype(jnp.float32)
        outs[0][...] = total[:half]
        outs[1][...] = total[half:].astype(jnp.bfloat16)

    return local_call(
        kernel,
        name,
        in_vmem([keep, got]),
        [shaped((half, columns)), shaped((half, columns), jnp.bfloat16)],
    )


def add_last(name, keep, got):
    def kernel(ins, outs, _):
        total = ins[0][...].astype(jnp.float32) + ins[1][...].astype(jnp.float32)
        outs[0][...] = total.astype(jnp.bfloat16)

    return local_call(kernel, name, in_vmem([keep, got]), [shaped(keep.shape, jnp.bfloat16)])[0]


def assemble(done, keep, got, places, rows, columns):
    def kernel(ins, outs, _):
        *done, keep, got = ins
        total = keep[...].astype(jnp.float32) + got[...].astype(jnp.float32)
        total = total.astype(jnp.bfloat16)
        for piece, spots in zip([*done, total], places):
            for at, to, count, column in spots:
                outs[0][to : to + count, column : column + piece.shape[1]] = piece[
                    at : at + count, :
                ]

    return local_call(
        kernel,
        "assemble",
        in_vmem([*done, keep, got]),
        [shaped((rows, columns), jnp.bfloat16)],
    )[0]


def reversed_bits(x, count):
    out, bit = 0, 1
    while bit < count:
        out = out * 2 + (x // bit) % 2
        bit *= 2
    return out


def shards(
    tokens,
    input_norm_gain,
    query_matrix,
    key_matrix,
    value_matrix,
    output_matrix,
    rotated_key_cache,
    cached_value_rows,
    cache_length_per_row,
    row_adapter_index,
    query_down_maps,
    query_up_maps,
    value_down_maps,
    value_up_maps,
):
    pool_count = lax.axis_size("pool")
    tp_count = lax.axis_size("tp")
    chips = pool_count // 2
    pool_at = lax.axis_index("pool")
    tp_at = lax.axis_index("tp")
    chip, core = pool_at // 2, pool_at % 2
    rows = tokens.shape[0]
    adapters, rank, piece = query_down_maps.shape
    base = query_matrix.shape[0]
    kv_heads = rotated_key_cache.shape[1]
    head = rotated_key_cache.shape[3]

    def scaled(start, width, tokens=tokens, gain=input_norm_gain, window=(0, rows)):
        x = lax.dynamic_slice(tokens, (window[0], start), (window[1], width)).astype(jnp.float32)
        factor = lax.dynamic_slice_in_dim(gain, start, width, 0).astype(jnp.float32)
        return (x * factor[None, :]).astype(jnp.bfloat16)

    own_ids = row_adapter_index.reshape(1, rows)
    ids = [
        own_ids if d == e == 0 else chip_move(own_ids, pool_count, d, e)
        for d in range(chips)
        for e in range(2)
    ]
    first = after(scaled(tp_at * piece, piece), *ids[1:])
    first, tokens_1, gain_1 = lax.optimization_barrier((first, tokens, input_norm_gain))
    same_core = [first] + [chip_move(first, pool_count, d) for d in range(1, chips)]

    cut = rows // 2
    chunks = [(0, cut), (cut, rows - cut)]
    own = scaled(pool_at * base, base, tokens_1, gain_1)
    partner_at = (pool_at // 2 * 2 + 1 - core) * base
    partner = [
        scaled(partner_at, base, tokens_1, gain_1, (at, rows // 2)) for at in (0, rows // 2)
    ]
    away = {}
    for d in range(1, chips):
        for e in range(2):
            target = (chip + d) % chips * 2 + (core + e) % 2
            away[d, e] = scaled(target * base, base, tokens_1, gain_1)
    first_id = (pool_at * adapters).reshape(1).astype(jnp.int32)
    lengths = cache_length_per_row.reshape(1, rows)
    share = pool_count // tp_count
    order = []
    for d in range(chips):
        for e in range(2):
            p = (chip - d) % chips * 2 + (core + e) % 2
            order.append(
                reversed_bits(jnp.bitwise_xor(p // share, tp_at), tp_count) * share + p % share
            )
    order = jnp.stack(order).astype(jnp.int32)

    flat_down = [x.reshape(adapters * rank, piece) for x in (query_down_maps, value_down_maps)]
    flat_up = [x.reshape(adapters * rank, x.shape[2]) for x in (query_up_maps, value_up_maps)]
    small = [own, *partner, *away.values(), first_id, lengths, order]
    query_matrix, *small = lax.optimization_barrier((query_matrix, *small))
    own, partner, small = small[0], small[1:3], small[3:]
    away = dict(zip(away, small))
    first_id, lengths, order = small[-3:]
    down_q, down_v, *weights = load(
        [*flat_down, query_matrix, key_matrix, value_matrix, *flat_up]
    )
    partner = [core_swap(x, pool_count) for x in partner]
    remote = [[] for _ in range(chips)]
    for (d, e), x in away.items():
        remote[d].append(chip_move(after(x, *same_core[1:]), pool_count, d, e))
    same_core[1:] = [after(x, down_q) for x in same_core[1:]]
    adapter_rows = [b for x in same_core for b in (x, core_swap(x, pool_count))]
    local_ids, shrunk = shrink(first_id, ids, adapter_rows, down_q, down_v)
    lows = [shrunk] + [
        lax.ppermute(shrunk, "tp", [(i, (i + d) % tp_count) for i in range(tp_count)])
        for d in range(1, tp_count)
    ]
    rest = tables(tokens, after(lengths, shrunk), head)
    own_sums, own_send, keys, values = project(
        "project_own",
        [(0, rows, jnp.float32), (rows, rows, jnp.bfloat16)],
        (0, 2 * rows),
        after(local_ids, rest[0]),
        lows,
        [own, *partner],
        weights,
        carried=[rotated_key_cache, cached_value_rows],
    )
    swapped = core_swap(own_send, pool_count)
    local_ids = after(local_ids, own_sums)
    moved = [[] for _ in chunks]
    both = None
    for d in range(1, chips):
        if both is not None:
            remote[d][0] = after(remote[d][0], both)
        at = 2 * d * rows
        (keep,) = project(
            f"project_{d}_0",
            [(0, rows, jnp.float32)],
            (at, rows),
            local_ids,
            lows,
            remote[d][:1],
            weights,
        )
        sends = project(
            f"project_{d}_1",
            [(first, part, jnp.bfloat16) for first, part in chunks],
            (at + rows, rows),
            local_ids,
            lows,
            [after(remote[d][1], keep)],
            weights,
        )
        for c, window in enumerate(chunks):
            swap = core_swap(sends[c], pool_count)
            if c:
                swap = after(swap, both)
            both = add_sums(f"add_{d}_{c}", window, keep, swap)
            moved[c].append(chip_move(both, pool_count, -d))
    moved[0][0] = after(moved[0][0], both)

    attended, earlier = [], []
    for c, window in enumerate(chunks):
        out, *earlier = attend(
            f"attend_{c}",
            window,
            own_sums,
            swapped,
            moved[c],
            rest,
            keys,
            values,
            earlier[:2],
            [] if c else [output_matrix],
        )
        if c == 0:
            out_weights = earlier[2]
        if c + 1 < len(chunks):
            out, *moved[c + 1] = lax.optimization_barrier((out, *moved[c + 1]))
        else:
            out = after(out, attended[-1][-1])
        attended.append([out] + [chip_move(out, pool_count, d) for d in range(1, chips)])
    new_key, new_value = earlier
    attended[0][0] = after(attended[0][0], new_key)

    columns = output_matrix.shape[1]
    layout = [(0, 0, 1), (1, 0, 2), (1, 2, 4), (1, 3, 4)]
    gathered, keeps, sends, products = {}, [], [], []

    def multiply():
        c, at, count = layout[len(keeps)]
        if c not in gathered:
            parts = [after(x, products[-1]) for x in attended[c]] if c else attended[c]
            gathered[c] = [b for x in parts for b in (x, core_swap(x, pool_count))]
        else:
            gathered[c][0] = after(gathered[c][0], products[-1])
        width = columns // count
        keep, send = output_part(
            f"output_{c}_{at}_{count}", (at * width, width), order, gathered[c], out_weights
        )
        keeps.append(keep)
        sends.append(send)
        products.append(keep)

    stages = reversed_bits(1, tp_count).bit_length()
    last = len(layout) - 1
    total, got, done, places = None, {}, [], []
    for i, (c, at, count) in enumerate(layout):
        start, part = chunks[c]
        column = at * columns // count
        places.append([(r * part, r * rows + start, part, column) for r in range(share)])
    for slot in range(last + stages):
        while len(keeps) < min(slot + 2, last + 1):
            multiply()
        for stage in range(stages):
            i = slot - stage
            if not 0 <= i <= last:
                continue
            if stage == 0:
                got[i] = tp_swap(sends[i], tp_count, 1)
            past = [products[-1]] + ([] if total is None else [total])
            came = after(got[i], *past)
            if stage + 1 < stages:
                keeps[i], total = add_halves(f"halves_{i}_{stage}", keeps[i], came)
                got[i] = tp_swap(total, tp_count, 2 << stage)
            elif i < last:
                total = add_last(f"last_{i}", keeps[i], came)
                done.append(total)
            else:
                attn_out = assemble(done, keeps[i], came, places, share * rows, columns)
    return attn_out, new_key, new_value


def solution(mesh):
    return jax.shard_map(
        shards,
        mesh=mesh,
        in_specs=(
            P(("groups", "pool"), None),
            P(),
            P("pool", "tp"),
            P("pool", "tp"),
            P("pool", "tp"),
            P("tp", "pool"),
            P(("groups", "pool"), "tp", None, None),
            P(("groups", "pool"), "tp", None, None),
            P(("groups", "pool")),
            P(("groups", "pool")),
            P("pool", None, "tp"),
            P("pool", None, "tp"),
            P("pool", None, "tp"),
            P("pool", None, "tp"),
        ),
        out_specs=(
            P(("groups", "tp"), "pool"),
            P(("groups", "pool"), "tp"),
            P(("groups", "pool"), "tp"),
        ),
        check_vma=False,
    )
```

```python
import functools
import math

import jax
import jax.numpy as jnp
from jax import lax
from jax.experimental import pallas as pl
from jax.experimental.pallas import tpu as pltpu
from jax.sharding import PartitionSpec as P

epsilon = 1e-05
adapter_scale = 0.5
rope_base = 500000.0
masked_score = -1e30


VMEM = pl.BlockSpec(memory_space=pltpu.VMEM)
HBM = pl.BlockSpec(memory_space=pltpu.HBM)
SMEM = pl.BlockSpec(memory_space=pltpu.SMEM)


def local_call(kernel, name, operands, outs, scratch=(), carried=(), mib=16):
    counts = (len(operands), len(carried), len(outs), len(carried), len(scratch))

    def body(*refs):
        groups, at = [], 0
        for n in counts:
            groups.append(refs[at : at + n])
            at += n
        ins, sources, out_refs, targets, scratch_refs = groups
        copies = [
            pltpu.make_async_copy(source, target, refs[-1].at[i])
            for i, (source, target) in enumerate(zip(sources, targets))
        ]
        for copy in copies:
            copy.start()
        kernel(ins, out_refs, scratch_refs)
        for copy in copies:
            copy.wait()

    sems = [pltpu.SemaphoreType.DMA((len(carried),))] if carried else []
    return pl.pallas_call(
        body,
        in_specs=[spec for _, spec in operands] + [HBM] * len(carried),
        out_specs=[VMEM] * (len(outs) + len(carried)),
        out_shape=[*outs, *[pltpu.VMEM(x.shape, x.dtype) for x in carried]],
        scratch_shapes=[*scratch, *sems],
        compiler_params=pltpu.CompilerParams(vmem_limit_bytes=mib * 1024 * 1024),
        cost_estimate=pl.CostEstimate(flops=1000, bytes_accessed=1000, transcendentals=0),
        name=name,
    )(
        *[x for x, _ in operands],
        *[pltpu.with_memory_space_constraint(x, pltpu.HBM) for x in carried],
    )


def in_vmem(arrays):
    return [(x, VMEM) for x in arrays]


def shaped(shape, dtype=jnp.float32):
    return jax.ShapeDtypeStruct(shape, dtype)


def after(x, *earlier):
    return lax.optimization_barrier((x, *earlier))[0]


def core_swap(x, pool_count):
    return lax.ppermute(x, "pool", [(p, p ^ 1) for p in range(pool_count)])


def chip_move(x, pool_count, d, e=0):
    chips = pool_count // 2
    return lax.ppermute(
        x,
        "pool",
        [(p, (p // 2 + d) % chips * 2 + ((p % 2) ^ e)) for p in range(pool_count)],
    )


def tp_swap(x, tp_count, step):
    return lax.ppermute(x, "tp", [(z, z ^ step) for z in range(tp_count)])


def shrink(first_id, ids, blocks, query_down, value_down):
    slots, _ = query_down.shape
    rows = blocks[0].shape[0]
    adapters = slots // 16
    count = len(blocks)

    def kernel(ins, outs, _):
        first_id, *ins = ins
        ids, blocks, tables = ins[:count], ins[count : 2 * count], ins[2 * count :]
        local_ids, out = outs
        for b in range(count):
            local_ids[:, b * rows : (b + 1) * rows] = ids[b][...] - first_id[0]
        for first in range(0, count, 2):
            x = jnp.concatenate([b[...] for b in blocks[first : first + 2]], axis=0)
            span = slice(first * rows, (first + 2) * rows)
            label = local_ids[:, span].reshape(1, 1, 2 * rows)
            chosen = lax.broadcasted_iota(jnp.int32, (adapters, 1, 2 * rows), 0) == label
            for at, table in enumerate(tables):
                terms = lax.dot_general(
                    table[...], x, (((1,), (1,)), ((), ())), preferred_element_type=jnp.float32
                ).reshape(adapters, 16, 2 * rows)
                out[at * 16 : (at + 1) * 16, span] = jnp.sum(
                    jnp.where(chosen, terms, 0.0), axis=0
                )

    return local_call(
        kernel,
        "shrink",
        [(first_id, SMEM), *in_vmem([*ids, *blocks, query_down, value_down])],
        [shaped((1, rows * count), jnp.int32), shaped((32, rows * count))],
    )


def tables(tokens, lengths, head):
    rows = tokens.shape[0]
    half = head // 2

    def kernel(ins, outs, _):
        tokens, lengths = ins
        scale, cosines, sines, column = outs
        values = tokens[...].astype(jnp.float32)
        mean_square = jnp.mean(values * values, axis=1, keepdims=True)
        scale[...] = lax.rsqrt(mean_square + epsilon)
        here = lax.broadcasted_iota(jnp.int32, (rows, rows), 0)
        there = lax.broadcasted_iota(jnp.int32, (rows, rows), 1)
        positions = jnp.sum(
            jnp.where(here == there, lengths[...].astype(jnp.float32), 0.0), axis=1, keepdims=True
        )
        column[...] = positions.astype(jnp.int32)
        lane = lax.broadcasted_iota(jnp.int32, (1, head), 1)
        exponent = (lane % half).astype(jnp.float32) * (-2.0 / head)
        angles = positions * jnp.exp(exponent * math.log(rope_base))
        cosines[...] = jnp.cos(angles)
        sines[...] = jnp.where(lane < half, -1.0, 1.0) * jnp.sin(angles)

    return local_call(
        kernel,
        "tables",
        in_vmem([tokens, lengths]),
        [
            shaped((rows, 1)),
            shaped((rows, head)),
            shaped((rows, head)),
            shaped((rows, 1), jnp.int32),
        ],
        mib=24,
    )


def load(arrays):
    def kernel(ins, outs, _):
        pass

    return local_call(kernel, "load", [], [], carried=arrays)


def spread_lows(low, ids, adapters):
    total = ids.shape[1]
    low = low.astype(jnp.bfloat16).astype(jnp.float32) * adapter_scale
    chosen = lax.broadcasted_iota(jnp.int32, (adapters, 1, total), 0) == ids.reshape(1, 1, total)
    return [
        jnp.where(chosen, low[at : at + 16][None], 0.0)
        .reshape(adapters * 16, total)
        .T.astype(jnp.bfloat16)
        for at in (0, 16)
    ]


def columns_at(start, width):
    return pl.ds(pl.multiple_of(start, width), width)


def project(name, kinds, span, ids, lows, blocks, weights, carried=()):
    wq, wk, wv, uq, uv = weights
    depth = blocks[0].shape[1]
    wide, kv, slots = wq.shape[1], wk.shape[1], uq.shape[0]
    tile = min(512, wide)
    start, total = span

    def kernel(ins, outs, scratch):
        ids, *ins = ins
        low_refs, blocks = ins[: len(lows)], ins[len(lows) : -5]
        wq, wk, wv, uq, uv = ins[-5:]
        xs, spread_q, spread_v = scratch
        at = 0
        for block in blocks:
            xs[at : at + block.shape[0], :] = block[...]
            at += block.shape[0]
        low = low_refs[0][:, start : start + total]
        for other in low_refs[1:]:
            low = low + other[:, start : start + total]
        spread_q[...], spread_v[...] = spread_lows(
            low, ids[:, start : start + total], slots // 16
        )

        def sums(w, spread=None, u=None):
            acc = jnp.dot(xs[...], w, preferred_element_type=jnp.float32)
            if u is not None:
                acc = acc + jnp.dot(spread[...], u, preferred_element_type=jnp.float32)
            return acc

        def write(acc, columns):
            for out, (first, count, dtype) in zip(outs, kinds):
                out[:, columns] = acc[first : first + count].astype(dtype)

        @pl.loop(0, wide // tile)
        def _(i):
            columns = columns_at(i * tile, tile)
            write(sums(wq[:, columns], spread_q, uq[:, columns]), columns)

        write(sums(wk[...]), slice(wide, wide + kv))
        write(sums(wv[...], spread_v, uv[...]), slice(wide + kv, wide + 2 * kv))

    spread = pltpu.VMEM((total, slots), jnp.bfloat16)
    return local_call(
        kernel,
        name,
        in_vmem([ids, *lows, *blocks, *weights]),
        [shaped((count, wide + 2 * kv), dtype) for _, count, dtype in kinds],
        [pltpu.VMEM((total, depth), jnp.bfloat16), spread, spread],
        carried=carried,
    )


def add_sums(name, window, keep, other):
    first, part = window

    def kernel(ins, outs, _):
        keep, other = ins
        outs[0][...] = (
            keep[first : first + part, :] + other[...].astype(jnp.float32)
        ).astype(jnp.bfloat16)

    return local_call(
        kernel, name, in_vmem([keep, other]), [shaped((part, keep.shape[1]), jnp.bfloat16)]
    )[0]


def attend_kernel(first_row, block, done, ins, outs, scratch):
    if done:
        for full, source in zip(outs[1:], ins[:2]):
            full[: source.shape[0], :] = source[...]
    keep, swapped, *moved, scale, cosines, sines, lengths, keys, values = ins[2:] if done else ins
    out, key_out, value_out = outs
    head = cosines.shape[1]
    rows = out.shape[0]
    _, kv_heads, cache, _ = keys.shape
    heads = out.shape[1] // head
    group = heads // kv_heads
    score_scale = 1.0 / math.sqrt(head)
    sub = 8

    column = lax.broadcasted_iota(jnp.int32, (sub, sub * cache), 1)
    start = lax.broadcasted_iota(jnp.int32, (sub, sub * cache), 0) * cache

    @pl.loop(0, rows // block)
    def _(i):
        attended, new_keys, new_values = [], [], []
        for half in range(block // sub):
            here = pl.ds(pl.multiple_of(i * block + half * sub, sub), sub)
            whole = pl.ds(pl.multiple_of(first_row + i * block + half * sub, sub), sub)
            x = keep[whole] + swapped[whole].astype(jnp.float32)
            for m in moved:
                x = x + m[here].astype(jnp.float32)
            x = x * scale[whole]
            cos, sin = cosines[whole], sines[whole]
            inside = (column >= start) & (column < start + lengths[whole])

            def piece(i):
                return x[:, i * head : (i + 1) * head]

            def turn(v):
                return v * cos + pltpu.roll(v, head // 2, 1) * sin

            for g in range(kv_heads):
                query = jnp.concatenate(
                    [turn(piece(g * group + h)) for h in range(group)], axis=0
                ).astype(jnp.bfloat16)
                new_key = turn(piece(heads + g)).astype(jnp.bfloat16).astype(jnp.float32)
                new_value = piece(heads + kv_heads + g).astype(jnp.bfloat16).astype(jnp.float32)
                k = keys[whole, g].reshape(sub * cache, head)
                v = values[whole, g].reshape(sub * cache, head)
                scores = (
                    lax.dot_general(
                        query, k, (((1,), (1,)), ((), ())), preferred_element_type=jnp.float32
                    )
                    * score_scale
                )
                own_key = jnp.concatenate([new_key] * group, axis=0)
                own = (
                    jnp.sum(query.astype(jnp.float32) * own_key, axis=1, keepdims=True)
                    * score_scale
                )
                scores = jnp.where(
                    inside[None], scores.reshape(group, sub, sub * cache), masked_score
                ).reshape(group * sub, sub * cache)
                peak = jnp.maximum(jnp.max(scores, axis=1, keepdims=True), own)
                weights = jnp.exp(scores - peak)
                own_weight = jnp.exp(own - peak)
                inverse = 1.0 / (jnp.sum(weights, axis=1, keepdims=True) + own_weight)
                mixed = jnp.dot(weights.astype(jnp.bfloat16), v, preferred_element_type=jnp.float32)
                own_value = jnp.concatenate([new_value] * group, axis=0)
                mixed = (mixed + own_weight * own_value) * inverse
                attended += [mixed[h * sub : (h + 1) * sub] for h in range(group)]
                new_keys.append(new_key)
                new_values.append(new_value)
        r = pl.ds(pl.multiple_of(i * block, block), block)

        def joined(pieces):
            n = len(pieces) * sub // block
            return jnp.concatenate(
                [jnp.concatenate(pieces[j::n], axis=0) for j in range(n)], axis=1
            ).astype(jnp.bfloat16)

        out[r] = joined(attended)
        r = pl.ds(pl.multiple_of((first_row if done else 0) + i * block, block), block)
        key_out[r] = joined(new_keys)
        value_out[r] = joined(new_values)


def attend(name, window, keep, swapped, moved, rest, keys, values, earlier, carried=()):
    _, columns = keep.shape
    _, kv_heads, _, head = keys.shape
    kv_cols = kv_heads * head
    first, part = window
    kv_rows = first + part if earlier else part
    return local_call(
        functools.partial(attend_kernel, first, 16, bool(earlier)),
        name,
        in_vmem([*earlier, keep, swapped, *moved, *rest, keys, values]),
        [
            shaped((part, columns - 2 * kv_cols), jnp.bfloat16),
            *[shaped((kv_rows, kv_cols), jnp.bfloat16)] * 2,
        ],
        carried=carried,
    )


def output_part(name, span, order, blocks, weights):
    rows = blocks[0].shape[0]
    first, columns = span
    depth = weights.shape[0]
    tile = math.gcd(512, columns)
    total = rows * len(blocks)

    def kernel(ins, outs, scratch):
        order, *blocks, weights = ins
        keep, send = outs
        (xs,) = scratch
        for b, block in enumerate(blocks):
            xs[pl.ds(pl.multiple_of(order[b] * rows, rows), rows), :] = block[...]

        @pl.loop(0, columns // tile)
        def _(i):
            w = weights[:, columns_at(first + i * tile, tile)]
            acc = jnp.dot(xs[...], w, preferred_element_type=jnp.float32).astype(jnp.bfloat16)
            keep[:, columns_at(i * tile, tile)] = acc[: total // 2]
            send[:, columns_at(i * tile, tile)] = acc[total // 2 :]

    return local_call(
        kernel,
        name,
        [(order, SMEM), *in_vmem([*blocks, weights])],
        [shaped((total // 2, columns), jnp.bfloat16)] * 2,
        [pltpu.VMEM((total, depth), jnp.bfloat16)],
    )


def add_halves(name, keep, got):
    half, columns = keep.shape[0] // 2, keep.shape[1]

    def kernel(ins, outs, _):
        keep, got = ins
        total = keep[...].astype(jnp.float32) + got[...].astype(jnp.float32)
        outs[0][...] = total[:half]
        outs[1][...] = total[half:].astype(jnp.bfloat16)

    return local_call(
        kernel,
        name,
        in_vmem([keep, got]),
        [shaped((half, columns)), shaped((half, columns), jnp.bfloat16)],
    )


def add_last(name, keep, got):
    def kernel(ins, outs, _):
        total = ins[0][...].astype(jnp.float32) + ins[1][...].astype(jnp.float32)
        outs[0][...] = total.astype(jnp.bfloat16)

    return local_call(kernel, name, in_vmem([keep, got]), [shaped(keep.shape, jnp.bfloat16)])[0]


def assemble(done, keep, got, places, rows, columns):
    def kernel(ins, outs, _):
        *done, keep, got = ins
        total = keep[...].astype(jnp.float32) + got[...].astype(jnp.float32)
        total = total.astype(jnp.bfloat16)
        for piece, spots in zip([*done, total], places):
            for at, to, count, column in spots:
                outs[0][to : to + count, column : column + piece.shape[1]] = piece[
                    at : at + count, :
                ]

    return local_call(
        kernel,
        "assemble",
        in_vmem([*done, keep, got]),
        [shaped((rows, columns), jnp.bfloat16)],
    )[0]


def reversed_bits(x, count):
    out, bit = 0, 1
    while bit < count:
        out = out * 2 + (x // bit) % 2
        bit *= 2
    return out


def shards(
    tokens,
    input_norm_gain,
    query_matrix,
    key_matrix,
    value_matrix,
    output_matrix,
    rotated_key_cache,
    cached_value_rows,
    cache_length_per_row,
    row_adapter_index,
    query_down_maps,
    query_up_maps,
    value_down_maps,
    value_up_maps,
):
    pool_count = lax.axis_size("pool")
    tp_count = lax.axis_size("tp")
    chips = pool_count // 2
    pool_at = lax.axis_index("pool")
    tp_at = lax.axis_index("tp")
    chip, core = pool_at // 2, pool_at % 2
    rows = tokens.shape[0]
    adapters, rank, piece = query_down_maps.shape
    base = query_matrix.shape[0]
    kv_heads = rotated_key_cache.shape[1]
    head = rotated_key_cache.shape[3]

    def scaled(start, width, tokens=tokens, gain=input_norm_gain, window=(0, rows)):
        x = lax.dynamic_slice(tokens, (window[0], start), (window[1], width)).astype(jnp.float32)
        factor = lax.dynamic_slice_in_dim(gain, start, width, 0).astype(jnp.float32)
        return (x * factor[None, :]).astype(jnp.bfloat16)

    own_ids = row_adapter_index.reshape(1, rows)
    ids = [
        own_ids if d == e == 0 else chip_move(own_ids, pool_count, d, e)
        for d in range(chips)
        for e in range(2)
    ]
    first = after(scaled(tp_at * piece, piece), *ids[1:])
    first, tokens_1, gain_1 = lax.optimization_barrier((first, tokens, input_norm_gain))
    same_core = [first] + [chip_move(first, pool_count, d) for d in range(1, chips)]

    cuts = [0, rows // 4, rows // 2, rows]
    chunks = [(start, stop - start) for start, stop in zip(cuts, cuts[1:])]
    own = scaled(pool_at * base, base, tokens_1, gain_1)
    partner_at = (pool_at // 2 * 2 + 1 - core) * base
    partner = [
        scaled(partner_at, base, tokens_1, gain_1, (at, rows // 2)) for at in (0, rows // 2)
    ]
    away = {}
    for d in range(1, chips):
        for e in range(2):
            target = (chip + d) % chips * 2 + (core + e) % 2
            away[d, e] = scaled(target * base, base, tokens_1, gain_1)
    first_id = (pool_at * adapters).reshape(1).astype(jnp.int32)
    lengths = cache_length_per_row.reshape(1, rows)
    share = pool_count // tp_count
    order = []
    for d in range(chips):
        for e in range(2):
            p = (chip - d) % chips * 2 + (core + e) % 2
            order.append(
                reversed_bits(jnp.bitwise_xor(p // share, tp_at), tp_count) * share + p % share
            )
    order = jnp.stack(order).astype(jnp.int32)

    flat_down = [x.reshape(adapters * rank, piece) for x in (query_down_maps, value_down_maps)]
    flat_up = [x.reshape(adapters * rank, x.shape[2]) for x in (query_up_maps, value_up_maps)]
    small = [own, *partner, *away.values(), first_id, lengths, order]
    query_matrix, *small = lax.optimization_barrier((query_matrix, *small))
    own, partner, small = small[0], small[1:3], small[3:]
    away = dict(zip(away, small))
    first_id, lengths, order = small[-3:]
    down_q, down_v, *weights = load(
        [*flat_down, query_matrix, key_matrix, value_matrix, *flat_up]
    )
    partner = [core_swap(x, pool_count) for x in partner]
    remote = [[] for _ in range(chips)]
    for (d, e), x in away.items():
        remote[d].append(chip_move(after(x, *same_core[1:]), pool_count, d, e))
    same_core[1:] = [after(x, down_q) for x in same_core[1:]]
    adapter_rows = [b for x in same_core for b in (x, core_swap(x, pool_count))]
    local_ids, shrunk = shrink(first_id, ids, adapter_rows, down_q, down_v)
    lows = [shrunk] + [
        lax.ppermute(shrunk, "tp", [(i, (i + d) % tp_count) for i in range(tp_count)])
        for d in range(1, tp_count)
    ]
    rest = tables(tokens, after(lengths, shrunk), head)
    own_sums, own_send, keys, values = project(
        "project_own",
        [(0, rows, jnp.float32), (rows, rows, jnp.bfloat16)],
        (0, 2 * rows),
        after(local_ids, rest[0]),
        lows,
        [own, *partner],
        weights,
        carried=[rotated_key_cache, cached_value_rows],
    )
    swapped = core_swap(own_send, pool_count)
    local_ids = after(local_ids, own_sums)
    partial, send = [], None
    for d in range(1, chips):
        if partial:
            remote[d][0] = after(remote[d][0], sends[0])
        at = 2 * d * rows
        (keep,) = project(
            f"project_{d}_0",
            [(0, rows, jnp.float32)],
            (at, rows),
            local_ids,
            lows,
            remote[d][:1],
            weights,
        )
        sends = project(
            f"project_{d}_1",
            [(first, part, jnp.bfloat16) for first, part in chunks],
            (at + rows, rows),
            local_ids,
            lows,
            [after(remote[d][1], keep)],
            weights,
        )
        partial.append((d, keep, sends))

    def reduced(c, *earlier):
        arrived = []
        for d, keep, sends in partial:
            swap = after(core_swap(sends[c], pool_count), *earlier)
            both = add_sums(f"add_{d}_{c}", chunks[c], keep, swap)
            arrived.append(chip_move(both, pool_count, -d))
            earlier = [both]
        return arrived, both

    moved = [None] * len(chunks)
    moved[0], both = reduced(0)
    moved[1], both = reduced(1, both)
    moved[0][0] = after(moved[0][0], both)

    columns = output_matrix.shape[1]
    layout = [(0, 0, 1), (1, 0, 1), (2, 0, 2), (2, 2, 4), (2, 3, 4)]
    attended, gathered, keeps, sends, products = [], {}, [], [], []

    def multiply(*earlier):
        c, at, count = layout[len(keeps)]
        if c not in gathered:
            parts = [after(x, *earlier) for x in attended[c]]
            gathered[c] = [b for x in parts for b in (x, core_swap(x, pool_count))]
        else:
            gathered[c][0] = after(gathered[c][0], products[-1])
        width = columns // count
        keep, send = output_part(
            f"output_{c}_{at}_{count}", (at * width, width), order, gathered[c], out_weights
        )
        keeps.append(keep)
        sends.append(send)
        products.append(keep)

    earlier = []
    for c, window in enumerate(chunks):
        if c == 2:
            multiply(earlier[0], both)
            moved[c][0] = after(moved[c][0], products[-1])
        out, *earlier = attend(
            f"attend_{c}",
            window,
            own_sums,
            swapped,
            moved[c],
            rest,
            keys,
            values,
            earlier[:2],
            [] if c else [output_matrix],
        )
        if c == 0:
            out_weights = earlier[2]
            out, *moved[1] = lax.optimization_barrier((out, *moved[1]))
        else:
            out = after(out, attended[-1][-1])
        attended.append([out] + [chip_move(out, pool_count, d) for d in range(1, chips)])
        if c + 2 < len(chunks):
            moved[c + 2], both = reduced(c + 2, attended[c][-1])
    new_key, new_value = earlier

    stages = reversed_bits(1, tp_count).bit_length()
    last = len(layout) - 1
    total, got, done, places = None, {}, [], []
    for i, (c, at, count) in enumerate(layout):
        start, part = chunks[c]
        column = at * columns // count
        places.append([(r * part, r * rows + start, part, column) for r in range(share)])
    for slot in range(last + stages):
        while len(keeps) < min(slot + 1 if slot < 2 else slot + 2, last + 1):
            multiply(products[-1], total, new_key)
        for stage in reversed(range(stages)) if slot < 3 else range(stages):
            i = slot - stage
            if not 0 <= i <= last:
                continue
            if stage == 0:
                got[i] = tp_swap(sends[i], tp_count, 1)
            past = [products[-1]] + ([] if total is None else [total])
            came = after(got[i], *past)
            if stage + 1 < stages:
                keeps[i], total = add_halves(f"halves_{i}_{stage}", keeps[i], came)
                got[i] = tp_swap(total, tp_count, 2 << stage)
            elif i < last:
                total = add_last(f"last_{i}", keeps[i], came)
                done.append(total)
            else:
                attn_out = assemble(done, keeps[i], came, places, share * rows, columns)
    return attn_out, new_key, new_value


def solution(mesh):
    return jax.shard_map(
        shards,
        mesh=mesh,
        in_specs=(
            P(("groups", "pool"), None),
            P(),
            P("pool", "tp"),
            P("pool", "tp"),
            P("pool", "tp"),
            P("tp", "pool"),
            P(("groups", "pool"), "tp", None, None),
            P(("groups", "pool"), "tp", None, None),
            P(("groups", "pool")),
            P(("groups", "pool")),
            P("pool", None, "tp"),
            P("pool", None, "tp"),
            P("pool", None, "tp"),
            P("pool", None, "tp"),
        ),
        out_specs=(
            P(("groups", "tp"), "pool"),
            P(("groups", "pool"), "tp"),
            P(("groups", "pool"), "tp"),
        ),
        check_vma=False,
    )
```

```python
import functools
import math

import jax
import jax.numpy as jnp
from jax import lax
from jax.experimental import pallas as pl
from jax.experimental.pallas import tpu as pltpu
from jax.sharding import PartitionSpec as P

epsilon = 1e-05
adapter_scale = 0.5
rope_base = 500000.0
masked_score = -1e30


VMEM = pl.BlockSpec(memory_space=pltpu.VMEM)
HBM = pl.BlockSpec(memory_space=pltpu.HBM)
SMEM = pl.BlockSpec(memory_space=pltpu.SMEM)


def local_call(kernel, name, operands, outs, scratch=(), carried=(), mib=16):
    counts = (len(operands), len(carried), len(outs), len(carried), len(scratch))

    def body(*refs):
        groups, at = [], 0
        for n in counts:
            groups.append(refs[at : at + n])
            at += n
        ins, sources, out_refs, targets, scratch_refs = groups
        copies = [
            pltpu.make_async_copy(source, target, refs[-1].at[i])
            for i, (source, target) in enumerate(zip(sources, targets))
        ]
        for copy in copies:
            copy.start()
        kernel(ins, out_refs, scratch_refs)
        for copy in copies:
            copy.wait()

    sems = [pltpu.SemaphoreType.DMA((len(carried),))] if carried else []
    return pl.pallas_call(
        body,
        in_specs=[spec for _, spec in operands] + [HBM] * len(carried),
        out_specs=[VMEM] * (len(outs) + len(carried)),
        out_shape=[*outs, *[pltpu.VMEM(x.shape, x.dtype) for x in carried]],
        scratch_shapes=[*scratch, *sems],
        compiler_params=pltpu.CompilerParams(vmem_limit_bytes=mib * 1024 * 1024),
        cost_estimate=pl.CostEstimate(flops=1000, bytes_accessed=1000, transcendentals=0),
        name=name,
    )(
        *[x for x, _ in operands],
        *[pltpu.with_memory_space_constraint(x, pltpu.HBM) for x in carried],
    )


def in_vmem(arrays):
    return [(x, VMEM) for x in arrays]


def shaped(shape, dtype=jnp.float32):
    return jax.ShapeDtypeStruct(shape, dtype)


def after(x, *earlier):
    return lax.optimization_barrier((x, *earlier))[0]


def core_swap(x, pool_count):
    return lax.ppermute(x, "pool", [(p, p ^ 1) for p in range(pool_count)])


def chip_move(x, pool_count, d, e=0):
    chips = pool_count // 2
    return lax.ppermute(
        x,
        "pool",
        [(p, (p // 2 + d) % chips * 2 + ((p % 2) ^ e)) for p in range(pool_count)],
    )


def tp_swap(x, tp_count, step):
    return lax.ppermute(x, "tp", [(z, z ^ step) for z in range(tp_count)])


def shrink(first_id, ids, blocks, query_down, value_down):
    slots, _ = query_down.shape
    rows = blocks[0].shape[0]
    adapters = slots // 16
    count = len(blocks)

    def kernel(ins, outs, _):
        first_id, *ins = ins
        ids, blocks, tables = ins[:count], ins[count : 2 * count], ins[2 * count :]
        local_ids, out = outs
        for b in range(count):
            local_ids[:, b * rows : (b + 1) * rows] = ids[b][...] - first_id[0]
        for first in range(0, count, 2):
            x = jnp.concatenate([b[...] for b in blocks[first : first + 2]], axis=0)
            span = slice(first * rows, (first + 2) * rows)
            label = local_ids[:, span].reshape(1, 1, 2 * rows)
            chosen = lax.broadcasted_iota(jnp.int32, (adapters, 1, 2 * rows), 0) == label
            for at, table in enumerate(tables):
                terms = lax.dot_general(
                    table[...], x, (((1,), (1,)), ((), ())), preferred_element_type=jnp.float32
                ).reshape(adapters, 16, 2 * rows)
                out[at * 16 : (at + 1) * 16, span] = jnp.sum(
                    jnp.where(chosen, terms, 0.0), axis=0
                )

    return local_call(
        kernel,
        "shrink",
        [(first_id, SMEM), *in_vmem([*ids, *blocks, query_down, value_down])],
        [shaped((1, rows * count), jnp.int32), shaped((32, rows * count))],
    )


def tables(tokens, lengths, head):
    rows = tokens.shape[0]
    half = head // 2

    def kernel(ins, outs, _):
        tokens, lengths = ins
        scale, cosines, sines, column = outs
        values = tokens[...].astype(jnp.float32)
        mean_square = jnp.mean(values * values, axis=1, keepdims=True)
        scale[...] = lax.rsqrt(mean_square + epsilon)
        here = lax.broadcasted_iota(jnp.int32, (rows, rows), 0)
        there = lax.broadcasted_iota(jnp.int32, (rows, rows), 1)
        positions = jnp.sum(
            jnp.where(here == there, lengths[...].astype(jnp.float32), 0.0), axis=1, keepdims=True
        )
        column[...] = positions.astype(jnp.int32)
        lane = lax.broadcasted_iota(jnp.int32, (1, head), 1)
        exponent = (lane % half).astype(jnp.float32) * (-2.0 / head)
        angles = positions * jnp.exp(exponent * math.log(rope_base))
        cosines[...] = jnp.cos(angles)
        sines[...] = jnp.where(lane < half, -1.0, 1.0) * jnp.sin(angles)

    return local_call(
        kernel,
        "tables",
        in_vmem([tokens, lengths]),
        [
            shaped((rows, 1)),
            shaped((rows, head)),
            shaped((rows, head)),
            shaped((rows, 1), jnp.int32),
        ],
        mib=24,
    )


def load(arrays):
    def kernel(ins, outs, _):
        pass

    return local_call(kernel, "load", [], [], carried=arrays)


def spread_lows(low, ids, adapters):
    total = ids.shape[1]
    low = low.astype(jnp.bfloat16).astype(jnp.float32) * adapter_scale
    chosen = lax.broadcasted_iota(jnp.int32, (adapters, 1, total), 0) == ids.reshape(1, 1, total)
    return [
        jnp.where(chosen, low[at : at + 16][None], 0.0)
        .reshape(adapters * 16, total)
        .T.astype(jnp.bfloat16)
        for at in (0, 16)
    ]


def columns_at(start, width):
    return pl.ds(pl.multiple_of(start, width), width)


def project(name, kinds, span, ids, lows, blocks, weights, carried=()):
    wq, wk, wv, uq, uv = weights
    depth = blocks[0].shape[1]
    wide, kv, slots = wq.shape[1], wk.shape[1], uq.shape[0]
    tile = min(512, wide)
    start, total = span

    def kernel(ins, outs, scratch):
        ids, *ins = ins
        low_refs, blocks = ins[: len(lows)], ins[len(lows) : -5]
        wq, wk, wv, uq, uv = ins[-5:]
        xs, spread_q, spread_v = scratch
        at = 0
        for block in blocks:
            xs[at : at + block.shape[0], :] = block[...]
            at += block.shape[0]
        low = low_refs[0][:, start : start + total]
        for other in low_refs[1:]:
            low = low + other[:, start : start + total]
        spread_q[...], spread_v[...] = spread_lows(
            low, ids[:, start : start + total], slots // 16
        )

        def sums(w, spread=None, u=None):
            acc = jnp.dot(xs[...], w, preferred_element_type=jnp.float32)
            if u is not None:
                acc = acc + jnp.dot(spread[...], u, preferred_element_type=jnp.float32)
            return acc

        def write(acc, columns):
            for out, (first, count, dtype) in zip(outs, kinds):
                out[:, columns] = acc[first : first + count].astype(dtype)

        @pl.loop(0, wide // tile)
        def _(i):
            columns = columns_at(i * tile, tile)
            write(sums(wq[:, columns], spread_q, uq[:, columns]), columns)

        write(sums(wk[...]), slice(wide, wide + kv))
        write(sums(wv[...], spread_v, uv[...]), slice(wide + kv, wide + 2 * kv))

    spread = pltpu.VMEM((total, slots), jnp.bfloat16)
    return local_call(
        kernel,
        name,
        in_vmem([ids, *lows, *blocks, *weights]),
        [shaped((count, wide + 2 * kv), dtype) for _, count, dtype in kinds],
        [pltpu.VMEM((total, depth), jnp.bfloat16), spread, spread],
        carried=carried,
    )


def add_sums(name, window, keep, other):
    first, part = window

    def kernel(ins, outs, _):
        keep, other = ins
        outs[0][...] = (
            keep[first : first + part, :] + other[...].astype(jnp.float32)
        ).astype(jnp.bfloat16)

    return local_call(
        kernel, name, in_vmem([keep, other]), [shaped((part, keep.shape[1]), jnp.bfloat16)]
    )[0]


def attend_kernel(first_row, block, done, ins, outs, scratch):
    if done:
        for full, source in zip(outs[1:], ins[:2]):
            full[: source.shape[0], :] = source[...]
    keep, swapped, *moved, scale, cosines, sines, lengths, keys, values = ins[2:] if done else ins
    out, key_out, value_out = outs
    head = cosines.shape[1]
    rows = out.shape[0]
    _, kv_heads, cache, _ = keys.shape
    heads = out.shape[1] // head
    group = heads // kv_heads
    score_scale = 1.0 / math.sqrt(head)
    sub = 8

    column = lax.broadcasted_iota(jnp.int32, (sub, sub * cache), 1)
    start = lax.broadcasted_iota(jnp.int32, (sub, sub * cache), 0) * cache

    @pl.loop(0, rows // block)
    def _(i):
        attended, new_keys, new_values = [], [], []
        for half in range(block // sub):
            here = pl.ds(pl.multiple_of(i * block + half * sub, sub), sub)
            whole = pl.ds(pl.multiple_of(first_row + i * block + half * sub, sub), sub)
            x = keep[whole] + swapped[whole].astype(jnp.float32)
            for m in moved:
                x = x + m[here].astype(jnp.float32)
            x = x * scale[whole]
            cos, sin = cosines[whole], sines[whole]
            inside = (column >= start) & (column < start + lengths[whole])

            def piece(i):
                return x[:, i * head : (i + 1) * head]

            def turn(v):
                return v * cos + pltpu.roll(v, head // 2, 1) * sin

            for g in range(kv_heads):
                query = jnp.concatenate(
                    [turn(piece(g * group + h)) for h in range(group)], axis=0
                ).astype(jnp.bfloat16)
                new_key = turn(piece(heads + g)).astype(jnp.bfloat16).astype(jnp.float32)
                new_value = piece(heads + kv_heads + g).astype(jnp.bfloat16).astype(jnp.float32)
                k = keys[whole, g].reshape(sub * cache, head)
                v = values[whole, g].reshape(sub * cache, head)
                scores = (
                    lax.dot_general(
                        query, k, (((1,), (1,)), ((), ())), preferred_element_type=jnp.float32
                    )
                    * score_scale
                )
                own_key = jnp.concatenate([new_key] * group, axis=0)
                own = (
                    jnp.sum(query.astype(jnp.float32) * own_key, axis=1, keepdims=True)
                    * score_scale
                )
                scores = jnp.where(
                    inside[None], scores.reshape(group, sub, sub * cache), masked_score
                ).reshape(group * sub, sub * cache)
                peak = jnp.maximum(jnp.max(scores, axis=1, keepdims=True), own)
                weights = jnp.exp(scores - peak)
                own_weight = jnp.exp(own - peak)
                inverse = 1.0 / (jnp.sum(weights, axis=1, keepdims=True) + own_weight)
                mixed = jnp.dot(weights.astype(jnp.bfloat16), v, preferred_element_type=jnp.float32)
                own_value = jnp.concatenate([new_value] * group, axis=0)
                mixed = (mixed + own_weight * own_value) * inverse
                attended += [mixed[h * sub : (h + 1) * sub] for h in range(group)]
                new_keys.append(new_key)
                new_values.append(new_value)
        r = pl.ds(pl.multiple_of(i * block, block), block)

        def joined(pieces):
            n = len(pieces) * sub // block
            return jnp.concatenate(
                [jnp.concatenate(pieces[j::n], axis=0) for j in range(n)], axis=1
            ).astype(jnp.bfloat16)

        out[r] = joined(attended)
        r = pl.ds(pl.multiple_of((first_row if done else 0) + i * block, block), block)
        key_out[r] = joined(new_keys)
        value_out[r] = joined(new_values)


def attend(name, window, keep, swapped, moved, rest, keys, values, earlier, carried=()):
    _, columns = keep.shape
    _, kv_heads, _, head = keys.shape
    kv_cols = kv_heads * head
    first, part = window
    kv_rows = first + part if earlier else part
    return local_call(
        functools.partial(attend_kernel, first, 16, bool(earlier)),
        name,
        in_vmem([*earlier, keep, swapped, *moved, *rest, keys, values]),
        [
            shaped((part, columns - 2 * kv_cols), jnp.bfloat16),
            *[shaped((kv_rows, kv_cols), jnp.bfloat16)] * 2,
        ],
        carried=carried,
    )


def output_part(name, span, order, blocks, weights):
    rows = blocks[0].shape[0]
    first, columns = span
    depth = weights.shape[0]
    tile = math.gcd(512, columns)
    total = rows * len(blocks)

    def kernel(ins, outs, scratch):
        order, *blocks, weights = ins
        keep, send = outs
        (xs,) = scratch
        for b, block in enumerate(blocks):
            xs[pl.ds(pl.multiple_of(order[b] * rows, rows), rows), :] = block[...]

        @pl.loop(0, columns // tile)
        def _(i):
            w = weights[:, columns_at(first + i * tile, tile)]
            acc = jnp.dot(xs[...], w, preferred_element_type=jnp.float32).astype(jnp.bfloat16)
            keep[:, columns_at(i * tile, tile)] = acc[: total // 2]
            send[:, columns_at(i * tile, tile)] = acc[total // 2 :]

    return local_call(
        kernel,
        name,
        [(order, SMEM), *in_vmem([*blocks, weights])],
        [shaped((total // 2, columns), jnp.bfloat16)] * 2,
        [pltpu.VMEM((total, depth), jnp.bfloat16)],
    )


def add_halves(name, keep, got):
    half, columns = keep.shape[0] // 2, keep.shape[1]

    def kernel(ins, outs, _):
        keep, got = ins
        total = keep[...].astype(jnp.float32) + got[...].astype(jnp.float32)
        outs[0][...] = total[:half]
        outs[1][...] = total[half:].astype(jnp.bfloat16)

    return local_call(
        kernel,
        name,
        in_vmem([keep, got]),
        [shaped((half, columns)), shaped((half, columns), jnp.bfloat16)],
    )


def add_last(name, keep, got):
    def kernel(ins, outs, _):
        total = ins[0][...].astype(jnp.float32) + ins[1][...].astype(jnp.float32)
        outs[0][...] = total.astype(jnp.bfloat16)

    return local_call(kernel, name, in_vmem([keep, got]), [shaped(keep.shape, jnp.bfloat16)])[0]


def assemble(done, keep, got, places, rows, columns):
    def kernel(ins, outs, _):
        *done, keep, got = ins
        total = keep[...].astype(jnp.float32) + got[...].astype(jnp.float32)
        total = total.astype(jnp.bfloat16)
        for piece, spots in zip([*done, total], places):
            for at, to, count, column in spots:
                outs[0][to : to + count, column : column + piece.shape[1]] = piece[
                    at : at + count, :
                ]

    return local_call(
        kernel,
        "assemble",
        in_vmem([*done, keep, got]),
        [shaped((rows, columns), jnp.bfloat16)],
    )[0]


def reversed_bits(x, count):
    out, bit = 0, 1
    while bit < count:
        out = out * 2 + (x // bit) % 2
        bit *= 2
    return out


def shards(
    tokens,
    input_norm_gain,
    query_matrix,
    key_matrix,
    value_matrix,
    output_matrix,
    rotated_key_cache,
    cached_value_rows,
    cache_length_per_row,
    row_adapter_index,
    query_down_maps,
    query_up_maps,
    value_down_maps,
    value_up_maps,
):
    pool_count = lax.axis_size("pool")
    tp_count = lax.axis_size("tp")
    chips = pool_count // 2
    pool_at = lax.axis_index("pool")
    tp_at = lax.axis_index("tp")
    chip, core = pool_at // 2, pool_at % 2
    rows = tokens.shape[0]
    adapters, rank, piece = query_down_maps.shape
    base = query_matrix.shape[0]
    kv_heads = rotated_key_cache.shape[1]
    head = rotated_key_cache.shape[3]

    def scaled(start, width, tokens=tokens, gain=input_norm_gain, window=(0, rows)):
        x = lax.dynamic_slice(tokens, (window[0], start), (window[1], width)).astype(jnp.float32)
        factor = lax.dynamic_slice_in_dim(gain, start, width, 0).astype(jnp.float32)
        return (x * factor[None, :]).astype(jnp.bfloat16)

    own_ids = row_adapter_index.reshape(1, rows)
    ids = [
        own_ids if d == e == 0 else chip_move(own_ids, pool_count, d, e)
        for d in range(chips)
        for e in range(2)
    ]
    first = after(scaled(tp_at * piece, piece), *ids[1:])
    first, tokens_1, gain_1 = lax.optimization_barrier((first, tokens, input_norm_gain))
    same_core = [first] + [chip_move(first, pool_count, d) for d in range(1, chips)]

    cuts = [0, rows // 4, rows // 2, rows]
    chunks = [(start, stop - start) for start, stop in zip(cuts, cuts[1:])]
    own = scaled(pool_at * base, base, tokens_1, gain_1)
    partner_at = (pool_at // 2 * 2 + 1 - core) * base
    partner = [
        scaled(partner_at, base, tokens_1, gain_1, (at, rows // 2)) for at in (0, rows // 2)
    ]
    away = {}
    for d in range(1, chips):
        for e in range(2):
            target = (chip + d) % chips * 2 + (core + e) % 2
            away[d, e] = scaled(target * base, base, tokens_1, gain_1)
    first_id = (pool_at * adapters).reshape(1).astype(jnp.int32)
    lengths = cache_length_per_row.reshape(1, rows)
    share = pool_count // tp_count
    order = []
    for d in range(chips):
        for e in range(2):
            p = (chip - d) % chips * 2 + (core + e) % 2
            order.append(
                reversed_bits(jnp.bitwise_xor(p // share, tp_at), tp_count) * share + p % share
            )
    order = jnp.stack(order).astype(jnp.int32)

    flat_down = [x.reshape(adapters * rank, piece) for x in (query_down_maps, value_down_maps)]
    flat_up = [x.reshape(adapters * rank, x.shape[2]) for x in (query_up_maps, value_up_maps)]
    small = [own, *partner, *away.values(), first_id, lengths, order]
    query_matrix, *small = lax.optimization_barrier((query_matrix, *small))
    own, partner, small = small[0], small[1:3], small[3:]
    away = dict(zip(away, small))
    first_id, lengths, order = small[-3:]
    down_q, down_v, *weights = load(
        [*flat_down, query_matrix, key_matrix, value_matrix, *flat_up]
    )
    partner = [core_swap(x, pool_count) for x in partner]
    remote = [[] for _ in range(chips)]
    for (d, e), x in away.items():
        remote[d].append(chip_move(after(x, *same_core[1:]), pool_count, d, e))
    same_core[1:] = [after(x, down_q) for x in same_core[1:]]
    adapter_rows = [b for x in same_core for b in (x, core_swap(x, pool_count))]
    local_ids, shrunk = shrink(first_id, ids, adapter_rows, down_q, down_v)
    lows = [shrunk] + [
        lax.ppermute(shrunk, "tp", [(i, (i + d) % tp_count) for i in range(tp_count)])
        for d in range(1, tp_count)
    ]
    rest = tables(tokens, after(lengths, shrunk), head)
    own_sums, own_send, keys, values = project(
        "project_own",
        [(0, rows, jnp.float32), (rows, rows, jnp.bfloat16)],
        (0, 2 * rows),
        after(local_ids, rest[0]),
        lows,
        [own, *partner],
        weights,
        carried=[rotated_key_cache, cached_value_rows],
    )
    swapped = core_swap(own_send, pool_count)
    local_ids = after(local_ids, own_sums)
    partial, send = [], None
    for d in range(1, chips):
        if partial:
            remote[d][0] = after(remote[d][0], sends[0])
        at = 2 * d * rows
        (keep,) = project(
            f"project_{d}_0",
            [(0, rows, jnp.float32)],
            (at, rows),
            local_ids,
            lows,
            remote[d][:1],
            weights,
        )
        sends = project(
            f"project_{d}_1",
            [(first, part, jnp.bfloat16) for first, part in chunks],
            (at + rows, rows),
            local_ids,
            lows,
            [after(remote[d][1], keep)],
            weights,
        )
        partial.append((d, keep, sends))

    def reduced(c, *earlier):
        arrived = []
        for d, keep, sends in partial:
            swap = after(core_swap(sends[c], pool_count), *earlier)
            both = add_sums(f"add_{d}_{c}", chunks[c], keep, swap)
            arrived.append(chip_move(both, pool_count, -d))
            earlier = [both]
        return arrived, both

    moved = [None] * len(chunks)
    moved[0], both = reduced(0)
    moved[1], both = reduced(1, both)
    moved[0][0] = after(moved[0][0], both)

    columns = output_matrix.shape[1]
    layout = [(0, 0, 1), (1, 0, 1), (2, 0, 2), (2, 2, 4), (2, 3, 4)]
    attended, gathered, keeps, sends, products = [], {}, [], [], []

    def multiply(*earlier):
        c, at, count = layout[len(keeps)]
        if c not in gathered:
            parts = [after(x, *earlier) for x in attended[c]]
            gathered[c] = [b for x in parts for b in (x, core_swap(x, pool_count))]
        else:
            gathered[c][0] = after(gathered[c][0], products[-1])
        width = columns // count
        keep, send = output_part(
            f"output_{c}_{at}_{count}", (at * width, width), order, gathered[c], out_weights
        )
        keeps.append(keep)
        sends.append(send)
        products.append(keep)

    earlier = []
    for c, window in enumerate(chunks):
        if c == 2:
            multiply(earlier[0], both)
            moved[c][0] = after(moved[c][0], products[-1])
        out, *earlier = attend(
            f"attend_{c}",
            window,
            own_sums,
            swapped,
            moved[c],
            rest,
            keys,
            values,
            earlier[:2],
            [] if c else [output_matrix],
        )
        if c == 0:
            out_weights = earlier[2]
            out, *moved[1] = lax.optimization_barrier((out, *moved[1]))
        else:
            out = after(out, attended[-1][-1])
        attended.append([out] + [chip_move(out, pool_count, d) for d in range(1, chips)])
        if c + 2 < len(chunks):
            moved[c + 2], both = reduced(c + 2, attended[c][0])
    new_key, new_value = earlier

    stages = reversed_bits(1, tp_count).bit_length()
    last = len(layout) - 1
    total, got, done, places = None, {}, [], []
    for i, (c, at, count) in enumerate(layout):
        start, part = chunks[c]
        column = at * columns // count
        places.append([(r * part, r * rows + start, part, column) for r in range(share)])
    for slot in range(last + stages):
        while len(keeps) < min(slot + 2 if slot > 1 else slot + 1, last + 1):
            multiply(products[-1], new_key, total)
        for stage in reversed(range(stages)) if slot == 1 else range(stages):
            i = slot - stage
            if not 0 <= i <= last:
                continue
            if stage == 0:
                got[i] = tp_swap(sends[i], tp_count, 1)
            past = [products[-1]] + ([] if total is None else [total])
            came = after(got[i], *past)
            if stage + 1 < stages:
                keeps[i], total = add_halves(f"halves_{i}_{stage}", keeps[i], came)
                got[i] = tp_swap(total, tp_count, 2 << stage)
            elif i < last:
                total = add_last(f"last_{i}", keeps[i], came)
                done.append(total)
            else:
                attn_out = assemble(done, keeps[i], came, places, share * rows, columns)
    return attn_out, new_key, new_value


def solution(mesh):
    return jax.shard_map(
        shards,
        mesh=mesh,
        in_specs=(
            P(("groups", "pool"), None),
            P(),
            P("pool", "tp"),
            P("pool", "tp"),
            P("pool", "tp"),
            P("tp", "pool"),
            P(("groups", "pool"), "tp", None, None),
            P(("groups", "pool"), "tp", None, None),
            P(("groups", "pool")),
            P(("groups", "pool")),
            P("pool", None, "tp"),
            P("pool", None, "tp"),
            P("pool", None, "tp"),
            P("pool", None, "tp"),
        ),
        out_specs=(
            P(("groups", "tp"), "pool"),
            P(("groups", "pool"), "tp"),
            P(("groups", "pool"), "tp"),
        ),
        check_vma=False,
    )
```

```python
import functools
import math

import jax
import jax.numpy as jnp
from jax import lax
from jax.experimental import pallas as pl
from jax.experimental.pallas import tpu as pltpu
from jax.sharding import PartitionSpec as P

epsilon = 1e-05
adapter_scale = 0.5
rope_base = 500000.0
masked_score = -1e30


VMEM = pl.BlockSpec(memory_space=pltpu.VMEM)
HBM = pl.BlockSpec(memory_space=pltpu.HBM)
SMEM = pl.BlockSpec(memory_space=pltpu.SMEM)


def local_call(kernel, name, operands, outs, scratch=(), carried=(), mib=16):
    counts = (len(operands), len(carried), len(outs), len(carried), len(scratch))

    def body(*refs):
        groups, at = [], 0
        for n in counts:
            groups.append(refs[at : at + n])
            at += n
        ins, sources, out_refs, targets, scratch_refs = groups
        copies = [
            pltpu.make_async_copy(source, target, refs[-1].at[i])
            for i, (source, target) in enumerate(zip(sources, targets))
        ]
        for copy in copies:
            copy.start()
        kernel(ins, out_refs, scratch_refs)
        for copy in copies:
            copy.wait()

    sems = [pltpu.SemaphoreType.DMA((len(carried),))] if carried else []
    return pl.pallas_call(
        body,
        in_specs=[spec for _, spec in operands] + [HBM] * len(carried),
        out_specs=[VMEM] * (len(outs) + len(carried)),
        out_shape=[*outs, *[pltpu.VMEM(x.shape, x.dtype) for x in carried]],
        scratch_shapes=[*scratch, *sems],
        compiler_params=pltpu.CompilerParams(vmem_limit_bytes=mib * 1024 * 1024),
        cost_estimate=pl.CostEstimate(flops=1000, bytes_accessed=1000, transcendentals=0),
        name=name,
    )(
        *[x for x, _ in operands],
        *[pltpu.with_memory_space_constraint(x, pltpu.HBM) for x in carried],
    )


def in_vmem(arrays):
    return [(x, VMEM) for x in arrays]


def shaped(shape, dtype=jnp.float32):
    return jax.ShapeDtypeStruct(shape, dtype)


def after(x, *earlier):
    return lax.optimization_barrier((x, *earlier))[0]


def core_swap(x, pool_count):
    return lax.ppermute(x, "pool", [(p, p ^ 1) for p in range(pool_count)])


def chip_move(x, pool_count, d, e=0):
    chips = pool_count // 2
    return lax.ppermute(
        x,
        "pool",
        [(p, (p // 2 + d) % chips * 2 + ((p % 2) ^ e)) for p in range(pool_count)],
    )


def tp_swap(x, tp_count, step):
    return lax.ppermute(x, "tp", [(z, z ^ step) for z in range(tp_count)])


def scaled_slices(name, starts, tokens, gain, width, wanted):
    rows = tokens.shape[0]
    count = starts.shape[0]

    def kernel(ins, outs, scratch):
        starts, gain, tokens = ins
        held, sems = scratch

        def copy(i):
            columns = pl.ds(pl.multiple_of(starts[i], 128), width)
            return pltpu.make_async_copy(tokens.at[:, columns], held.at[i], sems.at[i])

        for i in range(count):
            copy(i).start()
        for i in range(count):
            copy(i).wait()
            columns = pl.ds(pl.multiple_of(starts[i], 128), width)
            factor = gain[:, columns].astype(jnp.float32)
            for out, (which, first, part) in zip(outs, wanted):
                if which == i:
                    values = held[i, first : first + part].astype(jnp.float32)
                    out[...] = (values * factor).astype(jnp.bfloat16)

    tokens = pltpu.with_memory_space_constraint(tokens, pltpu.HBM)
    return local_call(
        kernel,
        name,
        [(starts, SMEM), (gain, VMEM), (tokens, HBM)],
        [shaped((part, width), jnp.bfloat16) for _, _, part in wanted],
        [
            pltpu.VMEM((count, rows, width), jnp.bfloat16),
            pltpu.SemaphoreType.DMA((count,)),
        ],
    )


def shrink(first_id, at, ids, blocks, query_down, value_down, width, tail):
    slots, _ = query_down.shape
    rows = blocks[0].shape[0]
    adapters = slots // 16
    count = len(blocks)

    def kernel(ins, outs, _):
        first_id, at, *ins = ins
        ids, blocks, tables = ins[:count], ins[count : 2 * count], ins[2 * count :]
        local_ids, out, *tails = outs
        for b, tail_out in enumerate(tails):
            columns = pl.ds(pl.multiple_of(at[0], 128), width)
            tail_out[...] = blocks[2 * b + 3][rows - tail :, columns]
        for b in range(count):
            local_ids[:, b * rows : (b + 1) * rows] = ids[b][...] - first_id[0]
        for first in range(0, count, 2):
            x = jnp.concatenate([b[...] for b in blocks[first : first + 2]], axis=0)
            span = slice(first * rows, (first + 2) * rows)
            label = local_ids[:, span].reshape(1, 1, 2 * rows)
            chosen = lax.broadcasted_iota(jnp.int32, (adapters, 1, 2 * rows), 0) == label
            for at, table in enumerate(tables):
                terms = lax.dot_general(
                    table[...], x, (((1,), (1,)), ((), ())), preferred_element_type=jnp.float32
                ).reshape(adapters, 16, 2 * rows)
                out[at * 16 : (at + 1) * 16, span] = jnp.sum(
                    jnp.where(chosen, terms, 0.0), axis=0
                )

    return local_call(
        kernel,
        "shrink",
        [(first_id, SMEM), (at, SMEM), *in_vmem([*ids, *blocks, query_down, value_down])],
        [
            shaped((1, rows * count), jnp.int32),
            shaped((32, rows * count)),
            *[shaped((tail, width), jnp.bfloat16)] * (count // 2 - 1),
        ],
    )


def tables(tokens, lengths, head):
    rows = tokens.shape[0]
    half = head // 2

    def kernel(ins, outs, _):
        tokens, lengths = ins
        scale, cosines, sines, column = outs
        values = tokens[...].astype(jnp.float32)
        mean_square = jnp.mean(values * values, axis=1, keepdims=True)
        scale[...] = lax.rsqrt(mean_square + epsilon)
        here = lax.broadcasted_iota(jnp.int32, (rows, rows), 0)
        there = lax.broadcasted_iota(jnp.int32, (rows, rows), 1)
        positions = jnp.sum(
            jnp.where(here == there, lengths[...].astype(jnp.float32), 0.0), axis=1, keepdims=True
        )
        column[...] = positions.astype(jnp.int32)
        lane = lax.broadcasted_iota(jnp.int32, (1, head), 1)
        exponent = (lane % half).astype(jnp.float32) * (-2.0 / head)
        angles = positions * jnp.exp(exponent * math.log(rope_base))
        cosines[...] = jnp.cos(angles)
        sines[...] = jnp.where(lane < half, -1.0, 1.0) * jnp.sin(angles)

    return local_call(
        kernel,
        "tables",
        in_vmem([tokens, lengths]),
        [
            shaped((rows, 1)),
            shaped((rows, head)),
            shaped((rows, head)),
            shaped((rows, 1), jnp.int32),
        ],
        mib=24,
    )


def load(arrays):
    def kernel(ins, outs, _):
        pass

    return local_call(kernel, "load", [], [], carried=arrays)


def spread_lows(low, ids, adapters):
    total = ids.shape[1]
    low = low.astype(jnp.bfloat16).astype(jnp.float32) * adapter_scale
    chosen = lax.broadcasted_iota(jnp.int32, (adapters, 1, total), 0) == ids.reshape(1, 1, total)
    return [
        jnp.where(chosen, low[at : at + 16][None], 0.0)
        .reshape(adapters * 16, total)
        .T.astype(jnp.bfloat16)
        for at in (0, 16)
    ]


def columns_at(start, width):
    return pl.ds(pl.multiple_of(start, width), width)


def project(name, kinds, span, ids, lows, blocks, weights, which=None, options=()):
    wq, wk, wv, uq, uv = weights
    depth = blocks[0].shape[1]
    wide, kv, slots = wq.shape[1], wk.shape[1], uq.shape[0]
    tile = min(512, wide)
    start, total = span

    def kernel(ins, outs, scratch):
        if options:
            which, *ins = ins
        ids, *ins = ins
        wq, wk, wv, uq, uv = ins[-5:]
        low_refs, ins = ins[: len(lows)], ins[len(lows) : -5]
        blocks, choices = ins[: len(ins) - len(options)], ins[len(ins) - len(options) :]
        xs, spread_q, spread_v = scratch
        at = 0
        for block in blocks:
            xs[at : at + block.shape[0], :] = block[...]
            at += block.shape[0]
        for j, choice in enumerate(choices):

            @pl.when(which[0] == j)
            def _():
                xs[at:, :] = choice[...]

        low = low_refs[0][:, start : start + total]
        for other in low_refs[1:]:
            low = low + other[:, start : start + total]
        spread_q[...], spread_v[...] = spread_lows(
            low, ids[:, start : start + total], slots // 16
        )

        def sums(w, spread=None, u=None):
            acc = jnp.dot(xs[...], w, preferred_element_type=jnp.float32)
            if u is not None:
                acc = acc + jnp.dot(spread[...], u, preferred_element_type=jnp.float32)
            return acc

        def write(acc, columns):
            for out, (first, count, dtype) in zip(outs, kinds):
                out[:, columns] = acc[first : first + count].astype(dtype)

        @pl.loop(0, wide // tile)
        def _(i):
            columns = columns_at(i * tile, tile)
            write(sums(wq[:, columns], spread_q, uq[:, columns]), columns)

        write(sums(wk[...]), slice(wide, wide + kv))
        write(sums(wv[...], spread_v, uv[...]), slice(wide + kv, wide + 2 * kv))

    spread = pltpu.VMEM((total, slots), jnp.bfloat16)
    return local_call(
        kernel,
        name,
        [(which, SMEM)] * bool(options)
        + in_vmem([ids, *lows, *blocks, *options, *weights]),
        [shaped((count, wide + 2 * kv), dtype) for _, count, dtype in kinds],
        [pltpu.VMEM((total, depth), jnp.bfloat16), spread, spread],
    )


def project_base(blocks, weights, carried):
    rows, depth = blocks[0].shape
    wide, kv = weights[0].shape[1], weights[1].shape[1]
    tile = min(512, wide)

    def kernel(ins, outs, scratch):
        *blocks, wq, wk, wv = ins
        (xs,) = scratch
        at = 0
        for block in blocks:
            xs[at : at + block.shape[0], :] = block[...]
            at += block.shape[0]

        def write(w, columns):
            acc = jnp.dot(xs[...], w, preferred_element_type=jnp.float32)
            outs[0][:, columns] = acc[:rows]
            outs[1][:, columns] = acc[rows:]

        @pl.loop(0, wide // tile)
        def _(i):
            columns = columns_at(i * tile, tile)
            write(wq[:, columns], columns)

        write(wk[...], slice(wide, wide + kv))
        write(wv[...], slice(wide + kv, wide + 2 * kv))

    return local_call(
        kernel,
        "project_base",
        in_vmem([*blocks, *weights]),
        [shaped((rows, wide + 2 * kv))] * 2,
        [pltpu.VMEM((2 * rows, depth), jnp.bfloat16)],
        carried=carried,
    )


def add_adapters(keep, send, ids, lows, uq, uv):
    rows = keep.shape[0]
    wide, kv, slots = uq.shape[1], uv.shape[1], uq.shape[0]
    tile = min(512, wide)

    def kernel(ins, outs, scratch):
        ids, *ins = ins
        low_refs, (keep0, send0, uq, uv) = ins[: len(lows)], ins[len(lows) :]
        keep, send = outs
        spread_q, spread_v = scratch
        low = low_refs[0][:, : 2 * rows]
        for other in low_refs[1:]:
            low = low + other[:, : 2 * rows]
        spread_q[...], spread_v[...] = spread_lows(low, ids[:, : 2 * rows], slots // 16)

        def write(extra, columns):
            keep[:, columns] = keep0[:, columns] + extra[:rows]
            send[:, columns] = (send0[:, columns] + extra[rows:]).astype(send.dtype)

        @pl.loop(0, wide // tile)
        def _(i):
            columns = columns_at(i * tile, tile)
            write(
                jnp.dot(spread_q[...], uq[:, columns], preferred_element_type=jnp.float32),
                columns,
            )

        keep[:, wide : wide + kv] = keep0[:, wide : wide + kv]
        send[:, wide : wide + kv] = send0[:, wide : wide + kv].astype(send.dtype)
        write(
            jnp.dot(spread_v[...], uv[...], preferred_element_type=jnp.float32),
            slice(wide + kv, wide + 2 * kv),
        )

    spread = pltpu.VMEM((2 * rows, slots), jnp.bfloat16)
    return local_call(
        kernel,
        "add_adapters",
        in_vmem([ids, *lows, keep, send, uq, uv]),
        [shaped(keep.shape), shaped(keep.shape, jnp.bfloat16)],
        [spread, spread],
    )


def add_sums(name, window, keep, other):
    first, part = window

    def kernel(ins, outs, _):
        keep, other = ins
        outs[0][...] = (
            keep[first : first + part, :] + other[...].astype(jnp.float32)
        ).astype(jnp.bfloat16)

    return local_call(
        kernel, name, in_vmem([keep, other]), [shaped((part, keep.shape[1]), jnp.bfloat16)]
    )[0]


def attend_kernel(first_row, block, done, ins, outs, scratch):
    if done:
        for full, source in zip(outs[1:], ins[:2]):
            full[: source.shape[0], :] = source[...]
    keep, swapped, *moved, scale, cosines, sines, lengths, keys, values = ins[2:] if done else ins
    out, key_out, value_out = outs
    head = cosines.shape[1]
    rows = out.shape[0]
    _, kv_heads, cache, _ = keys.shape
    heads = out.shape[1] // head
    group = heads // kv_heads
    score_scale = 1.0 / math.sqrt(head)
    sub = 8

    column = lax.broadcasted_iota(jnp.int32, (sub, sub * cache), 1)
    start = lax.broadcasted_iota(jnp.int32, (sub, sub * cache), 0) * cache

    @pl.loop(0, rows // block)
    def _(i):
        attended, new_keys, new_values = [], [], []
        for half in range(block // sub):
            here = pl.ds(pl.multiple_of(i * block + half * sub, sub), sub)
            whole = pl.ds(pl.multiple_of(first_row + i * block + half * sub, sub), sub)
            x = keep[whole] + swapped[whole].astype(jnp.float32)
            for m in moved:
                x = x + m[here].astype(jnp.float32)
            x = x * scale[whole]
            cos, sin = cosines[whole], sines[whole]
            inside = (column >= start) & (column < start + lengths[whole])

            def piece(i):
                return x[:, i * head : (i + 1) * head]

            def turn(v):
                return v * cos + pltpu.roll(v, head // 2, 1) * sin

            for g in range(kv_heads):
                query = jnp.concatenate(
                    [turn(piece(g * group + h)) for h in range(group)], axis=0
                ).astype(jnp.bfloat16)
                new_key = turn(piece(heads + g)).astype(jnp.bfloat16).astype(jnp.float32)
                new_value = piece(heads + kv_heads + g).astype(jnp.bfloat16).astype(jnp.float32)
                k = keys[whole, g].reshape(sub * cache, head)
                v = values[whole, g].reshape(sub * cache, head)
                scores = (
                    lax.dot_general(
                        query, k, (((1,), (1,)), ((), ())), preferred_element_type=jnp.float32
                    )
                    * score_scale
                )
                own_key = jnp.concatenate([new_key] * group, axis=0)
                own = (
                    jnp.sum(query.astype(jnp.float32) * own_key, axis=1, keepdims=True)
                    * score_scale
                )
                scores = jnp.where(
                    inside[None], scores.reshape(group, sub, sub * cache), masked_score
                ).reshape(group * sub, sub * cache)
                peak = jnp.maximum(jnp.max(scores, axis=1, keepdims=True), own)
                weights = jnp.exp(scores - peak)
                own_weight = jnp.exp(own - peak)
                inverse = 1.0 / (jnp.sum(weights, axis=1, keepdims=True) + own_weight)
                mixed = jnp.dot(weights.astype(jnp.bfloat16), v, preferred_element_type=jnp.float32)
                own_value = jnp.concatenate([new_value] * group, axis=0)
                mixed = (mixed + own_weight * own_value) * inverse
                attended += [mixed[h * sub : (h + 1) * sub] for h in range(group)]
                new_keys.append(new_key)
                new_values.append(new_value)
        r = pl.ds(pl.multiple_of(i * block, block), block)

        def joined(pieces):
            n = len(pieces) * sub // block
            return jnp.concatenate(
                [jnp.concatenate(pieces[j::n], axis=0) for j in range(n)], axis=1
            ).astype(jnp.bfloat16)

        out[r] = joined(attended)
        r = pl.ds(pl.multiple_of((first_row if done else 0) + i * block, block), block)
        key_out[r] = joined(new_keys)
        value_out[r] = joined(new_values)


def attend(name, window, keep, swapped, moved, rest, keys, values, earlier, carried=()):
    _, columns = keep.shape
    _, kv_heads, _, head = keys.shape
    kv_cols = kv_heads * head
    first, part = window
    kv_rows = first + part if earlier else part
    return local_call(
        functools.partial(attend_kernel, first, 16, bool(earlier)),
        name,
        in_vmem([*earlier, keep, swapped, *moved, *rest, keys, values]),
        [
            shaped((part, columns - 2 * kv_cols), jnp.bfloat16),
            *[shaped((kv_rows, kv_cols), jnp.bfloat16)] * 2,
        ],
        carried=carried,
    )


def output_part(name, span, order, blocks, weights):
    rows = blocks[0].shape[0]
    first, columns = span
    depth = weights.shape[0]
    tile = math.gcd(512, columns)
    total = rows * len(blocks)

    def kernel(ins, outs, scratch):
        order, *blocks, weights = ins
        keep, send = outs
        (xs,) = scratch
        for b, block in enumerate(blocks):
            xs[pl.ds(pl.multiple_of(order[b] * rows, rows), rows), :] = block[...]

        @pl.loop(0, columns // tile)
        def _(i):
            w = weights[:, columns_at(first + i * tile, tile)]
            acc = jnp.dot(xs[...], w, preferred_element_type=jnp.float32).astype(jnp.bfloat16)
            keep[:, columns_at(i * tile, tile)] = acc[: total // 2]
            send[:, columns_at(i * tile, tile)] = acc[total // 2 :]

    return local_call(
        kernel,
        name,
        [(order, SMEM), *in_vmem([*blocks, weights])],
        [shaped((total // 2, columns), jnp.bfloat16)] * 2,
        [pltpu.VMEM((total, depth), jnp.bfloat16)],
    )


def add_halves(name, keep, got):
    half, columns = keep.shape[0] // 2, keep.shape[1]

    def kernel(ins, outs, _):
        keep, got = ins
        total = keep[...].astype(jnp.float32) + got[...].astype(jnp.float32)
        outs[0][...] = total[:half]
        outs[1][...] = total[half:].astype(jnp.bfloat16)

    return local_call(
        kernel,
        name,
        in_vmem([keep, got]),
        [shaped((half, columns)), shaped((half, columns), jnp.bfloat16)],
    )


def add_last(name, keep, got):
    def kernel(ins, outs, _):
        total = ins[0][...].astype(jnp.float32) + ins[1][...].astype(jnp.float32)
        outs[0][...] = total.astype(jnp.bfloat16)

    return local_call(kernel, name, in_vmem([keep, got]), [shaped(keep.shape, jnp.bfloat16)])[0]


def assemble(done, keep, got, places, rows, columns):
    def kernel(ins, outs, _):
        *done, keep, got = ins
        total = keep[...].astype(jnp.float32) + got[...].astype(jnp.float32)
        total = total.astype(jnp.bfloat16)
        for piece, spots in zip([*done, total], places):
            for at, to, count, column in spots:
                outs[0][to : to + count, column : column + piece.shape[1]] = piece[
                    at : at + count, :
                ]

    return local_call(
        kernel,
        "assemble",
        in_vmem([*done, keep, got]),
        [shaped((rows, columns), jnp.bfloat16)],
    )[0]


def reversed_bits(x, count):
    out, bit = 0, 1
    while bit < count:
        out = out * 2 + (x // bit) % 2
        bit *= 2
    return out


def shards(
    tokens,
    input_norm_gain,
    query_matrix,
    key_matrix,
    value_matrix,
    output_matrix,
    rotated_key_cache,
    cached_value_rows,
    cache_length_per_row,
    row_adapter_index,
    query_down_maps,
    query_up_maps,
    value_down_maps,
    value_up_maps,
):
    pool_count = lax.axis_size("pool")
    tp_count = lax.axis_size("tp")
    chips = pool_count // 2
    pool_at = lax.axis_index("pool")
    tp_at = lax.axis_index("tp")
    chip, core = pool_at // 2, pool_at % 2
    rows = tokens.shape[0]
    adapters, rank, piece = query_down_maps.shape
    base = query_matrix.shape[0]
    kv_heads = rotated_key_cache.shape[1]
    head = rotated_key_cache.shape[3]

    own_ids = row_adapter_index.reshape(1, rows)
    ids = [
        own_ids if d == e == 0 else chip_move(own_ids, pool_count, d, e)
        for d in range(chips)
        for e in range(2)
    ]
    gain = input_norm_gain.reshape(1, -1)
    (first,) = scaled_slices(
        "slice_tp", (tp_at * piece).reshape(1), tokens, gain, piece, [(0, 0, rows)]
    )
    first = after(first, *ids[1:])
    first, gain_1 = lax.optimization_barrier((first, gain))
    same_core = [first] + [chip_move(first, pool_count, d) for d in range(1, chips)]

    cut = rows // 2
    chunks = [(0, cut), (cut, rows - cut)]
    tail = rows * 3 // 8
    starts = [pool_at * base, (pool_at // 2 * 2 + 1 - core) * base]
    wanted = [(0, 0, rows), (1, 0, rows // 2), (1, rows // 2, rows // 2)]
    places = [(d, e) for d in range(1, chips) for e in range(2)]
    for i, (d, e) in enumerate(places):
        starts.append(((chip + d) % chips * 2 + (core + e) % 2) * base)
        wanted.append((2 + i, 0, rows - tail if e else rows))
    own, *slices = scaled_slices(
        "slice_pool", jnp.stack(starts).astype(jnp.int32), tokens, gain_1, base, wanted
    )
    partner, away = slices[:2], dict(zip(places, slices[2:]))
    first_id = (pool_at * adapters).reshape(1).astype(jnp.int32)
    at_piece = (pool_at * base % piece).reshape(1).astype(jnp.int32)
    which = ((tp_at - pool_at * base // piece) % tp_count).reshape(1).astype(jnp.int32)
    lengths = cache_length_per_row.reshape(1, rows)
    share = pool_count // tp_count
    order = []
    for d in range(chips):
        for e in range(2):
            p = (chip - d) % chips * 2 + (core + e) % 2
            order.append(
                reversed_bits(jnp.bitwise_xor(p // share, tp_at), tp_count) * share + p % share
            )
    order = jnp.stack(order).astype(jnp.int32)

    flat_down = [x.reshape(adapters * rank, piece) for x in (query_down_maps, value_down_maps)]
    flat_up = [x.reshape(adapters * rank, x.shape[2]) for x in (query_up_maps, value_up_maps)]
    small = [own, first_id, at_piece, which, lengths, order]
    query_matrix, *small = lax.optimization_barrier((query_matrix, *small))
    own, first_id, at_piece, which, lengths, order = small
    down_q, down_v, *weights = load(
        [*flat_down, query_matrix, key_matrix, value_matrix, *flat_up]
    )
    partner = [core_swap(x, pool_count) for x in partner]
    own_keep, own_send, keys, values = project_base(
        [own, *partner], weights[:3], [rotated_key_cache, cached_value_rows]
    )
    remote = [[] for _ in range(chips)]
    for (d, e), x in away.items():
        remote[d].append(chip_move(after(x, *same_core[1:]), pool_count, d, e))
    same_core[1:] = [after(x, own_keep) for x in same_core[1:]]
    adapter_rows = [b for x in same_core for b in (x, core_swap(x, pool_count))]
    local_ids, shrunk, *tails = shrink(
        first_id, at_piece, ids, adapter_rows, down_q, down_v, base, tail
    )
    lows = [shrunk] + [
        lax.ppermute(shrunk, "tp", [(i, (i + d) % tp_count) for i in range(tp_count)])
        for d in range(1, tp_count)
    ]
    rest = tables(tokens, after(lengths, shrunk), head)

    def along_tp(x, k):
        pairs = []
        for p in range(pool_count):
            z = p * base // piece
            pairs.append((p * tp_count + z, p * tp_count + (z + k) % tp_count))
        return lax.ppermute(x, ("pool", "tp"), pairs)

    tails = [after(x, rest[0]) for x in tails]
    tails = [[x] + [along_tp(x, k) for k in range(1, tp_count)] for x in tails]
    own_sums, own_send = add_adapters(
        own_keep, own_send, after(local_ids, rest[0]), lows, *weights[3:]
    )
    swapped = core_swap(own_send, pool_count)
    local_ids = after(local_ids, own_sums)
    moved = [[] for _ in chunks]
    both = None
    for d in range(1, chips):
        if both is not None:
            remote[d][0] = after(remote[d][0], both)
        at = 2 * d * rows
        (keep,) = project(
            f"project_{d}_0",
            [(0, rows, jnp.float32)],
            (at, rows),
            local_ids,
            lows,
            remote[d][:1],
            weights,
        )
        sends = project(
            f"project_{d}_1",
            [(first, part, jnp.bfloat16) for first, part in chunks],
            (at + rows, rows),
            local_ids,
            lows,
            [after(remote[d][1], keep)],
            weights,
            which,
            tails[d - 1],
        )
        for c, window in enumerate(chunks):
            swap = core_swap(sends[c], pool_count)
            if c:
                swap = after(swap, both)
            both = add_sums(f"add_{d}_{c}", window, keep, swap)
            moved[c].append(chip_move(both, pool_count, -d))
    moved[0][0] = after(moved[0][0], both)

    attended, earlier = [], []
    for c, window in enumerate(chunks):
        out, *earlier = attend(
            f"attend_{c}",
            window,
            own_sums,
            swapped,
            moved[c],
            rest,
            keys,
            values,
            earlier[:2],
            [] if c else [output_matrix],
        )
        if c == 0:
            out_weights = earlier[2]
        if c + 1 < len(chunks):
            out, *moved[c + 1] = lax.optimization_barrier((out, *moved[c + 1]))
        else:
            out = after(out, attended[-1][-1])
        attended.append([out] + [chip_move(out, pool_count, d) for d in range(1, chips)])
    new_key, new_value = earlier
    attended[0][0] = after(attended[0][0], new_key)

    columns = output_matrix.shape[1]
    layout = [(0, 0, 1), (1, 0, 2), (1, 2, 4), (1, 3, 4)]
    gathered, keeps, sends, products = {}, [], [], []

    def multiply():
        c, at, count = layout[len(keeps)]
        if c not in gathered:
            parts = [after(x, products[-1]) for x in attended[c]] if c else attended[c]
            gathered[c] = [b for x in parts for b in (x, core_swap(x, pool_count))]
        else:
            gathered[c][0] = after(gathered[c][0], products[-1])
        width = columns // count
        keep, send = output_part(
            f"output_{c}_{at}_{count}", (at * width, width), order, gathered[c], out_weights
        )
        keeps.append(keep)
        sends.append(send)
        products.append(keep)

    stages = reversed_bits(1, tp_count).bit_length()
    last = len(layout) - 1
    total, got, done, places = None, {}, [], []
    for i, (c, at, count) in enumerate(layout):
        start, part = chunks[c]
        column = at * columns // count
        places.append([(r * part, r * rows + start, part, column) for r in range(share)])
    for slot in range(last + stages):
        while len(keeps) < min(slot + 2, last + 1):
            multiply()
        for stage in range(stages):
            i = slot - stage
            if not 0 <= i <= last:
                continue
            if stage == 0:
                got[i] = tp_swap(sends[i], tp_count, 1)
            past = [products[-1]] + ([] if total is None else [total])
            came = after(got[i], *past)
            if stage + 1 < stages:
                keeps[i], total = add_halves(f"halves_{i}_{stage}", keeps[i], came)
                got[i] = tp_swap(total, tp_count, 2 << stage)
            elif i < last:
                total = add_last(f"last_{i}", keeps[i], came)
                done.append(total)
            else:
                attn_out = assemble(done, keeps[i], came, places, share * rows, columns)
    return attn_out, new_key, new_value


def solution(mesh):
    return jax.shard_map(
        shards,
        mesh=mesh,
        in_specs=(
            P(("groups", "pool"), None),
            P(),
            P("pool", "tp"),
            P("pool", "tp"),
            P("pool", "tp"),
            P("tp", "pool"),
            P(("groups", "pool"), "tp", None, None),
            P(("groups", "pool"), "tp", None, None),
            P(("groups", "pool")),
            P(("groups", "pool")),
            P("pool", None, "tp"),
            P("pool", None, "tp"),
            P("pool", None, "tp"),
            P("pool", None, "tp"),
        ),
        out_specs=(
            P(("groups", "tp"), "pool"),
            P(("groups", "pool"), "tp"),
            P(("groups", "pool"), "tp"),
        ),
        check_vma=False,
    )
```

```python
import functools
import math

import jax
import jax.numpy as jnp
from jax import lax
from jax.experimental import pallas as pl
from jax.experimental.pallas import tpu as pltpu
from jax.sharding import PartitionSpec as P

epsilon = 1e-05
adapter_scale = 0.5
rope_base = 500000.0
masked_score = -1e30


VMEM = pl.BlockSpec(memory_space=pltpu.VMEM)
HBM = pl.BlockSpec(memory_space=pltpu.HBM)
SMEM = pl.BlockSpec(memory_space=pltpu.SMEM)


def local_call(kernel, name, operands, outs, scratch=(), carried=(), mib=16):
    counts = (len(operands), len(carried), len(outs), len(carried), len(scratch))

    def body(*refs):
        groups, at = [], 0
        for n in counts:
            groups.append(refs[at : at + n])
            at += n
        ins, sources, out_refs, targets, scratch_refs = groups
        copies = [
            pltpu.make_async_copy(source, target, refs[-1].at[i])
            for i, (source, target) in enumerate(zip(sources, targets))
        ]
        for copy in copies:
            copy.start()
        kernel(ins, out_refs, scratch_refs)
        for copy in copies:
            copy.wait()

    sems = [pltpu.SemaphoreType.DMA((len(carried),))] if carried else []
    return pl.pallas_call(
        body,
        in_specs=[spec for _, spec in operands] + [HBM] * len(carried),
        out_specs=[VMEM] * (len(outs) + len(carried)),
        out_shape=[*outs, *[pltpu.VMEM(x.shape, x.dtype) for x in carried]],
        scratch_shapes=[*scratch, *sems],
        compiler_params=pltpu.CompilerParams(vmem_limit_bytes=mib * 1024 * 1024),
        cost_estimate=pl.CostEstimate(flops=1000, bytes_accessed=1000, transcendentals=0),
        name=name,
    )(
        *[x for x, _ in operands],
        *[pltpu.with_memory_space_constraint(x, pltpu.HBM) for x in carried],
    )


def in_vmem(arrays):
    return [(x, VMEM) for x in arrays]


def shaped(shape, dtype=jnp.float32):
    return jax.ShapeDtypeStruct(shape, dtype)


def after(x, *earlier):
    return lax.optimization_barrier((x, *earlier))[0]


def core_swap(x, pool_count):
    return lax.ppermute(x, "pool", [(p, p ^ 1) for p in range(pool_count)])


def chip_move(x, pool_count, d, e=0):
    chips = pool_count // 2
    return lax.ppermute(
        x,
        "pool",
        [(p, (p // 2 + d) % chips * 2 + ((p % 2) ^ e)) for p in range(pool_count)],
    )


def tp_swap(x, tp_count, step):
    return lax.ppermute(x, "tp", [(z, z ^ step) for z in range(tp_count)])


def scaled_slices(name, starts, tokens, gain, width, wanted):
    rows = tokens.shape[0]
    count = starts.shape[0]

    def kernel(ins, outs, scratch):
        starts, gain, tokens = ins
        held, sems = scratch

        def copy(i):
            columns = pl.ds(pl.multiple_of(starts[i], 128), width)
            return pltpu.make_async_copy(tokens.at[:, columns], held.at[i], sems.at[i])

        for i in range(count):
            copy(i).start()
        for i in range(count):
            copy(i).wait()
            columns = pl.ds(pl.multiple_of(starts[i], 128), width)
            factor = gain[:, columns].astype(jnp.float32)
            for out, (which, first, part) in zip(outs, wanted):
                if which == i:
                    values = held[i, first : first + part].astype(jnp.float32)
                    out[...] = (values * factor).astype(jnp.bfloat16)

    tokens = pltpu.with_memory_space_constraint(tokens, pltpu.HBM)
    return local_call(
        kernel,
        name,
        [(starts, SMEM), (gain, VMEM), (tokens, HBM)],
        [shaped((part, width), jnp.bfloat16) for _, _, part in wanted],
        [
            pltpu.VMEM((count, rows, width), jnp.bfloat16),
            pltpu.SemaphoreType.DMA((count,)),
        ],
    )


def shrink(first_id, at, ids, blocks, query_down, value_down, width, tail):
    slots, _ = query_down.shape
    rows = blocks[0].shape[0]
    adapters = slots // 16
    count = len(blocks)

    def kernel(ins, outs, _):
        first_id, at, *ins = ins
        ids, blocks, tables = ins[:count], ins[count : 2 * count], ins[2 * count :]
        local_ids, out, *tails = outs
        for b, tail_out in enumerate(tails):
            columns = pl.ds(pl.multiple_of(at[0], 128), width)
            tail_out[...] = blocks[2 * b + 3][rows - tail :, columns]
        for b in range(count):
            local_ids[:, b * rows : (b + 1) * rows] = ids[b][...] - first_id[0]
        for first in range(0, count, 2):
            x = jnp.concatenate([b[...] for b in blocks[first : first + 2]], axis=0)
            span = slice(first * rows, (first + 2) * rows)
            label = local_ids[:, span].reshape(1, 1, 2 * rows)
            chosen = lax.broadcasted_iota(jnp.int32, (adapters, 1, 2 * rows), 0) == label
            for at, table in enumerate(tables):
                terms = lax.dot_general(
                    table[...], x, (((1,), (1,)), ((), ())), preferred_element_type=jnp.float32
                ).reshape(adapters, 16, 2 * rows)
                out[at * 16 : (at + 1) * 16, span] = jnp.sum(
                    jnp.where(chosen, terms, 0.0), axis=0
                )

    return local_call(
        kernel,
        "shrink",
        [(first_id, SMEM), (at, SMEM), *in_vmem([*ids, *blocks, query_down, value_down])],
        [
            shaped((1, rows * count), jnp.int32),
            shaped((32, rows * count)),
            *[shaped((tail, width), jnp.bfloat16)] * (count // 2 - 1),
        ],
    )


def tables(tokens, lengths, head):
    rows = tokens.shape[0]
    half = head // 2

    def kernel(ins, outs, _):
        tokens, lengths = ins
        scale, cosines, sines, column = outs
        values = tokens[...].astype(jnp.float32)
        mean_square = jnp.mean(values * values, axis=1, keepdims=True)
        scale[...] = lax.rsqrt(mean_square + epsilon)
        here = lax.broadcasted_iota(jnp.int32, (rows, rows), 0)
        there = lax.broadcasted_iota(jnp.int32, (rows, rows), 1)
        positions = jnp.sum(
            jnp.where(here == there, lengths[...].astype(jnp.float32), 0.0), axis=1, keepdims=True
        )
        column[...] = positions.astype(jnp.int32)
        lane = lax.broadcasted_iota(jnp.int32, (1, head), 1)
        exponent = (lane % half).astype(jnp.float32) * (-2.0 / head)
        angles = positions * jnp.exp(exponent * math.log(rope_base))
        cosines[...] = jnp.cos(angles)
        sines[...] = jnp.where(lane < half, -1.0, 1.0) * jnp.sin(angles)

    return local_call(
        kernel,
        "tables",
        in_vmem([tokens, lengths]),
        [
            shaped((rows, 1)),
            shaped((rows, head)),
            shaped((rows, head)),
            shaped((rows, 1), jnp.int32),
        ],
        mib=24,
    )


def load(arrays):
    def kernel(ins, outs, _):
        pass

    return local_call(kernel, "load", [], [], carried=arrays)


def spread_lows(low, ids, adapters):
    total = ids.shape[1]
    low = low.astype(jnp.bfloat16).astype(jnp.float32) * adapter_scale
    chosen = lax.broadcasted_iota(jnp.int32, (adapters, 1, total), 0) == ids.reshape(1, 1, total)
    return [
        jnp.where(chosen, low[at : at + 16][None], 0.0)
        .reshape(adapters * 16, total)
        .T.astype(jnp.bfloat16)
        for at in (0, 16)
    ]


def columns_at(start, width):
    return pl.ds(pl.multiple_of(start, width), width)


def project(name, kinds, span, ids, lows, blocks, weights, which=None, options=()):
    wq, wk, wv, uq, uv = weights
    depth = blocks[0].shape[1]
    wide, kv, slots = wq.shape[1], wk.shape[1], uq.shape[0]
    tile = min(512, wide)
    start, total = span

    def kernel(ins, outs, scratch):
        if options:
            which, *ins = ins
        ids, *ins = ins
        wq, wk, wv, uq, uv = ins[-5:]
        low_refs, ins = ins[: len(lows)], ins[len(lows) : -5]
        blocks, choices = ins[: len(ins) - len(options)], ins[len(ins) - len(options) :]
        xs, spread_q, spread_v = scratch
        at = 0
        for block in blocks:
            xs[at : at + block.shape[0], :] = block[...]
            at += block.shape[0]
        for j, choice in enumerate(choices):

            @pl.when(which[0] == j)
            def _():
                xs[at:, :] = choice[...]

        low = low_refs[0][:, start : start + total]
        for other in low_refs[1:]:
            low = low + other[:, start : start + total]
        spread_q[...], spread_v[...] = spread_lows(
            low, ids[:, start : start + total], slots // 16
        )

        def sums(w, spread=None, u=None):
            acc = jnp.dot(xs[...], w, preferred_element_type=jnp.float32)
            if u is not None:
                acc = acc + jnp.dot(spread[...], u, preferred_element_type=jnp.float32)
            return acc

        def write(acc, columns):
            for out, (first, count, dtype) in zip(outs, kinds):
                out[:, columns] = acc[first : first + count].astype(dtype)

        @pl.loop(0, wide // tile)
        def _(i):
            columns = columns_at(i * tile, tile)
            write(sums(wq[:, columns], spread_q, uq[:, columns]), columns)

        write(sums(wk[...]), slice(wide, wide + kv))
        write(sums(wv[...], spread_v, uv[...]), slice(wide + kv, wide + 2 * kv))

    spread = pltpu.VMEM((total, slots), jnp.bfloat16)
    return local_call(
        kernel,
        name,
        [(which, SMEM)] * bool(options)
        + in_vmem([ids, *lows, *blocks, *options, *weights]),
        [shaped((count, wide + 2 * kv), dtype) for _, count, dtype in kinds],
        [pltpu.VMEM((total, depth), jnp.bfloat16), spread, spread],
    )


def project_base(blocks, weights, carried):
    rows, depth = blocks[0].shape
    wide, kv = weights[0].shape[1], weights[1].shape[1]
    tile = min(512, wide)

    def kernel(ins, outs, scratch):
        *blocks, wq, wk, wv = ins
        (xs,) = scratch
        at = 0
        for block in blocks:
            xs[at : at + block.shape[0], :] = block[...]
            at += block.shape[0]

        def write(w, columns):
            acc = jnp.dot(xs[...], w, preferred_element_type=jnp.float32)
            outs[0][:, columns] = acc[:rows]
            outs[1][:, columns] = acc[rows:]

        @pl.loop(0, wide // tile)
        def _(i):
            columns = columns_at(i * tile, tile)
            write(wq[:, columns], columns)

        write(wk[...], slice(wide, wide + kv))
        write(wv[...], slice(wide + kv, wide + 2 * kv))

    return local_call(
        kernel,
        "project_base",
        in_vmem([*blocks, *weights]),
        [shaped((rows, wide + 2 * kv))] * 2,
        [pltpu.VMEM((2 * rows, depth), jnp.bfloat16)],
        carried=carried,
    )


def add_adapters(keep, send, ids, lows, uq, uv):
    rows = keep.shape[0]
    wide, kv, slots = uq.shape[1], uv.shape[1], uq.shape[0]
    tile = min(512, wide)

    def kernel(ins, outs, scratch):
        ids, *ins = ins
        low_refs, (keep0, send0, uq, uv) = ins[: len(lows)], ins[len(lows) :]
        keep, send = outs
        spread_q, spread_v = scratch
        low = low_refs[0][:, : 2 * rows]
        for other in low_refs[1:]:
            low = low + other[:, : 2 * rows]
        spread_q[...], spread_v[...] = spread_lows(low, ids[:, : 2 * rows], slots // 16)

        def write(extra, columns):
            keep[:, columns] = keep0[:, columns] + extra[:rows]
            send[:, columns] = (send0[:, columns] + extra[rows:]).astype(send.dtype)

        @pl.loop(0, wide // tile)
        def _(i):
            columns = columns_at(i * tile, tile)
            write(
                jnp.dot(spread_q[...], uq[:, columns], preferred_element_type=jnp.float32),
                columns,
            )

        keep[:, wide : wide + kv] = keep0[:, wide : wide + kv]
        send[:, wide : wide + kv] = send0[:, wide : wide + kv].astype(send.dtype)
        write(
            jnp.dot(spread_v[...], uv[...], preferred_element_type=jnp.float32),
            slice(wide + kv, wide + 2 * kv),
        )

    spread = pltpu.VMEM((2 * rows, slots), jnp.bfloat16)
    return local_call(
        kernel,
        "add_adapters",
        in_vmem([ids, *lows, keep, send, uq, uv]),
        [shaped(keep.shape), shaped(keep.shape, jnp.bfloat16)],
        [spread, spread],
    )


def add_sums(name, window, keep, other):
    first, part = window

    def kernel(ins, outs, _):
        keep, other = ins
        outs[0][...] = (
            keep[first : first + part, :] + other[...].astype(jnp.float32)
        ).astype(jnp.bfloat16)

    return local_call(
        kernel, name, in_vmem([keep, other]), [shaped((part, keep.shape[1]), jnp.bfloat16)]
    )[0]


def attend_kernel(first_row, block, done, ins, outs, scratch):
    if done:
        for full, source in zip(outs[1:], ins[:2]):
            full[: source.shape[0], :] = source[...]
    keep, swapped, *moved, scale, cosines, sines, lengths, keys, values = ins[2:] if done else ins
    out, key_out, value_out = outs
    head = cosines.shape[1]
    rows = out.shape[0]
    _, kv_heads, cache, _ = keys.shape
    heads = out.shape[1] // head
    group = heads // kv_heads
    score_scale = 1.0 / math.sqrt(head)
    sub = 8

    column = lax.broadcasted_iota(jnp.int32, (sub, sub * cache), 1)
    start = lax.broadcasted_iota(jnp.int32, (sub, sub * cache), 0) * cache

    @pl.loop(0, rows // block)
    def _(i):
        attended, new_keys, new_values = [], [], []
        for half in range(block // sub):
            here = pl.ds(pl.multiple_of(i * block + half * sub, sub), sub)
            whole = pl.ds(pl.multiple_of(first_row + i * block + half * sub, sub), sub)
            x = keep[whole] + swapped[whole].astype(jnp.float32)
            for m in moved:
                x = x + m[here].astype(jnp.float32)
            x = x * scale[whole]
            cos, sin = cosines[whole], sines[whole]
            inside = (column >= start) & (column < start + lengths[whole])

            def piece(i):
                return x[:, i * head : (i + 1) * head]

            def turn(v):
                return v * cos + pltpu.roll(v, head // 2, 1) * sin

            for g in range(kv_heads):
                query = jnp.concatenate(
                    [turn(piece(g * group + h)) for h in range(group)], axis=0
                ).astype(jnp.bfloat16)
                new_key = turn(piece(heads + g)).astype(jnp.bfloat16).astype(jnp.float32)
                new_value = piece(heads + kv_heads + g).astype(jnp.bfloat16).astype(jnp.float32)
                k = keys[whole, g].reshape(sub * cache, head)
                v = values[whole, g].reshape(sub * cache, head)
                scores = (
                    lax.dot_general(
                        query, k, (((1,), (1,)), ((), ())), preferred_element_type=jnp.float32
                    )
                    * score_scale
                )
                own_key = jnp.concatenate([new_key] * group, axis=0)
                own = (
                    jnp.sum(query.astype(jnp.float32) * own_key, axis=1, keepdims=True)
                    * score_scale
                )
                scores = jnp.where(
                    inside[None], scores.reshape(group, sub, sub * cache), masked_score
                ).reshape(group * sub, sub * cache)
                peak = jnp.maximum(jnp.max(scores, axis=1, keepdims=True), own)
                weights = jnp.exp(scores - peak)
                own_weight = jnp.exp(own - peak)
                inverse = 1.0 / (jnp.sum(weights, axis=1, keepdims=True) + own_weight)
                mixed = jnp.dot(weights.astype(jnp.bfloat16), v, preferred_element_type=jnp.float32)
                own_value = jnp.concatenate([new_value] * group, axis=0)
                mixed = (mixed + own_weight * own_value) * inverse
                attended += [mixed[h * sub : (h + 1) * sub] for h in range(group)]
                new_keys.append(new_key)
                new_values.append(new_value)
        r = pl.ds(pl.multiple_of(i * block, block), block)

        def joined(pieces):
            n = len(pieces) * sub // block
            return jnp.concatenate(
                [jnp.concatenate(pieces[j::n], axis=0) for j in range(n)], axis=1
            ).astype(jnp.bfloat16)

        out[r] = joined(attended)
        r = pl.ds(pl.multiple_of((first_row if done else 0) + i * block, block), block)
        key_out[r] = joined(new_keys)
        value_out[r] = joined(new_values)


def attend(name, window, keep, swapped, moved, rest, keys, values, earlier, carried=()):
    _, columns = keep.shape
    _, kv_heads, _, head = keys.shape
    kv_cols = kv_heads * head
    first, part = window
    kv_rows = first + part if earlier else part
    return local_call(
        functools.partial(attend_kernel, first, 16, bool(earlier)),
        name,
        in_vmem([*earlier, keep, swapped, *moved, *rest, keys, values]),
        [
            shaped((part, columns - 2 * kv_cols), jnp.bfloat16),
            *[shaped((kv_rows, kv_cols), jnp.bfloat16)] * 2,
        ],
        carried=carried,
    )


def output_part(name, span, order, blocks, weights):
    rows = blocks[0].shape[0]
    first, columns = span
    depth = weights.shape[0]
    tile = math.gcd(512, columns)
    total = rows * len(blocks)

    def kernel(ins, outs, scratch):
        order, *blocks, weights = ins
        keep, send = outs
        (xs,) = scratch
        for b, block in enumerate(blocks):
            xs[pl.ds(pl.multiple_of(order[b] * rows, rows), rows), :] = block[...]

        @pl.loop(0, columns // tile)
        def _(i):
            w = weights[:, columns_at(first + i * tile, tile)]
            acc = jnp.dot(xs[...], w, preferred_element_type=jnp.float32).astype(jnp.bfloat16)
            keep[:, columns_at(i * tile, tile)] = acc[: total // 2]
            send[:, columns_at(i * tile, tile)] = acc[total // 2 :]

    return local_call(
        kernel,
        name,
        [(order, SMEM), *in_vmem([*blocks, weights])],
        [shaped((total // 2, columns), jnp.bfloat16)] * 2,
        [pltpu.VMEM((total, depth), jnp.bfloat16)],
    )


def add_halves(name, keep, got):
    half, columns = keep.shape[0] // 2, keep.shape[1]

    def kernel(ins, outs, _):
        keep, got = ins
        total = keep[...].astype(jnp.float32) + got[...].astype(jnp.float32)
        outs[0][...] = total[:half]
        outs[1][...] = total[half:].astype(jnp.bfloat16)

    return local_call(
        kernel,
        name,
        in_vmem([keep, got]),
        [shaped((half, columns)), shaped((half, columns), jnp.bfloat16)],
    )


def add_last(name, keep, got):
    def kernel(ins, outs, _):
        total = ins[0][...].astype(jnp.float32) + ins[1][...].astype(jnp.float32)
        outs[0][...] = total.astype(jnp.bfloat16)

    return local_call(kernel, name, in_vmem([keep, got]), [shaped(keep.shape, jnp.bfloat16)])[0]


def assemble(done, keep, got, places, rows, columns):
    def kernel(ins, outs, _):
        *done, keep, got = ins
        total = keep[...].astype(jnp.float32) + got[...].astype(jnp.float32)
        total = total.astype(jnp.bfloat16)
        for piece, spots in zip([*done, total], places):
            for at, to, count, column in spots:
                outs[0][to : to + count, column : column + piece.shape[1]] = piece[
                    at : at + count, :
                ]

    return local_call(
        kernel,
        "assemble",
        in_vmem([*done, keep, got]),
        [shaped((rows, columns), jnp.bfloat16)],
    )[0]


def reversed_bits(x, count):
    out, bit = 0, 1
    while bit < count:
        out = out * 2 + (x // bit) % 2
        bit *= 2
    return out


def shards(
    tokens,
    input_norm_gain,
    query_matrix,
    key_matrix,
    value_matrix,
    output_matrix,
    rotated_key_cache,
    cached_value_rows,
    cache_length_per_row,
    row_adapter_index,
    query_down_maps,
    query_up_maps,
    value_down_maps,
    value_up_maps,
):
    pool_count = lax.axis_size("pool")
    tp_count = lax.axis_size("tp")
    chips = pool_count // 2
    pool_at = lax.axis_index("pool")
    tp_at = lax.axis_index("tp")
    chip, core = pool_at // 2, pool_at % 2
    rows = tokens.shape[0]
    adapters, rank, piece = query_down_maps.shape
    base = query_matrix.shape[0]
    kv_heads = rotated_key_cache.shape[1]
    head = rotated_key_cache.shape[3]

    own_ids = row_adapter_index.reshape(1, rows)
    ids = [
        own_ids if d == e == 0 else chip_move(own_ids, pool_count, d, e)
        for d in range(chips)
        for e in range(2)
    ]
    gain = input_norm_gain.reshape(1, -1)
    (first,) = scaled_slices(
        "slice_tp", (tp_at * piece).reshape(1), tokens, gain, piece, [(0, 0, rows)]
    )
    first = after(first, *ids[1:])
    first, gain_1 = lax.optimization_barrier((first, gain))
    same_core = [first] + [chip_move(first, pool_count, d) for d in range(1, chips)]

    cut = rows // 2
    chunks = [(0, cut), (cut, rows - cut)]
    tail = rows // 4
    starts = [pool_at * base, (pool_at // 2 * 2 + 1 - core) * base]
    wanted = [(0, 0, rows), (1, 0, rows // 2), (1, rows // 2, rows // 2)]
    places = [(d, e) for d in range(1, chips) for e in range(2)]
    for i, (d, e) in enumerate(places):
        starts.append(((chip + d) % chips * 2 + (core + e) % 2) * base)
        wanted.append((2 + i, 0, rows - tail if e else rows))
    own, *slices = scaled_slices(
        "slice_pool", jnp.stack(starts).astype(jnp.int32), tokens, gain_1, base, wanted
    )
    partner, away = slices[:2], dict(zip(places, slices[2:]))
    first_id = (pool_at * adapters).reshape(1).astype(jnp.int32)
    at_piece = (pool_at * base % piece).reshape(1).astype(jnp.int32)
    which = ((tp_at - pool_at * base // piece) % tp_count).reshape(1).astype(jnp.int32)
    lengths = cache_length_per_row.reshape(1, rows)
    share = pool_count // tp_count
    order = []
    for d in range(chips):
        for e in range(2):
            p = (chip - d) % chips * 2 + (core + e) % 2
            order.append(
                reversed_bits(jnp.bitwise_xor(p // share, tp_at), tp_count) * share + p % share
            )
    order = jnp.stack(order).astype(jnp.int32)

    flat_down = [x.reshape(adapters * rank, piece) for x in (query_down_maps, value_down_maps)]
    flat_up = [x.reshape(adapters * rank, x.shape[2]) for x in (query_up_maps, value_up_maps)]
    small = [own, first_id, at_piece, which, lengths, order]
    query_matrix, *small = lax.optimization_barrier((query_matrix, *small))
    own, first_id, at_piece, which, lengths, order = small
    down_q, down_v, *weights = load(
        [*flat_down, query_matrix, key_matrix, value_matrix, *flat_up]
    )
    partner = [core_swap(x, pool_count) for x in partner]
    own_keep, own_send, keys, values = project_base(
        [own, *partner], weights[:3], [rotated_key_cache, cached_value_rows]
    )
    remote = [[] for _ in range(chips)]
    for (d, e), x in away.items():
        remote[d].append(chip_move(after(x, *same_core[1:]), pool_count, d, e))
    same_core[1:] = [after(x, own_keep) for x in same_core[1:]]
    adapter_rows = [b for x in same_core for b in (x, core_swap(x, pool_count))]
    local_ids, shrunk, *tails = shrink(
        first_id, at_piece, ids, adapter_rows, down_q, down_v, base, tail
    )
    lows = [shrunk] + [
        lax.ppermute(shrunk, "tp", [(i, (i + d) % tp_count) for i in range(tp_count)])
        for d in range(1, tp_count)
    ]
    rest = tables(tokens, after(lengths, shrunk), head)

    def along_tp(x, k):
        pairs = []
        for p in range(pool_count):
            z = p * base // piece
            pairs.append((p * tp_count + z, p * tp_count + (z + k) % tp_count))
        return lax.ppermute(x, ("pool", "tp"), pairs)

    tails = [after(x, rest[0]) for x in tails]
    tails = [[x] + [along_tp(x, k) for k in range(1, tp_count)] for x in tails]
    own_sums, own_send = add_adapters(
        own_keep, own_send, after(local_ids, rest[0]), lows, *weights[3:]
    )
    swapped = core_swap(own_send, pool_count)
    local_ids = after(local_ids, own_sums)
    moved = [[] for _ in chunks]
    both = None
    for d in range(1, chips):
        if both is not None:
            remote[d][0] = after(remote[d][0], both)
        at = 2 * d * rows
        (keep,) = project(
            f"project_{d}_0",
            [(0, rows, jnp.float32)],
            (at, rows),
            local_ids,
            lows,
            remote[d][:1],
            weights,
        )
        sends = project(
            f"project_{d}_1",
            [(first, part, jnp.bfloat16) for first, part in chunks],
            (at + rows, rows),
            local_ids,
            lows,
            [after(remote[d][1], keep)],
            weights,
            which,
            tails[d - 1],
        )
        for c, window in enumerate(chunks):
            swap = core_swap(sends[c], pool_count)
            if c:
                swap = after(swap, both)
            both = add_sums(f"add_{d}_{c}", window, keep, swap)
            moved[c].append(chip_move(both, pool_count, -d))
    moved[0][0] = after(moved[0][0], both)

    attended, earlier = [], []
    for c, window in enumerate(chunks):
        out, *earlier = attend(
            f"attend_{c}",
            window,
            own_sums,
            swapped,
            moved[c],
            rest,
            keys,
            values,
            earlier[:2],
            [] if c else [output_matrix],
        )
        if c == 0:
            out_weights = earlier[2]
        if c:
            out = after(out, attended[-1][-1])
        attended.append([out] + [chip_move(out, pool_count, d) for d in range(1, chips)])
    new_key, new_value = earlier
    attended[0][0] = after(attended[0][0], new_key)

    columns = output_matrix.shape[1]
    layout = [(0, 0, 1), (1, 0, 2), (1, 2, 4), (1, 3, 4)]
    gathered, keeps, sends, products = {}, [], [], []

    def multiply():
        c, at, count = layout[len(keeps)]
        if c not in gathered:
            parts = [after(x, products[-1]) for x in attended[c]] if c else attended[c]
            gathered[c] = [b for x in parts for b in (x, core_swap(x, pool_count))]
        else:
            gathered[c][0] = after(gathered[c][0], products[-1])
        width = columns // count
        keep, send = output_part(
            f"output_{c}_{at}_{count}", (at * width, width), order, gathered[c], out_weights
        )
        keeps.append(keep)
        sends.append(send)
        products.append(keep)

    stages = reversed_bits(1, tp_count).bit_length()
    last = len(layout) - 1
    total, got, done, places = None, {}, [], []
    for i, (c, at, count) in enumerate(layout):
        start, part = chunks[c]
        column = at * columns // count
        places.append([(r * part, r * rows + start, part, column) for r in range(share)])
    for slot in range(last + stages):
        while len(keeps) < min(slot + 2, last + 1):
            multiply()
        for stage in range(stages):
            i = slot - stage
            if not 0 <= i <= last:
                continue
            if stage == 0:
                got[i] = tp_swap(sends[i], tp_count, 1)
            past = [products[-1]] + ([] if total is None else [total])
            came = after(got[i], *past)
            if stage + 1 < stages:
                keeps[i], total = add_halves(f"halves_{i}_{stage}", keeps[i], came)
                got[i] = tp_swap(total, tp_count, 2 << stage)
            elif i < last:
                total = add_last(f"last_{i}", keeps[i], came)
                done.append(total)
            else:
                attn_out = assemble(done, keeps[i], came, places, share * rows, columns)
    return attn_out, new_key, new_value


def solution(mesh):
    return jax.shard_map(
        shards,
        mesh=mesh,
        in_specs=(
            P(("groups", "pool"), None),
            P(),
            P("pool", "tp"),
            P("pool", "tp"),
            P("pool", "tp"),
            P("tp", "pool"),
            P(("groups", "pool"), "tp", None, None),
            P(("groups", "pool"), "tp", None, None),
            P(("groups", "pool")),
            P(("groups", "pool")),
            P("pool", None, "tp"),
            P("pool", None, "tp"),
            P("pool", None, "tp"),
            P("pool", None, "tp"),
        ),
        out_specs=(
            P(("groups", "tp"), "pool"),
            P(("groups", "pool"), "tp"),
            P(("groups", "pool"), "tp"),
        ),
        check_vma=False,
    )
```

```python
import functools
import math

import jax
import jax.numpy as jnp
from jax import lax
from jax.experimental import pallas as pl
from jax.experimental.pallas import tpu as pltpu
from jax.sharding import PartitionSpec as P

epsilon = 1e-05
adapter_scale = 0.5
rope_base = 500000.0
masked_score = -1e30


VMEM = pl.BlockSpec(memory_space=pltpu.VMEM)
HBM = pl.BlockSpec(memory_space=pltpu.HBM)
SMEM = pl.BlockSpec(memory_space=pltpu.SMEM)


def local_call(kernel, name, operands, outs, scratch=(), carried=(), mib=16):
    counts = (len(operands), len(carried), len(outs), len(carried), len(scratch))

    def body(*refs):
        groups, at = [], 0
        for n in counts:
            groups.append(refs[at : at + n])
            at += n
        ins, sources, out_refs, targets, scratch_refs = groups
        copies = [
            pltpu.make_async_copy(source, target, refs[-1].at[i])
            for i, (source, target) in enumerate(zip(sources, targets))
        ]
        for copy in copies:
            copy.start()
        kernel(ins, out_refs, scratch_refs)
        for copy in copies:
            copy.wait()

    sems = [pltpu.SemaphoreType.DMA((len(carried),))] if carried else []
    return pl.pallas_call(
        body,
        in_specs=[spec for _, spec in operands] + [HBM] * len(carried),
        out_specs=[VMEM] * (len(outs) + len(carried)),
        out_shape=[*outs, *[pltpu.VMEM(x.shape, x.dtype) for x in carried]],
        scratch_shapes=[*scratch, *sems],
        compiler_params=pltpu.CompilerParams(vmem_limit_bytes=mib * 1024 * 1024),
        cost_estimate=pl.CostEstimate(flops=1000, bytes_accessed=1000, transcendentals=0),
        name=name,
    )(
        *[x for x, _ in operands],
        *[pltpu.with_memory_space_constraint(x, pltpu.HBM) for x in carried],
    )


def in_vmem(arrays):
    return [(x, VMEM) for x in arrays]


def shaped(shape, dtype=jnp.float32):
    return jax.ShapeDtypeStruct(shape, dtype)


def after(x, *earlier):
    return lax.optimization_barrier((x, *earlier))[0]


def core_swap(x, pool_count):
    return lax.ppermute(x, "pool", [(p, p ^ 1) for p in range(pool_count)])


def chip_move(x, pool_count, d, e=0):
    chips = pool_count // 2
    return lax.ppermute(
        x,
        "pool",
        [(p, (p // 2 + d) % chips * 2 + ((p % 2) ^ e)) for p in range(pool_count)],
    )


def tp_swap(x, tp_count, step):
    return lax.ppermute(x, "tp", [(z, z ^ step) for z in range(tp_count)])


def scaled_slices(name, starts, tokens, gain, width, wanted):
    rows = tokens.shape[0]
    count = starts.shape[0]

    def kernel(ins, outs, scratch):
        starts, gain, tokens = ins
        held, sems = scratch

        def copy(i):
            columns = pl.ds(pl.multiple_of(starts[i], 128), width)
            return pltpu.make_async_copy(tokens.at[:, columns], held.at[i], sems.at[i])

        for i in range(count):
            copy(i).start()
        for i in range(count):
            copy(i).wait()
            columns = pl.ds(pl.multiple_of(starts[i], 128), width)
            factor = gain[:, columns].astype(jnp.float32)
            for out, (which, first, part) in zip(outs, wanted):
                if which == i:
                    values = held[i, first : first + part].astype(jnp.float32)
                    out[...] = (values * factor).astype(jnp.bfloat16)

    tokens = pltpu.with_memory_space_constraint(tokens, pltpu.HBM)
    return local_call(
        kernel,
        name,
        [(starts, SMEM), (gain, VMEM), (tokens, HBM)],
        [shaped((part, width), jnp.bfloat16) for _, _, part in wanted],
        [
            pltpu.VMEM((count, rows, width), jnp.bfloat16),
            pltpu.SemaphoreType.DMA((count,)),
        ],
    )


def shrink(first_id, ids, blocks, query_down, value_down):
    slots, _ = query_down.shape
    rows = blocks[0].shape[0]
    adapters = slots // 16
    count = len(blocks)

    def kernel(ins, outs, _):
        first_id, *ins = ins
        ids, blocks, tables = ins[:count], ins[count : 2 * count], ins[2 * count :]
        local_ids, out = outs
        for b in range(count):
            local_ids[:, b * rows : (b + 1) * rows] = ids[b][...] - first_id[0]
        for first in range(0, count, 2):
            x = jnp.concatenate([b[...] for b in blocks[first : first + 2]], axis=0)
            span = slice(first * rows, (first + 2) * rows)
            label = local_ids[:, span].reshape(1, 1, 2 * rows)
            chosen = lax.broadcasted_iota(jnp.int32, (adapters, 1, 2 * rows), 0) == label
            for at, table in enumerate(tables):
                terms = lax.dot_general(
                    table[...], x, (((1,), (1,)), ((), ())), preferred_element_type=jnp.float32
                ).reshape(adapters, 16, 2 * rows)
                out[at * 16 : (at + 1) * 16, span] = jnp.sum(
                    jnp.where(chosen, terms, 0.0), axis=0
                )

    return local_call(
        kernel,
        "shrink",
        [(first_id, SMEM), *in_vmem([*ids, *blocks, query_down, value_down])],
        [
            shaped((1, rows * count), jnp.int32),
            shaped((32, rows * count)),
        ],
    )


def tables(tokens, lengths, head):
    rows = tokens.shape[0]
    half = head // 2

    def kernel(ins, outs, _):
        tokens, lengths = ins
        scale, cosines, sines, column = outs
        values = tokens[...].astype(jnp.float32)
        mean_square = jnp.mean(values * values, axis=1, keepdims=True)
        scale[...] = lax.rsqrt(mean_square + epsilon)
        here = lax.broadcasted_iota(jnp.int32, (rows, rows), 0)
        there = lax.broadcasted_iota(jnp.int32, (rows, rows), 1)
        positions = jnp.sum(
            jnp.where(here == there, lengths[...].astype(jnp.float32), 0.0), axis=1, keepdims=True
        )
        column[...] = positions.astype(jnp.int32)
        lane = lax.broadcasted_iota(jnp.int32, (1, head), 1)
        exponent = (lane % half).astype(jnp.float32) * (-2.0 / head)
        angles = positions * jnp.exp(exponent * math.log(rope_base))
        cosines[...] = jnp.cos(angles)
        sines[...] = jnp.where(lane < half, -1.0, 1.0) * jnp.sin(angles)

    return local_call(
        kernel,
        "tables",
        in_vmem([tokens, lengths]),
        [
            shaped((rows, 1)),
            shaped((rows, head)),
            shaped((rows, head)),
            shaped((rows, 1), jnp.int32),
        ],
        mib=24,
    )


def load(arrays):
    def kernel(ins, outs, _):
        pass

    return local_call(kernel, "load", [], [], carried=arrays)


def spread_lows(low, ids, adapters):
    total = ids.shape[1]
    low = low.astype(jnp.bfloat16).astype(jnp.float32) * adapter_scale
    chosen = lax.broadcasted_iota(jnp.int32, (adapters, 1, total), 0) == ids.reshape(1, 1, total)
    return [
        jnp.where(chosen, low[at : at + 16][None], 0.0)
        .reshape(adapters * 16, total)
        .T.astype(jnp.bfloat16)
        for at in (0, 16)
    ]


def columns_at(start, width):
    return pl.ds(pl.multiple_of(start, width), width)


def project(name, kinds, span, ids, lows, blocks, weights):
    wq, wk, wv, uq, uv = weights
    depth = blocks[0].shape[1]
    wide, kv, slots = wq.shape[1], wk.shape[1], uq.shape[0]
    tile = min(512, wide)
    start, total = span

    def kernel(ins, outs, scratch):
        ids, *ins = ins
        wq, wk, wv, uq, uv = ins[-5:]
        low_refs, blocks = ins[: len(lows)], ins[len(lows) : -5]
        xs, spread_q, spread_v = scratch
        at = 0
        for block in blocks:
            xs[at : at + block.shape[0], :] = block[...]
            at += block.shape[0]
        low = low_refs[0][:, start : start + total]
        for other in low_refs[1:]:
            low = low + other[:, start : start + total]
        spread_q[...], spread_v[...] = spread_lows(
            low, ids[:, start : start + total], slots // 16
        )

        def sums(w, spread=None, u=None):
            acc = jnp.dot(xs[...], w, preferred_element_type=jnp.float32)
            if u is not None:
                acc = acc + jnp.dot(spread[...], u, preferred_element_type=jnp.float32)
            return acc

        def write(acc, columns):
            for out, (first, count, dtype) in zip(outs, kinds):
                out[:, columns] = acc[first : first + count].astype(dtype)

        @pl.loop(0, wide // tile)
        def _(i):
            columns = columns_at(i * tile, tile)
            write(sums(wq[:, columns], spread_q, uq[:, columns]), columns)

        write(sums(wk[...]), slice(wide, wide + kv))
        write(sums(wv[...], spread_v, uv[...]), slice(wide + kv, wide + 2 * kv))

    spread = pltpu.VMEM((total, slots), jnp.bfloat16)
    return local_call(
        kernel,
        name,
        in_vmem([ids, *lows, *blocks, *weights]),
        [shaped((count, wide + 2 * kv), dtype) for _, count, dtype in kinds],
        [pltpu.VMEM((total, depth), jnp.bfloat16), spread, spread],
    )


def project_base(blocks, weights, carried):
    rows, depth = blocks[0].shape
    wide, kv = weights[0].shape[1], weights[1].shape[1]
    tile = min(512, wide)

    def kernel(ins, outs, scratch):
        *blocks, wq, wk, wv = ins
        (xs,) = scratch
        at = 0
        for block in blocks:
            xs[at : at + block.shape[0], :] = block[...]
            at += block.shape[0]

        def write(w, columns):
            acc = jnp.dot(xs[...], w, preferred_element_type=jnp.float32)
            outs[0][:, columns] = acc[:rows]
            outs[1][:, columns] = acc[rows:]

        @pl.loop(0, wide // tile)
        def _(i):
            columns = columns_at(i * tile, tile)
            write(wq[:, columns], columns)

        write(wk[...], slice(wide, wide + kv))
        write(wv[...], slice(wide + kv, wide + 2 * kv))

    return local_call(
        kernel,
        "project_base",
        in_vmem([*blocks, *weights]),
        [shaped((rows, wide + 2 * kv))] * 2,
        [pltpu.VMEM((2 * rows, depth), jnp.bfloat16)],
        carried=carried,
    )


def add_adapters(keep, send, ids, lows, uq, uv):
    rows = keep.shape[0]
    wide, kv, slots = uq.shape[1], uv.shape[1], uq.shape[0]
    tile = min(512, wide)

    def kernel(ins, outs, scratch):
        ids, *ins = ins
        low_refs, (keep0, send0, uq, uv) = ins[: len(lows)], ins[len(lows) :]
        keep, send = outs
        spread_q, spread_v = scratch
        low = low_refs[0][:, : 2 * rows]
        for other in low_refs[1:]:
            low = low + other[:, : 2 * rows]
        spread_q[...], spread_v[...] = spread_lows(low, ids[:, : 2 * rows], slots // 16)

        def write(extra, columns):
            keep[:, columns] = keep0[:, columns] + extra[:rows]
            send[:, columns] = (send0[:, columns] + extra[rows:]).astype(send.dtype)

        @pl.loop(0, wide // tile)
        def _(i):
            columns = columns_at(i * tile, tile)
            write(
                jnp.dot(spread_q[...], uq[:, columns], preferred_element_type=jnp.float32),
                columns,
            )

        keep[:, wide : wide + kv] = keep0[:, wide : wide + kv]
        send[:, wide : wide + kv] = send0[:, wide : wide + kv].astype(send.dtype)
        write(
            jnp.dot(spread_v[...], uv[...], preferred_element_type=jnp.float32),
            slice(wide + kv, wide + 2 * kv),
        )

    spread = pltpu.VMEM((2 * rows, slots), jnp.bfloat16)
    return local_call(
        kernel,
        "add_adapters",
        in_vmem([ids, *lows, keep, send, uq, uv]),
        [shaped(keep.shape), shaped(keep.shape, jnp.bfloat16)],
        [spread, spread],
    )


def add_sums(name, window, keep, others):
    first, part = window

    def kernel(ins, outs, _):
        keep, *others = ins
        at = 0
        for other in others:
            n = other.shape[0]
            total = keep[first + at : first + at + n, :] + other[...].astype(jnp.float32)
            outs[0][at : at + n, :] = total.astype(jnp.bfloat16)
            at += n

    return local_call(
        kernel, name, in_vmem([keep, *others]), [shaped((part, keep.shape[1]), jnp.bfloat16)]
    )[0]


def attend_kernel(first_row, block, done, ins, outs, scratch):
    if done:
        for full, source in zip(outs[1:], ins[:2]):
            full[: source.shape[0], :] = source[...]
    keep, swapped, *moved, scale, cosines, sines, lengths, keys, values = ins[2:] if done else ins
    out, key_out, value_out = outs
    head = cosines.shape[1]
    rows = out.shape[0]
    _, kv_heads, cache, _ = keys.shape
    heads = out.shape[1] // head
    group = heads // kv_heads
    score_scale = 1.0 / math.sqrt(head)
    sub = 8

    column = lax.broadcasted_iota(jnp.int32, (sub, sub * cache), 1)
    start = lax.broadcasted_iota(jnp.int32, (sub, sub * cache), 0) * cache

    @pl.loop(0, rows // block)
    def _(i):
        attended, new_keys, new_values = [], [], []
        for half in range(block // sub):
            here = pl.ds(pl.multiple_of(i * block + half * sub, sub), sub)
            whole = pl.ds(pl.multiple_of(first_row + i * block + half * sub, sub), sub)
            x = keep[whole] + swapped[whole].astype(jnp.float32)
            for m in moved:
                x = x + m[here].astype(jnp.float32)
            x = x * scale[whole]
            cos, sin = cosines[whole], sines[whole]
            inside = (column >= start) & (column < start + lengths[whole])

            def piece(i):
                return x[:, i * head : (i + 1) * head]

            def turn(v):
                return v * cos + pltpu.roll(v, head // 2, 1) * sin

            for g in range(kv_heads):
                query = jnp.concatenate(
                    [turn(piece(g * group + h)) for h in range(group)], axis=0
                ).astype(jnp.bfloat16)
                new_key = turn(piece(heads + g)).astype(jnp.bfloat16).astype(jnp.float32)
                new_value = piece(heads + kv_heads + g).astype(jnp.bfloat16).astype(jnp.float32)
                k = keys[whole, g].reshape(sub * cache, head)
                v = values[whole, g].reshape(sub * cache, head)
                scores = (
                    lax.dot_general(
                        query, k, (((1,), (1,)), ((), ())), preferred_element_type=jnp.float32
                    )
                    * score_scale
                )
                own_key = jnp.concatenate([new_key] * group, axis=0)
                own = (
                    jnp.sum(query.astype(jnp.float32) * own_key, axis=1, keepdims=True)
                    * score_scale
                )
                scores = jnp.where(
                    inside[None], scores.reshape(group, sub, sub * cache), masked_score
                ).reshape(group * sub, sub * cache)
                peak = jnp.maximum(jnp.max(scores, axis=1, keepdims=True), own)
                weights = jnp.exp(scores - peak)
                own_weight = jnp.exp(own - peak)
                inverse = 1.0 / (jnp.sum(weights, axis=1, keepdims=True) + own_weight)
                mixed = jnp.dot(weights.astype(jnp.bfloat16), v, preferred_element_type=jnp.float32)
                own_value = jnp.concatenate([new_value] * group, axis=0)
                mixed = (mixed + own_weight * own_value) * inverse
                attended += [mixed[h * sub : (h + 1) * sub] for h in range(group)]
                new_keys.append(new_key)
                new_values.append(new_value)
        r = pl.ds(pl.multiple_of(i * block, block), block)

        def joined(pieces):
            n = len(pieces) * sub // block
            return jnp.concatenate(
                [jnp.concatenate(pieces[j::n], axis=0) for j in range(n)], axis=1
            ).astype(jnp.bfloat16)

        out[r] = joined(attended)
        r = pl.ds(pl.multiple_of((first_row if done else 0) + i * block, block), block)
        key_out[r] = joined(new_keys)
        value_out[r] = joined(new_values)


def attend(name, window, keep, swapped, moved, rest, keys, values, earlier, carried=()):
    _, columns = keep.shape
    _, kv_heads, _, head = keys.shape
    kv_cols = kv_heads * head
    first, part = window
    kv_rows = first + part if earlier else part
    return local_call(
        functools.partial(attend_kernel, first, 16, bool(earlier)),
        name,
        in_vmem([*earlier, keep, swapped, *moved, *rest, keys, values]),
        [
            shaped((part, columns - 2 * kv_cols), jnp.bfloat16),
            *[shaped((kv_rows, kv_cols), jnp.bfloat16)] * 2,
        ],
        carried=carried,
    )


def output_part(name, span, order, blocks, weights):
    rows = blocks[0].shape[0]
    first, columns = span
    depth = weights.shape[0]
    tile = math.gcd(512, columns)
    total = rows * len(blocks)

    def kernel(ins, outs, scratch):
        order, *blocks, weights = ins
        keep, send = outs
        (xs,) = scratch
        for b, block in enumerate(blocks):
            xs[pl.ds(pl.multiple_of(order[b] * rows, rows), rows), :] = block[...]

        @pl.loop(0, columns // tile)
        def _(i):
            w = weights[:, columns_at(first + i * tile, tile)]
            acc = jnp.dot(xs[...], w, preferred_element_type=jnp.float32).astype(jnp.bfloat16)
            keep[:, columns_at(i * tile, tile)] = acc[: total // 2]
            send[:, columns_at(i * tile, tile)] = acc[total // 2 :]

    return local_call(
        kernel,
        name,
        [(order, SMEM), *in_vmem([*blocks, weights])],
        [shaped((total // 2, columns), jnp.bfloat16)] * 2,
        [pltpu.VMEM((total, depth), jnp.bfloat16)],
    )


def add_halves(name, keep, got):
    half, columns = keep.shape[0] // 2, keep.shape[1]

    def kernel(ins, outs, _):
        keep, got = ins
        total = keep[...].astype(jnp.float32) + got[...].astype(jnp.float32)
        outs[0][...] = total[:half]
        outs[1][...] = total[half:].astype(jnp.bfloat16)

    return local_call(
        kernel,
        name,
        in_vmem([keep, got]),
        [shaped((half, columns)), shaped((half, columns), jnp.bfloat16)],
    )


def add_last(name, keep, got):
    def kernel(ins, outs, _):
        total = ins[0][...].astype(jnp.float32) + ins[1][...].astype(jnp.float32)
        outs[0][...] = total.astype(jnp.bfloat16)

    return local_call(kernel, name, in_vmem([keep, got]), [shaped(keep.shape, jnp.bfloat16)])[0]


def assemble(done, keep, got, places, rows, columns):
    def kernel(ins, outs, _):
        *done, keep, got = ins
        total = keep[...].astype(jnp.float32) + got[...].astype(jnp.float32)
        total = total.astype(jnp.bfloat16)
        for piece, spots in zip([*done, total], places):
            for at, to, count, column in spots:
                outs[0][to : to + count, column : column + piece.shape[1]] = piece[
                    at : at + count, :
                ]

    return local_call(
        kernel,
        "assemble",
        in_vmem([*done, keep, got]),
        [shaped((rows, columns), jnp.bfloat16)],
    )[0]


def reversed_bits(x, count):
    out, bit = 0, 1
    while bit < count:
        out = out * 2 + (x // bit) % 2
        bit *= 2
    return out


def shards(
    tokens,
    input_norm_gain,
    query_matrix,
    key_matrix,
    value_matrix,
    output_matrix,
    rotated_key_cache,
    cached_value_rows,
    cache_length_per_row,
    row_adapter_index,
    query_down_maps,
    query_up_maps,
    value_down_maps,
    value_up_maps,
):
    pool_count = lax.axis_size("pool")
    tp_count = lax.axis_size("tp")
    chips = pool_count // 2
    pool_at = lax.axis_index("pool")
    tp_at = lax.axis_index("tp")
    chip, core = pool_at // 2, pool_at % 2
    rows = tokens.shape[0]
    adapters, rank, piece = query_down_maps.shape
    base = query_matrix.shape[0]
    kv_heads = rotated_key_cache.shape[1]
    head = rotated_key_cache.shape[3]

    own_ids = row_adapter_index.reshape(1, rows)
    ids = [
        own_ids if d == e == 0 else chip_move(own_ids, pool_count, d, e)
        for d in range(chips)
        for e in range(2)
    ]
    gain = input_norm_gain.reshape(1, -1)
    (first,) = scaled_slices(
        "slice_tp", (tp_at * piece).reshape(1), tokens, gain, piece, [(0, 0, rows)]
    )
    first = after(first, *ids[1:])
    first, gain_1 = lax.optimization_barrier((first, gain))
    same_core = [first] + [chip_move(first, pool_count, d) for d in range(1, chips)]

    cut = rows // 2
    chunks = [(0, cut), (cut, rows - cut)]
    starts = [pool_at * base, (pool_at // 2 * 2 + 1 - core) * base]
    wanted = [(0, 0, rows), (1, 0, rows // 2), (1, rows // 2, rows // 2)]
    places = []
    for d in range(1, chips):
        for e in range(2):
            for c, (at, part) in enumerate(chunks if e else [(0, rows)]):
                places.append((d, e, c))
                wanted.append((len(starts), at, part))
            starts.append(((chip + d) % chips * 2 + (core + e) % 2) * base)
    own, *slices = scaled_slices(
        "slice_pool", jnp.stack(starts).astype(jnp.int32), tokens, gain_1, base, wanted
    )
    partner, away = slices[:2], dict(zip(places, slices[2:]))
    first_id = (pool_at * adapters).reshape(1).astype(jnp.int32)
    lengths = cache_length_per_row.reshape(1, rows)
    share = pool_count // tp_count
    order = []
    for d in range(chips):
        for e in range(2):
            p = (chip - d) % chips * 2 + (core + e) % 2
            order.append(
                reversed_bits(jnp.bitwise_xor(p // share, tp_at), tp_count) * share + p % share
            )
    order = jnp.stack(order).astype(jnp.int32)

    flat_down = [x.reshape(adapters * rank, piece) for x in (query_down_maps, value_down_maps)]
    flat_up = [x.reshape(adapters * rank, x.shape[2]) for x in (query_up_maps, value_up_maps)]
    small = [own, first_id, lengths, order]
    query_matrix, *small = lax.optimization_barrier((query_matrix, *small))
    own, first_id, lengths, order = small
    down_q, down_v, *weights = load(
        [*flat_down, query_matrix, key_matrix, value_matrix, *flat_up]
    )
    partner = [core_swap(x, pool_count) for x in partner]
    own_keep, own_send, keys, values = project_base(
        [own, *partner], weights[:3], [rotated_key_cache, cached_value_rows]
    )
    remote = {}
    for (d, e, c), x in away.items():
        remote[d, e, c] = chip_move(after(x, *same_core[1:]), pool_count, d, e)
    same_core[1:] = [after(x, own_keep) for x in same_core[1:]]
    adapter_rows = [b for x in same_core for b in (x, core_swap(x, pool_count))]
    local_ids, shrunk = shrink(first_id, ids, adapter_rows, down_q, down_v)
    lows = [shrunk] + [
        lax.ppermute(shrunk, "tp", [(i, (i + d) % tp_count) for i in range(tp_count)])
        for d in range(1, tp_count)
    ]
    rest = tables(tokens, after(lengths, shrunk), head)

    own_sums, own_send = add_adapters(
        own_keep, own_send, after(local_ids, rest[0]), lows, *weights[3:]
    )
    swapped = core_swap(own_send, pool_count)
    local_ids = after(local_ids, own_sums)
    moved = [[] for _ in chunks]
    keeps, sends, last = {}, {}, own_sums
    for d in range(1, chips):
        at = 2 * d * rows
        (keeps[d],) = project(
            f"project_{d}_0",
            [(0, rows, jnp.float32)],
            (at, rows),
            local_ids,
            lows,
            [after(remote[d, 0, 0], last)],
            weights,
        )
        last = keeps[d]
    for c, (first, part) in enumerate(chunks):
        piece_rows = part // 2
        kinds = [(i, piece_rows, jnp.bfloat16) for i in range(0, part, piece_rows)]
        for d in range(1, chips):
            sends[c, d] = project(
                f"project_{d}_1_{c}",
                kinds,
                ((2 * d + 1) * rows + first, part),
                local_ids,
                lows,
                [after(remote[d, 1, c], last)],
                weights,
            )
            last = sends[c, d][0]
    both = None
    for c, window in enumerate(chunks):
        for d in range(1, chips):
            keep = keeps[d]
            if c:
                keep = after(keep, both)
            else:
                keep = after(keep, *[x for (_, _, c), x in remote.items() if c])
            swaps = [core_swap(x, pool_count) for x in sends[c, d]]
            both = add_sums(f"add_{d}_{c}", window, keep, swaps)
            moved[c].append(chip_move(both, pool_count, -d))
    moved[0][0] = after(moved[0][0], both)

    attended, earlier = [], []
    for c, window in enumerate(chunks):
        out, *earlier = attend(
            f"attend_{c}",
            window,
            own_sums,
            swapped,
            moved[c],
            rest,
            keys,
            values,
            earlier[:2],
            [] if c else [output_matrix],
        )
        if c == 0:
            out_weights = earlier[2]
        if c:
            out = after(out, attended[-1][-1])
        attended.append([out] + [chip_move(out, pool_count, d) for d in range(1, chips)])
    new_key, new_value = earlier
    attended[0][0] = after(attended[0][0], new_key)

    columns = output_matrix.shape[1]
    layout = [(0, 0, 1), (1, 0, 2), (1, 2, 4), (1, 3, 4)]
    gathered, keeps, sends, products = {}, [], [], []

    def multiply():
        c, at, count = layout[len(keeps)]
        if c not in gathered:
            parts = [after(x, products[-1]) for x in attended[c]] if c else attended[c]
            gathered[c] = [b for x in parts for b in (x, core_swap(x, pool_count))]
        else:
            gathered[c][0] = after(gathered[c][0], products[-1])
        width = columns // count
        keep, send = output_part(
            f"output_{c}_{at}_{count}", (at * width, width), order, gathered[c], out_weights
        )
        keeps.append(keep)
        sends.append(send)
        products.append(keep)

    stages = reversed_bits(1, tp_count).bit_length()
    last = len(layout) - 1
    total, got, done, places = None, {}, [], []
    for i, (c, at, count) in enumerate(layout):
        start, part = chunks[c]
        column = at * columns // count
        places.append([(r * part, r * rows + start, part, column) for r in range(share)])
    for slot in range(last + stages):
        while len(keeps) < min(slot + 2, last + 1):
            multiply()
        for stage in range(stages):
            i = slot - stage
            if not 0 <= i <= last:
                continue
            if stage == 0:
                got[i] = tp_swap(sends[i], tp_count, 1)
            past = [products[-1]] + ([] if total is None else [total])
            came = after(got[i], *past)
            if stage + 1 < stages:
                keeps[i], total = add_halves(f"halves_{i}_{stage}", keeps[i], came)
                got[i] = tp_swap(total, tp_count, 2 << stage)
            elif i < last:
                total = add_last(f"last_{i}", keeps[i], came)
                done.append(total)
            else:
                attn_out = assemble(done, keeps[i], came, places, share * rows, columns)
    return attn_out, new_key, new_value


def solution(mesh):
    return jax.shard_map(
        shards,
        mesh=mesh,
        in_specs=(
            P(("groups", "pool"), None),
            P(),
            P("pool", "tp"),
            P("pool", "tp"),
            P("pool", "tp"),
            P("tp", "pool"),
            P(("groups", "pool"), "tp", None, None),
            P(("groups", "pool"), "tp", None, None),
            P(("groups", "pool")),
            P(("groups", "pool")),
            P("pool", None, "tp"),
            P("pool", None, "tp"),
            P("pool", None, "tp"),
            P("pool", None, "tp"),
        ),
        out_specs=(
            P(("groups", "tp"), "pool"),
            P(("groups", "pool"), "tp"),
            P(("groups", "pool"), "tp"),
        ),
        check_vma=False,
    )
```

```python
import functools
import math

import jax
import jax.numpy as jnp
from jax import lax
from jax.experimental import pallas as pl
from jax.experimental.pallas import tpu as pltpu
from jax.sharding import PartitionSpec as P

epsilon = 1e-05
adapter_scale = 0.5
rope_base = 500000.0
masked_score = -1e30


VMEM = pl.BlockSpec(memory_space=pltpu.VMEM)
HBM = pl.BlockSpec(memory_space=pltpu.HBM)
SMEM = pl.BlockSpec(memory_space=pltpu.SMEM)


def local_call(kernel, name, operands, outs, scratch=(), carried=(), mib=16):
    counts = (len(operands), len(carried), len(outs), len(carried), len(scratch))

    def body(*refs):
        groups, at = [], 0
        for n in counts:
            groups.append(refs[at : at + n])
            at += n
        ins, sources, out_refs, targets, scratch_refs = groups
        copies = [
            pltpu.make_async_copy(source, target, refs[-1].at[i])
            for i, (source, target) in enumerate(zip(sources, targets))
        ]
        for copy in copies:
            copy.start()
        kernel(ins, out_refs, scratch_refs)
        for copy in copies:
            copy.wait()

    sems = [pltpu.SemaphoreType.DMA((len(carried),))] if carried else []
    return pl.pallas_call(
        body,
        in_specs=[spec for _, spec in operands] + [HBM] * len(carried),
        out_specs=[VMEM] * (len(outs) + len(carried)),
        out_shape=[*outs, *[pltpu.VMEM(x.shape, x.dtype) for x in carried]],
        scratch_shapes=[*scratch, *sems],
        compiler_params=pltpu.CompilerParams(vmem_limit_bytes=mib * 1024 * 1024),
        cost_estimate=pl.CostEstimate(flops=1000, bytes_accessed=1000, transcendentals=0),
        name=name,
    )(
        *[x for x, _ in operands],
        *[pltpu.with_memory_space_constraint(x, pltpu.HBM) for x in carried],
    )


def in_vmem(arrays):
    return [(x, VMEM) for x in arrays]


def shaped(shape, dtype=jnp.float32):
    return jax.ShapeDtypeStruct(shape, dtype)


def after(x, *earlier):
    return lax.optimization_barrier((x, *earlier))[0]


def core_swap(x, pool_count):
    return lax.ppermute(x, "pool", [(p, p ^ 1) for p in range(pool_count)])


def chip_move(x, pool_count, d, e=0):
    chips = pool_count // 2
    return lax.ppermute(
        x,
        "pool",
        [(p, (p // 2 + d) % chips * 2 + ((p % 2) ^ e)) for p in range(pool_count)],
    )


def tp_swap(x, tp_count, step):
    return lax.ppermute(x, "tp", [(z, z ^ step) for z in range(tp_count)])


def scaled_slices(name, starts, tokens, gain, width, wanted):
    rows = tokens.shape[0]
    count = starts.shape[0]

    def kernel(ins, outs, scratch):
        starts, gain, tokens = ins
        held, factors, sems = scratch

        def copy(i):
            columns = pl.ds(pl.multiple_of(starts[i], 128), width)
            return pltpu.make_async_copy(tokens.at[:, columns], held.at[i], sems.at[i])

        for i in range(count):
            copy(i).start()
        factors[...] = gain[...].astype(jnp.float32)
        for i in range(count):
            copy(i).wait()
            row = starts[i] // 128
            for j in range(width // 128):
                columns = slice(j * 128, (j + 1) * 128)
                factor = factors[pl.ds(row + j, 1), :]
                for out, (which, first, part) in zip(outs, wanted):
                    if which == i:
                        values = held[i, first : first + part, columns].astype(jnp.float32)
                        out[:, columns] = (values * factor).astype(jnp.bfloat16)

    tokens = pltpu.with_memory_space_constraint(tokens, pltpu.HBM)
    return local_call(
        kernel,
        name,
        [(starts, SMEM), (gain, VMEM), (tokens, HBM)],
        [shaped((part, width), jnp.bfloat16) for _, _, part in wanted],
        [
            pltpu.VMEM((count, rows, width), jnp.bfloat16),
            pltpu.VMEM(gain.shape, jnp.float32),
            pltpu.SemaphoreType.DMA((count,)),
        ],
    )


def shrink(first_id, ids, blocks, query_down, value_down):
    slots, _ = query_down.shape
    rows = blocks[0].shape[0]
    adapters = slots // 16
    count = len(blocks)

    def kernel(ins, outs, _):
        first_id, *ins = ins
        ids, blocks, tables = ins[:count], ins[count : 2 * count], ins[2 * count :]
        local_ids, out = outs
        for b in range(count):
            local_ids[:, b * rows : (b + 1) * rows] = ids[b][...] - first_id[0]
        for first in range(0, count, 2):
            x = jnp.concatenate([b[...] for b in blocks[first : first + 2]], axis=0)
            span = slice(first * rows, (first + 2) * rows)
            label = local_ids[:, span].reshape(1, 1, 2 * rows)
            chosen = lax.broadcasted_iota(jnp.int32, (adapters, 1, 2 * rows), 0) == label
            for at, table in enumerate(tables):
                terms = lax.dot_general(
                    table[...], x, (((1,), (1,)), ((), ())), preferred_element_type=jnp.float32
                ).reshape(adapters, 16, 2 * rows)
                out[at * 16 : (at + 1) * 16, span] = jnp.sum(
                    jnp.where(chosen, terms, 0.0), axis=0
                )

    return local_call(
        kernel,
        "shrink",
        [(first_id, SMEM), *in_vmem([*ids, *blocks, query_down, value_down])],
        [
            shaped((1, rows * count), jnp.int32),
            shaped((32, rows * count)),
        ],
    )


def tables(tokens, lengths, head):
    rows = tokens.shape[0]
    half = head // 2

    def kernel(ins, outs, _):
        tokens, lengths = ins
        scale, cosines, sines, column = outs
        values = tokens[...].astype(jnp.float32)
        mean_square = jnp.mean(values * values, axis=1, keepdims=True)
        scale[...] = lax.rsqrt(mean_square + epsilon)
        here = lax.broadcasted_iota(jnp.int32, (rows, rows), 0)
        there = lax.broadcasted_iota(jnp.int32, (rows, rows), 1)
        positions = jnp.sum(
            jnp.where(here == there, lengths[...].astype(jnp.float32), 0.0), axis=1, keepdims=True
        )
        column[...] = positions.astype(jnp.int32)
        lane = lax.broadcasted_iota(jnp.int32, (1, head), 1)
        exponent = (lane % half).astype(jnp.float32) * (-2.0 / head)
        angles = positions * jnp.exp(exponent * math.log(rope_base))
        cosines[...] = jnp.cos(angles)
        sines[...] = jnp.where(lane < half, -1.0, 1.0) * jnp.sin(angles)

    return local_call(
        kernel,
        "tables",
        in_vmem([tokens, lengths]),
        [
            shaped((rows, 1)),
            shaped((rows, head)),
            shaped((rows, head)),
            shaped((rows, 1), jnp.int32),
        ],
        mib=24,
    )


def load(arrays):
    def kernel(ins, outs, _):
        pass

    return local_call(kernel, "load", [], [], carried=arrays)


def spread_lows(low, ids, adapters):
    total = ids.shape[1]
    low = low.astype(jnp.bfloat16).astype(jnp.float32) * adapter_scale
    chosen = lax.broadcasted_iota(jnp.int32, (adapters, 1, total), 0) == ids.reshape(1, 1, total)
    return [
        jnp.where(chosen, low[at : at + 16][None], 0.0)
        .reshape(adapters * 16, total)
        .T.astype(jnp.bfloat16)
        for at in (0, 16)
    ]


def columns_at(start, width):
    return pl.ds(pl.multiple_of(start, width), width)


def project(name, kinds, span, ids, lows, blocks, weights):
    wq, wk, wv, uq, uv = weights
    depth = blocks[0].shape[1]
    wide, kv, slots = wq.shape[1], wk.shape[1], uq.shape[0]
    tile = min(512, wide)
    start, total = span

    def kernel(ins, outs, scratch):
        ids, *ins = ins
        wq, wk, wv, uq, uv = ins[-5:]
        low_refs, blocks = ins[: len(lows)], ins[len(lows) : -5]
        xs, spread_q, spread_v = scratch
        at = 0
        for block in blocks:
            xs[at : at + block.shape[0], :] = block[...]
            at += block.shape[0]
        low = low_refs[0][:, start : start + total]
        for other in low_refs[1:]:
            low = low + other[:, start : start + total]
        spread_q[...], spread_v[...] = spread_lows(
            low, ids[:, start : start + total], slots // 16
        )

        def sums(w, spread=None, u=None):
            acc = jnp.dot(xs[...], w, preferred_element_type=jnp.float32)
            if u is not None:
                acc = acc + jnp.dot(spread[...], u, preferred_element_type=jnp.float32)
            return acc

        def write(acc, columns):
            for out, (first, count, dtype) in zip(outs, kinds):
                out[:, columns] = acc[first : first + count].astype(dtype)

        @pl.loop(0, wide // tile)
        def _(i):
            columns = columns_at(i * tile, tile)
            write(sums(wq[:, columns], spread_q, uq[:, columns]), columns)

        write(sums(wk[...]), slice(wide, wide + kv))
        write(sums(wv[...], spread_v, uv[...]), slice(wide + kv, wide + 2 * kv))

    spread = pltpu.VMEM((total, slots), jnp.bfloat16)
    return local_call(
        kernel,
        name,
        in_vmem([ids, *lows, *blocks, *weights]),
        [shaped((count, wide + 2 * kv), dtype) for _, count, dtype in kinds],
        [pltpu.VMEM((total, depth), jnp.bfloat16), spread, spread],
    )


def project_base(blocks, weights, carried):
    rows, depth = blocks[0].shape
    wide, kv = weights[0].shape[1], weights[1].shape[1]
    tile = min(512, wide)

    def kernel(ins, outs, scratch):
        *blocks, wq, wk, wv = ins
        (xs,) = scratch
        at = 0
        for block in blocks:
            xs[at : at + block.shape[0], :] = block[...]
            at += block.shape[0]

        def write(w, columns):
            acc = jnp.dot(xs[...], w, preferred_element_type=jnp.float32)
            outs[0][:, columns] = acc[:rows]
            outs[1][:, columns] = acc[rows:]

        @pl.loop(0, wide // tile)
        def _(i):
            columns = columns_at(i * tile, tile)
            write(wq[:, columns], columns)

        write(wk[...], slice(wide, wide + kv))
        write(wv[...], slice(wide + kv, wide + 2 * kv))

    return local_call(
        kernel,
        "project_base",
        in_vmem([*blocks, *weights]),
        [shaped((rows, wide + 2 * kv))] * 2,
        [pltpu.VMEM((2 * rows, depth), jnp.bfloat16)],
        carried=carried,
    )


def add_adapters(keep, send, ids, lows, uq, uv):
    rows = keep.shape[0]
    wide, kv, slots = uq.shape[1], uv.shape[1], uq.shape[0]
    tile = min(512, wide)

    def kernel(ins, outs, scratch):
        ids, *ins = ins
        low_refs, (keep0, send0, uq, uv) = ins[: len(lows)], ins[len(lows) :]
        keep, send = outs
        spread_q, spread_v = scratch
        low = low_refs[0][:, : 2 * rows]
        for other in low_refs[1:]:
            low = low + other[:, : 2 * rows]
        spread_q[...], spread_v[...] = spread_lows(low, ids[:, : 2 * rows], slots // 16)

        def write(extra, columns):
            keep[:, columns] = keep0[:, columns] + extra[:rows]
            send[:, columns] = (send0[:, columns] + extra[rows:]).astype(send.dtype)

        @pl.loop(0, wide // tile)
        def _(i):
            columns = columns_at(i * tile, tile)
            write(
                jnp.dot(spread_q[...], uq[:, columns], preferred_element_type=jnp.float32),
                columns,
            )

        keep[:, wide : wide + kv] = keep0[:, wide : wide + kv]
        send[:, wide : wide + kv] = send0[:, wide : wide + kv].astype(send.dtype)
        write(
            jnp.dot(spread_v[...], uv[...], preferred_element_type=jnp.float32),
            slice(wide + kv, wide + 2 * kv),
        )

    spread = pltpu.VMEM((2 * rows, slots), jnp.bfloat16)
    return local_call(
        kernel,
        "add_adapters",
        in_vmem([ids, *lows, keep, send, uq, uv]),
        [shaped(keep.shape), shaped(keep.shape, jnp.bfloat16)],
        [spread, spread],
    )


def add_sums(name, window, keep, others):
    first, part = window

    def kernel(ins, outs, _):
        keep, *others = ins
        at = 0
        for other in others:
            n = other.shape[0]
            total = keep[first + at : first + at + n, :] + other[...].astype(jnp.float32)
            outs[0][at : at + n, :] = total.astype(jnp.bfloat16)
            at += n

    return local_call(
        kernel, name, in_vmem([keep, *others]), [shaped((part, keep.shape[1]), jnp.bfloat16)]
    )[0]


def attend_kernel(first_row, block, done, ins, outs, scratch):
    if done:
        for full, source in zip(outs[1:], ins[:2]):
            full[: source.shape[0], :] = source[...]
    keep, swapped, *moved, scale, cosines, sines, lengths, keys, values = ins[2:] if done else ins
    out, key_out, value_out = outs
    head = cosines.shape[1]
    rows = out.shape[0]
    _, kv_heads, cache, _ = keys.shape
    heads = out.shape[1] // head
    group = heads // kv_heads
    score_scale = 1.0 / math.sqrt(head)
    sub = 8

    column = lax.broadcasted_iota(jnp.int32, (sub, sub * cache), 1)
    start = lax.broadcasted_iota(jnp.int32, (sub, sub * cache), 0) * cache

    @pl.loop(0, rows // block)
    def _(i):
        attended, new_keys, new_values = [], [], []
        for half in range(block // sub):
            here = pl.ds(pl.multiple_of(i * block + half * sub, sub), sub)
            whole = pl.ds(pl.multiple_of(first_row + i * block + half * sub, sub), sub)
            x = keep[whole] + swapped[whole].astype(jnp.float32)
            for m in moved:
                x = x + m[here].astype(jnp.float32)
            x = x * scale[whole]
            cos, sin = cosines[whole], sines[whole]
            inside = (column >= start) & (column < start + lengths[whole])

            def piece(i):
                return x[:, i * head : (i + 1) * head]

            def turn(v):
                return v * cos + pltpu.roll(v, head // 2, 1) * sin

            for g in range(kv_heads):
                query = jnp.concatenate(
                    [turn(piece(g * group + h)) for h in range(group)], axis=0
                ).astype(jnp.bfloat16)
                new_key = turn(piece(heads + g)).astype(jnp.bfloat16).astype(jnp.float32)
                new_value = piece(heads + kv_heads + g).astype(jnp.bfloat16).astype(jnp.float32)
                k = keys[whole, g].reshape(sub * cache, head)
                v = values[whole, g].reshape(sub * cache, head)
                scores = (
                    lax.dot_general(
                        query, k, (((1,), (1,)), ((), ())), preferred_element_type=jnp.float32
                    )
                    * score_scale
                )
                own_key = jnp.concatenate([new_key] * group, axis=0)
                own = (
                    jnp.sum(query.astype(jnp.float32) * own_key, axis=1, keepdims=True)
                    * score_scale
                )
                scores = jnp.where(
                    inside[None], scores.reshape(group, sub, sub * cache), masked_score
                ).reshape(group * sub, sub * cache)
                peak = jnp.maximum(jnp.max(scores, axis=1, keepdims=True), own)
                weights = jnp.exp(scores - peak)
                own_weight = jnp.exp(own - peak)
                inverse = 1.0 / (jnp.sum(weights, axis=1, keepdims=True) + own_weight)
                mixed = jnp.dot(weights.astype(jnp.bfloat16), v, preferred_element_type=jnp.float32)
                own_value = jnp.concatenate([new_value] * group, axis=0)
                mixed = (mixed + own_weight * own_value) * inverse
                attended += [mixed[h * sub : (h + 1) * sub] for h in range(group)]
                new_keys.append(new_key)
                new_values.append(new_value)
        r = pl.ds(pl.multiple_of(i * block, block), block)

        def joined(pieces):
            n = len(pieces) * sub // block
            return jnp.concatenate(
                [jnp.concatenate(pieces[j::n], axis=0) for j in range(n)], axis=1
            ).astype(jnp.bfloat16)

        out[r] = joined(attended)
        r = pl.ds(pl.multiple_of((first_row if done else 0) + i * block, block), block)
        key_out[r] = joined(new_keys)
        value_out[r] = joined(new_values)


def attend(name, window, keep, swapped, moved, rest, keys, values, earlier, carried=()):
    _, columns = keep.shape
    _, kv_heads, _, head = keys.shape
    kv_cols = kv_heads * head
    first, part = window
    kv_rows = first + part if earlier else part
    return local_call(
        functools.partial(attend_kernel, first, 16, bool(earlier)),
        name,
        in_vmem([*earlier, keep, swapped, *moved, *rest, keys, values]),
        [
            shaped((part, columns - 2 * kv_cols), jnp.bfloat16),
            *[shaped((kv_rows, kv_cols), jnp.bfloat16)] * 2,
        ],
        carried=carried,
    )


def output_part(name, span, order, blocks, weights):
    rows = blocks[0].shape[0]
    first, columns = span
    depth = weights.shape[0]
    tile = math.gcd(512, columns)
    total = rows * len(blocks)

    def kernel(ins, outs, scratch):
        order, *blocks, weights = ins
        keep, send = outs
        (xs,) = scratch
        for b, block in enumerate(blocks):
            xs[pl.ds(pl.multiple_of(order[b] * rows, rows), rows), :] = block[...]

        @pl.loop(0, columns // tile)
        def _(i):
            w = weights[:, columns_at(first + i * tile, tile)]
            acc = jnp.dot(xs[...], w, preferred_element_type=jnp.float32).astype(jnp.bfloat16)
            keep[:, columns_at(i * tile, tile)] = acc[: total // 2]
            send[:, columns_at(i * tile, tile)] = acc[total // 2 :]

    return local_call(
        kernel,
        name,
        [(order, SMEM), *in_vmem([*blocks, weights])],
        [shaped((total // 2, columns), jnp.bfloat16)] * 2,
        [pltpu.VMEM((total, depth), jnp.bfloat16)],
    )


def add_halves(name, keep, got):
    half, columns = keep.shape[0] // 2, keep.shape[1]

    def kernel(ins, outs, _):
        keep, got = ins
        total = keep[...].astype(jnp.float32) + got[...].astype(jnp.float32)
        outs[0][...] = total[:half]
        outs[1][...] = total[half:].astype(jnp.bfloat16)

    return local_call(
        kernel,
        name,
        in_vmem([keep, got]),
        [shaped((half, columns)), shaped((half, columns), jnp.bfloat16)],
    )


def add_last(name, keep, got):
    def kernel(ins, outs, _):
        total = ins[0][...].astype(jnp.float32) + ins[1][...].astype(jnp.float32)
        outs[0][...] = total.astype(jnp.bfloat16)

    return local_call(kernel, name, in_vmem([keep, got]), [shaped(keep.shape, jnp.bfloat16)])[0]


def assemble(done, keep, got, places, rows, columns):
    def kernel(ins, outs, _):
        *done, keep, got = ins
        total = keep[...].astype(jnp.float32) + got[...].astype(jnp.float32)
        total = total.astype(jnp.bfloat16)
        for piece, spots in zip([*done, total], places):
            for at, to, count, column in spots:
                outs[0][to : to + count, column : column + piece.shape[1]] = piece[
                    at : at + count, :
                ]

    return local_call(
        kernel,
        "assemble",
        in_vmem([*done, keep, got]),
        [shaped((rows, columns), jnp.bfloat16)],
    )[0]


def reversed_bits(x, count):
    out, bit = 0, 1
    while bit < count:
        out = out * 2 + (x // bit) % 2
        bit *= 2
    return out


def shards(
    tokens,
    input_norm_gain,
    query_matrix,
    key_matrix,
    value_matrix,
    output_matrix,
    rotated_key_cache,
    cached_value_rows,
    cache_length_per_row,
    row_adapter_index,
    query_down_maps,
    query_up_maps,
    value_down_maps,
    value_up_maps,
):
    pool_count = lax.axis_size("pool")
    tp_count = lax.axis_size("tp")
    chips = pool_count // 2
    pool_at = lax.axis_index("pool")
    tp_at = lax.axis_index("tp")
    chip, core = pool_at // 2, pool_at % 2
    rows = tokens.shape[0]
    adapters, rank, piece = query_down_maps.shape
    base = query_matrix.shape[0]
    kv_heads = rotated_key_cache.shape[1]
    head = rotated_key_cache.shape[3]

    own_ids = row_adapter_index.reshape(1, rows)
    ids = [
        own_ids if d == e == 0 else chip_move(own_ids, pool_count, d, e)
        for d in range(chips)
        for e in range(2)
    ]
    gain = input_norm_gain.reshape(-1, 128)
    (first,) = scaled_slices(
        "slice_tp", (tp_at * piece).reshape(1), tokens, gain, piece, [(0, 0, rows)]
    )
    first = after(first, *ids[1:])
    first, gain_1 = lax.optimization_barrier((first, gain))
    same_core = [first] + [chip_move(first, pool_count, d) for d in range(1, chips)]

    cut = rows // 2
    chunks = [(0, cut), (cut, rows - cut)]
    starts = [pool_at * base, (pool_at // 2 * 2 + 1 - core) * base]
    wanted = [(0, 0, rows), (1, 0, rows // 2), (1, rows // 2, rows // 2)]
    places = []
    for d in range(1, chips):
        for e in range(2):
            for c, (at, part) in enumerate(chunks if e else [(0, rows)]):
                places.append((d, e, c))
                wanted.append((len(starts), at, part))
            starts.append(((chip + d) % chips * 2 + (core + e) % 2) * base)
    own, *slices = scaled_slices(
        "slice_pool", jnp.stack(starts).astype(jnp.int32), tokens, gain_1, base, wanted
    )
    partner, away = slices[:2], dict(zip(places, slices[2:]))
    first_id = (pool_at * adapters).reshape(1).astype(jnp.int32)
    lengths = cache_length_per_row.reshape(1, rows)
    share = pool_count // tp_count
    order = []
    for d in range(chips):
        for e in range(2):
            p = (chip - d) % chips * 2 + (core + e) % 2
            order.append(
                reversed_bits(jnp.bitwise_xor(p // share, tp_at), tp_count) * share + p % share
            )
    order = jnp.stack(order).astype(jnp.int32)

    flat_down = [x.reshape(adapters * rank, piece) for x in (query_down_maps, value_down_maps)]
    flat_up = [x.reshape(adapters * rank, x.shape[2]) for x in (query_up_maps, value_up_maps)]
    small = [own, first_id, lengths, order]
    query_matrix, *small = lax.optimization_barrier((query_matrix, *small))
    own, first_id, lengths, order = small
    down_q, down_v, *weights = load(
        [*flat_down, query_matrix, key_matrix, value_matrix, *flat_up]
    )
    partner = [core_swap(x, pool_count) for x in partner]
    own_keep, own_send, keys, values = project_base(
        [own, *partner], weights[:3], [rotated_key_cache, cached_value_rows]
    )
    remote = {}
    for (d, e, c), x in away.items():
        remote[d, e, c] = chip_move(after(x, *same_core[1:]), pool_count, d, e)
    same_core[1:] = [after(x, own_keep) for x in same_core[1:]]
    adapter_rows = [b for x in same_core for b in (x, core_swap(x, pool_count))]
    local_ids, shrunk = shrink(first_id, ids, adapter_rows, down_q, down_v)
    lows = [shrunk] + [
        lax.ppermute(shrunk, "tp", [(i, (i + d) % tp_count) for i in range(tp_count)])
        for d in range(1, tp_count)
    ]
    rest = tables(tokens, after(lengths, shrunk), head)

    own_sums, own_send = add_adapters(
        own_keep, own_send, after(local_ids, rest[0]), lows, *weights[3:]
    )
    swapped = core_swap(own_send, pool_count)
    local_ids = after(local_ids, own_sums)
    moved = [[] for _ in chunks]
    keeps, sends, last = {}, {}, own_sums
    for c, (first, part) in enumerate(chunks):
        for d in range(1, chips):
            ahead = 0 if c else rows
            sent = [(ahead + i, part // 2, jnp.bfloat16) for i in (0, part // 2)]
            blocks = [remote[d, 1, c]] if c else [remote[d, 0, 0], remote[d, 1, 0]]
            results = project(
                f"project_{d}_{c}",
                sent if c else [(0, rows, jnp.float32), *sent],
                ((2 * d + 1) * rows + first - ahead, ahead + part),
                local_ids,
                lows,
                [after(blocks[0], last), *blocks[1:]],
                weights,
            )
            last = results[0]
            if c == 0:
                keeps[d], *results = results
            sends[c, d] = results
    both = None
    for c, window in enumerate(chunks):
        for d in range(1, chips):
            keep = keeps[d]
            if c:
                keep = after(keep, both)
            else:
                keep = after(keep, *[x for (_, _, c), x in remote.items() if c])
            swaps = [core_swap(x, pool_count) for x in sends[c, d]]
            both = add_sums(f"add_{d}_{c}", window, keep, swaps)
            moved[c].append(chip_move(both, pool_count, -d))
    moved[0][0] = after(moved[0][0], both)

    attended, earlier = [], []
    for c, window in enumerate(chunks):
        out, *earlier = attend(
            f"attend_{c}",
            window,
            own_sums,
            swapped,
            moved[c],
            rest,
            keys,
            values,
            earlier[:2],
            [] if c else [output_matrix],
        )
        if c == 0:
            out_weights = earlier[2]
        if c:
            out = after(out, attended[-1][-1])
        attended.append([out] + [chip_move(out, pool_count, d) for d in range(1, chips)])
    new_key, new_value = earlier
    attended[0][0] = after(attended[0][0], new_key)

    columns = output_matrix.shape[1]
    layout = [(0, 0, 1), (1, 0, 2), (1, 2, 4), (1, 3, 4)]
    gathered, keeps, sends, products = {}, [], [], []

    def multiply():
        c, at, count = layout[len(keeps)]
        if c not in gathered:
            parts = [after(x, products[-1]) for x in attended[c]] if c else attended[c]
            gathered[c] = [b for x in parts for b in (x, core_swap(x, pool_count))]
        else:
            gathered[c][0] = after(gathered[c][0], products[-1])
        width = columns // count
        keep, send = output_part(
            f"output_{c}_{at}_{count}", (at * width, width), order, gathered[c], out_weights
        )
        keeps.append(keep)
        sends.append(send)
        products.append(keep)

    stages = reversed_bits(1, tp_count).bit_length()
    last = len(layout) - 1
    total, got, done, places = None, {}, [], []
    for i, (c, at, count) in enumerate(layout):
        start, part = chunks[c]
        column = at * columns // count
        places.append([(r * part, r * rows + start, part, column) for r in range(share)])
    for slot in range(last + stages):
        while len(keeps) < min(slot + 2, last + 1):
            multiply()
        for stage in range(stages):
            i = slot - stage
            if not 0 <= i <= last:
                continue
            if stage == 0:
                got[i] = tp_swap(sends[i], tp_count, 1)
            past = [products[-1]] + ([] if total is None else [total])
            came = after(got[i], *past)
            if stage + 1 < stages:
                keeps[i], total = add_halves(f"halves_{i}_{stage}", keeps[i], came)
                got[i] = tp_swap(total, tp_count, 2 << stage)
            elif i < last:
                total = add_last(f"last_{i}", keeps[i], came)
                done.append(total)
            else:
                attn_out = assemble(done, keeps[i], came, places, share * rows, columns)
    return attn_out, new_key, new_value


def solution(mesh):
    return jax.shard_map(
        shards,
        mesh=mesh,
        in_specs=(
            P(("groups", "pool"), None),
            P(),
            P("pool", "tp"),
            P("pool", "tp"),
            P("pool", "tp"),
            P("tp", "pool"),
            P(("groups", "pool"), "tp", None, None),
            P(("groups", "pool"), "tp", None, None),
            P(("groups", "pool")),
            P(("groups", "pool")),
            P("pool", None, "tp"),
            P("pool", None, "tp"),
            P("pool", None, "tp"),
            P("pool", None, "tp"),
        ),
        out_specs=(
            P(("groups", "tp"), "pool"),
            P(("groups", "pool"), "tp"),
            P(("groups", "pool"), "tp"),
        ),
        check_vma=False,
    )
```
